512 devices in a mesh: fsdp: 8 (over x_lo, y), seq: 64 (over x_hi, z, core).
Axes of the slice: x: 4 (x_hi: 2, x_lo: 2; x = x_hi * 2 + x_lo), y: 4, z: 16, core: 2. Of those that a mesh axis runs over, the one named last changes fastest.
Arguments:
- tokens: bfloat16 [8, 64, 256, 1024], P('fsdp', 'seq'), may hold values from -6 to 6
- norm_gain: float32 [1024], replicated, may hold values from 0.1 to 1.9
- w_qkv: bfloat16 [1024, 3072], P('seq', 'fsdp'), may hold values from -0.9832583 to 0.9832583
- w_out: bfloat16 [1024, 1024], P('seq', 'fsdp'), may hold values from -0.1875 to 0.1875
- row_blocks: int32 [8], replicated, may hold values from 1 to 8, as said below
- col_rows: int32 [8], replicated, may hold values from 2 to 64, as said below
Outputs:
- mixed: bfloat16 [8, 64, 256, 1024], P('fsdp', 'seq')
The draws below stay inside these ranges and needn't reach their ends.
Inputs may be any that keep to these rules, and one draw needn't show every extreme that they name: `row_blocks`: every value from 1 to 8 is taken by some row head. `col_rows`: some column head reaches over all 64 rows and some over exactly 2.
All inputs are finite; a program needn't handle non-finite values.
Results may differ from the reference program's by a relative error of at most 0.0052.
Values may be sent and summed in bfloat16 or wider, within the bound.
No kernel may reach another device: no remote copies, remote signals or barrier semaphores. Data moves between devices by JAX's collectives and lax.ppermute only.
A program may use at most 64 MiB of HBM per device.

```python
import jax
import jax.numpy as jnp
from jax import lax

D = 1024
HEADS = 16
STRIDE = 256
BLOCK = 32
HEAD_DIM = 64
ROWS = 64
CLIPS = 8


def draw_tokens(key, part):
    key = jax.random.fold_in(key, 5)
    first = jax.random.fold_in(key, 0)
    shape = (CLIPS, ROWS, STRIDE, D)
    base = jnp.clip(jax.random.normal(first, shape, jnp.float32), -6.0, 6.0)
    return base.astype(jnp.bfloat16)


def draw_w_qkv(key, part):
    key = jax.random.fold_in(key, 7)
    first = jax.random.fold_in(key, 0)
    base = jnp.clip(jax.random.normal(first, (D, 3 * D), jnp.float32), -6.0, 6.0) * D ** (-0.5)
    return base.astype(jnp.bfloat16)


def draw_row_blocks(key, part):
    key = jax.random.fold_in(key, 11)
    order = jax.random.permutation(key, HEADS // 2)
    return (order % (STRIDE // BLOCK) + 1).astype(jnp.int32)


def draw_col_rows(key, part):
    key = jax.random.fold_in(key, 23)
    first, second = jax.random.split(key)
    values = jax.random.randint(first, (HEADS // 2,), 2, ROWS + 1)
    order = jax.random.permutation(second, HEADS // 2)
    values = jnp.where(order == 0, ROWS, values)
    values = jnp.where(order == 1, 2, values)
    return values.astype(jnp.int32)


def block_scale(key, dims, pieces, least, largest):
    def one(dim, shards_of):
        steps = jax.random.uniform(jax.random.fold_in(jax.random.fold_in(key, 6), dim), (shards_of,), jnp.float32, least / len(pieces), largest / len(pieces))
        return jnp.repeat(jnp.exp(steps), dims[dim] // shards_of).reshape((-1,) + (1,) * (len(dims) - dim - 1))

    level = one(*pieces[0])
    for cut in pieces[1:]:
        level = level * one(*cut)
    return level


def noise(own_key, extent, spread, most, shards=(), kind=jnp.bfloat16):
    values = jax.random.normal(own_key, extent, jnp.float32) * spread
    if len(shards) > 0:
        values = block_scale(own_key, extent, shards, -0.22, 0.18) * values
    return jnp.clip(values, min=-most, max=most).astype(kind)


def setup_inputs(seed: int = 0) -> dict:
    seeds = jax.random.split(jax.random.key(seed), 7)
    return {
        "tokens": draw_tokens(jax.random.fold_in(seeds[6], 71), 0),
        "norm_gain": jnp.clip(1.0 + 0.18 * jax.random.normal(seeds[1], (D,), jnp.float32), 0.1, 1.9),
        "w_qkv": draw_w_qkv(jax.random.fold_in(seeds[6], 71), 0),
        "w_out": noise(seeds[3], (D, D), D ** -0.5, 0.1875, ((0, 64), (1, 8))),
        "row_blocks": draw_row_blocks(jax.random.fold_in(seeds[6], 71), 0),
        "col_rows": draw_col_rows(jax.random.fold_in(seeds[6], 71), 0),
    }


def attend_rows(block, row_blocks):
    clips, rows, length, width3 = block.shape
    width = width3 // 3
    heads = width // HEAD_DIM
    query = block[..., :width].reshape(clips, rows, length, heads, HEAD_DIM).astype(jnp.float32)
    keys = block[..., width:2 * width].reshape(clips, rows, length, heads, HEAD_DIM).astype(jnp.float32)
    values = block[..., 2 * width:].reshape(clips, rows, length, heads, HEAD_DIM).astype(jnp.float32)
    scores = jnp.einsum('crphd,crqhd->crhpq', query, keys) / jnp.sqrt(jnp.float32(HEAD_DIM))
    where_pos = jnp.arange(length, dtype=jnp.int32)
    later = where_pos[None, :] <= where_pos[:, None]
    reach = where_pos[None, :] // BLOCK >= where_pos[:, None] // BLOCK - row_blocks[:, None, None] + 1
    allowed = later[None] & reach
    scores = jnp.where(allowed, scores, jnp.float32(-1e+30))
    top = lax.optimization_barrier(jnp.max(scores, axis=-1, keepdims=True))
    expo = jnp.exp(scores - top)
    weights = (expo / lax.optimization_barrier(jnp.sum(expo, axis=-1, keepdims=True))).astype(jnp.bfloat16)
    result = jnp.einsum('crhpq,crqhd->crphd', weights.astype(jnp.float32), values)
    return result.astype(jnp.bfloat16).reshape(clips, rows, length, width)

def attend_columns(block, col_rows):
    clips, rows, cols, width3 = block.shape
    width = width3 // 3
    heads = width // HEAD_DIM
    query = block[..., :width].reshape(clips, rows, cols, heads, HEAD_DIM).astype(jnp.float32)
    keys = block[..., width:2 * width].reshape(clips, rows, cols, heads, HEAD_DIM).astype(jnp.float32)
    values = block[..., 2 * width:].reshape(clips, rows, cols, heads, HEAD_DIM).astype(jnp.float32)
    scores = jnp.einsum('crkhd,cskhd->ckhrs', query, keys) / jnp.sqrt(jnp.float32(HEAD_DIM))
    where_row = jnp.arange(rows, dtype=jnp.int32)
    earlier = where_row[None, :] <= where_row[:, None]
    reach = where_row[None, None, :] > where_row[None, :, None] - col_rows[:, None, None]
    allowed = earlier[None] & reach
    scores = jnp.where(allowed, scores, jnp.float32(-1e+30))
    top = lax.optimization_barrier(jnp.max(scores, axis=-1, keepdims=True))
    expo = jnp.exp(scores - top)
    weights = (expo / lax.optimization_barrier(jnp.sum(expo, axis=-1, keepdims=True))).astype(jnp.bfloat16)
    result = jnp.einsum('ckhrs,cskhd->crkhd', weights.astype(jnp.float32), values)
    return result.astype(jnp.bfloat16).reshape(clips, rows, cols, width)

def reference(tokens, norm_gain, w_qkv, w_out, row_blocks, col_rows):

    def one_clip(clip):
        inputs = clip[None].astype(jnp.float32)
        scale = lax.rsqrt(lax.optimization_barrier(jnp.mean(inputs * inputs, axis=-1, keepdims=True)) + 1e-05)
        normed = (inputs * scale * norm_gain).astype(jnp.bfloat16)
        qkv = jnp.dot(normed, w_qkv, preferred_element_type=jnp.float32).astype(jnp.bfloat16)
        half = qkv.shape[-1] // 2
        row_out = attend_rows(qkv[..., :half], row_blocks)
        col_out = attend_columns(qkv[..., half:], col_rows)
        joined = jnp.concatenate([row_out, col_out], axis=-1)
        mixed = inputs + jnp.dot(joined, w_out, preferred_element_type=jnp.float32)
        return mixed.astype(jnp.bfloat16)[0]
    return lax.map(one_clip, tokens)
```

```python
import functools

import jax
import jax.numpy as jnp
from jax import lax
from jax.experimental import pallas as pl
from jax.experimental.pallas import tpu as pltpu
from jax.sharding import Mesh
from jax.sharding import PartitionSpec as P

XL, Y, XH, Z, C = 2, 4, 2, 16, 2
FEATURES, STRIDE, HEADS, HEAD_DIM, BLOCK = 1024, 256, 8, 64, 32
HALF = HEADS * HEAD_DIM
WIDTH = 3 * HALF
SWAP = [(0, 1), (1, 0)]
FAR = 1 << 20


def attention_kernel(place, reach_ref, gain_ref, x_ref, own_ref, other_ref, out_ref, w_ref, n_ref, qkv_ref):
    by_column = place[0] == 1
    core = place[1]
    for a in range(XL):
        for y in range(Y):
            block = a * Y + y
            cols = pl.ds(y * 384, 384)
            for z in range(Z):
                base = (32 * a + 2 * z) * 16
                mine = pl.multiple_of(base + 16 * core, 16)
                theirs = pl.multiple_of(base + 16 * (1 - core), 16)
                w_ref[pl.ds(mine, 16), cols] = own_ref[block, pl.ds(16 * z, 16), :]
                w_ref[pl.ds(theirs, 16), cols] = other_ref[block, pl.ds(16 * z, 16), :]

    def norm(i, _):
        rows = pl.ds(pl.multiple_of(i * 64, 64), 64)
        x = x_ref[rows, :].astype(jnp.float32)
        scale = lax.rsqrt(jnp.mean(x * x, axis=-1, keepdims=True) + 1e-05)
        n_ref[rows, :] = (x * scale * gain_ref[...]).astype(jnp.bfloat16)
        return 0

    lax.fori_loop(0, 8, norm, 0)

    def project(i, _):
        cols = pl.ds(pl.multiple_of(i * 256, 256), 256)
        qkv_ref[:, cols] = jnp.dot(
            n_ref[...], w_ref[:, cols], preferred_element_type=jnp.float32
        ).astype(jnp.bfloat16)
        return 0

    lax.fori_loop(0, WIDTH // 256, project, 0)

    i = lax.broadcasted_iota(jnp.int32, (STRIDE, STRIDE), 0)
    j = lax.broadcasted_iota(jnp.int32, (STRIDE, STRIDE), 1)
    back = (i >> 3) - (j >> 3)
    same = ((i ^ j) & 7) == 0
    in_row = jnp.where(j <= i, (i >> 5) - (j >> 5), FAR)
    near = jnp.where(same & (back >= 0), back, FAR)
    near = jnp.where(by_column, near, in_row)
    far = jnp.where(same & by_column, back + 32, FAR)

    for h in range(HEADS):
        reach = jnp.where(by_column, reach_ref[1, h], reach_ref[0, h])
        q = qkv_ref[:, h * 64 : h * 64 + 64]
        k = qkv_ref[:, HALF + h * 64 : HALF + h * 64 + 64]
        v = qkv_ref[:, 2 * HALF + h * 64 : 2 * HALF + h * 64 + 64]
        contract = (((1,), (1,)), ((), ()))

        def scores(qs, ks, dist):
            s = lax.dot_general(qs, ks, contract, preferred_element_type=jnp.float32)
            return jnp.where(dist < reach, s * 0.125, -1e30)

        qa, qb, ka, kb, va, vb = q[:256], q[256:], k[:256], k[256:], v[:256], v[256:]
        saa, sab, sbb = scores(qa, ka, near), scores(qa, kb, far), scores(qb, kb, near)
        ma = jnp.maximum(
            jnp.max(saa, axis=-1, keepdims=True), jnp.max(sab, axis=-1, keepdims=True)
        )
        mb = jnp.max(sbb, axis=-1, keepdims=True)
        paa, pab, pbb = jnp.exp(saa - ma), jnp.exp(sab - ma), jnp.exp(sbb - mb)
        la = jnp.sum(paa, axis=-1, keepdims=True) + jnp.sum(pab, axis=-1, keepdims=True)
        lb = jnp.sum(pbb, axis=-1, keepdims=True)
        oa = jnp.dot(paa.astype(jnp.bfloat16), va, preferred_element_type=jnp.float32)
        oa = oa + jnp.dot(pab.astype(jnp.bfloat16), vb, preferred_element_type=jnp.float32)
        ob = jnp.dot(pbb.astype(jnp.bfloat16), vb, preferred_element_type=jnp.float32)
        out_ref[:256, h * 64 : h * 64 + 64] = (oa / la).astype(jnp.bfloat16)
        out_ref[256:, h * 64 : h * 64 + 64] = (ob / lb).astype(jnp.bfloat16)


def attention(place, reach, gain, x, own, other):
    vmem = pl.BlockSpec(memory_space=pltpu.VMEM)
    smem = pl.BlockSpec(memory_space=pltpu.SMEM)
    return pl.pallas_call(
        attention_kernel,
        out_shape=jax.ShapeDtypeStruct((2 * STRIDE, HALF), jnp.bfloat16),
        in_specs=[smem, smem, vmem, vmem, vmem, vmem],
        out_specs=vmem,
        scratch_shapes=[
            pltpu.VMEM((FEATURES, WIDTH), jnp.bfloat16),
            pltpu.VMEM((2 * STRIDE, FEATURES), jnp.bfloat16),
            pltpu.VMEM((2 * STRIDE, WIDTH), jnp.bfloat16),
        ],
        compiler_params=pltpu.CompilerParams(vmem_limit_bytes=40 * 1024 * 1024),
        cost_estimate=pl.CostEstimate(
            flops=2 * 512 * 1024 * 1536 + 16 * 3 * 256 * 256 * 128,
            bytes_accessed=6 << 20,
            transcendentals=8 * 3 * 256 * 256,
        ),
        name="attention",
    )(place, reach, gain, x, own, other)


def body(tokens, norm_gain, w_qkv, w_out, row_blocks, col_rows):
    xh, c = lax.axis_index("xh"), lax.axis_index("c")
    by_column = xh == 1
    rows = tokens.reshape(STRIDE, FEATURES)

    block = jnp.concatenate([w_qkv, w_out], axis=1)
    block = lax.ppermute(block, ("xl", "xh"), [(0, 0), (1, 2), (2, 1), (3, 3)])

    send = jnp.concatenate(
        [rows.reshape(Z, 16, FEATURES), jnp.broadcast_to(block, (Z, 16, 512))], axis=2
    )
    recv = lax.all_to_all(send, "z", split_axis=0, concat_axis=0)
    turned = recv[:, :, :FEATURES]
    part_qkv = recv[:, :, FEATURES : FEATURES + 384].reshape(Z * 16, 384)
    part_out = recv[:, :, FEATURES + 384 :].reshape(Z * 16, 128)

    own = lax.all_to_all(
        jnp.broadcast_to(part_qkv, (XL * Y, Z * 16, 384)), ("xl", "y"), split_axis=0, concat_axis=0
    )
    other = lax.ppermute(own, "c", SWAP)
    out_own = lax.all_gather(part_out, ("xl", "y", "xh"), axis=0)

    straight = rows.reshape(Z, 16, FEATURES)
    mine = jnp.where(by_column, turned, straight)
    given = jnp.where(by_column, straight, turned)
    both = jnp.stack([mine, lax.ppermute(given, "xh", SWAP)])
    low, high = both[:, :, :8], both[:, :, 8:]
    keep = jnp.where(c == 0, low, high)
    got = lax.ppermute(jnp.where(c == 0, high, low), "c", SWAP)
    even, odd = jnp.where(c == 0, keep, got), jnp.where(c == 0, got, keep)
    columns = jnp.stack([even, odd], axis=2).reshape(2 * STRIDE, FEATURES)
    x = jnp.where(by_column, columns, both.reshape(2 * STRIDE, FEATURES))

    place = jnp.stack([xh, c]).astype(jnp.int32)
    reach = jnp.stack([row_blocks, col_rows])
    out = attention(place, reach, norm_gain.reshape(1, FEATURES), x, own, other)

    back = lax.ppermute(out[STRIDE:], "xh", SWAP)
    row_out = jnp.where(by_column, back, out[:STRIDE])
    col_mid = jnp.where(by_column, out[:STRIDE], back)
    col_out = lax.all_to_all(
        col_mid.reshape(Z * C, 8, HALF), ("z", "c"), split_axis=0, concat_axis=0
    ).reshape(STRIDE, HALF)

    out_other = lax.ppermute(out_own, "c", SWAP)
    pair = jnp.where(c == 0, jnp.stack([out_own, out_other]), jnp.stack([out_other, out_own]))
    full_out = pair.reshape(C, XL, Y, XH, Z, 16, 128).transpose(1, 4, 0, 5, 3, 2, 6)
    full_out = full_out.reshape(FEATURES, FEATURES)

    joined = jnp.concatenate([row_out, col_out], axis=1)
    mixed = rows.astype(jnp.float32) + jnp.dot(joined, full_out, preferred_element_type=jnp.float32)
    return mixed.astype(jnp.bfloat16).reshape(tokens.shape)


def solution(mesh):
    fine = Mesh(mesh.devices.reshape(XL, Y, XH, Z, C), ("xl", "y", "xh", "z", "c"))
    fsdp, seq = ("xl", "y"), ("xh", "z", "c")
    return jax.shard_map(
        body,
        mesh=fine,
        in_specs=(P(fsdp, seq, None, None), P(), P(seq, fsdp), P(seq, fsdp), P(), P()),
        out_specs=P(fsdp, seq, None, None),
        check_vma=False,
    )
```

```python
import functools

import jax
import jax.numpy as jnp
from jax import lax
from jax.experimental import pallas as pl
from jax.experimental.pallas import tpu as pltpu
from jax.sharding import Mesh
from jax.sharding import PartitionSpec as P

XL, Y, XH, Z, C = 2, 4, 2, 16, 2
FEATURES, STRIDE, HEADS, HEAD_DIM, BLOCK = 1024, 256, 8, 64, 32
HALF = HEADS * HEAD_DIM
WIDTH = 3 * HALF
SWAP = [(0, 1), (1, 0)]
FAR = 1 << 20


def attention_kernel(place, reach_ref, gain_ref, x_ref, own_ref, other_ref, out_ref, w_ref, n_ref, qkv_ref):
    by_column = place[0] == 1
    core = place[1]
    for a in range(XL):
        for y in range(Y):
            block = a * Y + y
            cols = pl.ds(y * 384, 384)
            for z in range(Z):
                base = (32 * a + 2 * z) * 16
                mine = pl.multiple_of(base + 16 * core, 16)
                theirs = pl.multiple_of(base + 16 * (1 - core), 16)
                w_ref[pl.ds(mine, 16), cols] = own_ref[block, pl.ds(16 * z, 16), :384]
                w_ref[pl.ds(theirs, 16), cols] = other_ref[block, pl.ds(16 * z, 16), :384]

    def norm(i, _):
        rows = pl.ds(pl.multiple_of(i * 64, 64), 64)
        x = x_ref[rows, :].astype(jnp.float32)
        scale = lax.rsqrt(jnp.mean(x * x, axis=-1, keepdims=True) + 1e-05)
        n_ref[rows, :] = (x * scale * gain_ref[...]).astype(jnp.bfloat16)
        return 0

    lax.fori_loop(0, 8, norm, 0)

    def project(i, _):
        cols = pl.ds(pl.multiple_of(i * 256, 256), 256)
        qkv_ref[:, cols] = jnp.dot(
            n_ref[...], w_ref[:, cols], preferred_element_type=jnp.float32
        ).astype(jnp.bfloat16)
        return 0

    lax.fori_loop(0, WIDTH // 256, project, 0)

    i = lax.broadcasted_iota(jnp.int32, (STRIDE, STRIDE), 0)
    j = lax.broadcasted_iota(jnp.int32, (STRIDE, STRIDE), 1)
    back = (i >> 3) - (j >> 3)
    same = ((i ^ j) & 7) == 0
    in_row = jnp.where(j <= i, (i >> 5) - (j >> 5), FAR)
    near = jnp.where(same & (back >= 0), back, FAR)
    near = jnp.where(by_column, near, in_row)
    far = jnp.where(same & by_column, back + 32, FAR)

    for h in range(HEADS):
        reach = jnp.where(by_column, reach_ref[1, h], reach_ref[0, h])
        q = qkv_ref[:, h * 64 : h * 64 + 64]
        k = qkv_ref[:, HALF + h * 64 : HALF + h * 64 + 64]
        v = qkv_ref[:, 2 * HALF + h * 64 : 2 * HALF + h * 64 + 64]
        contract = (((1,), (1,)), ((), ()))

        def scores(qs, ks, dist):
            s = lax.dot_general(qs, ks, contract, preferred_element_type=jnp.float32)
            return jnp.where(dist < reach, s * 0.125, -1e30)

        qa, qb, ka, kb, va, vb = q[:256], q[256:], k[:256], k[256:], v[:256], v[256:]
        saa, sab, sbb = scores(qa, ka, near), scores(qa, kb, far), scores(qb, kb, near)
        ma = jnp.maximum(
            jnp.max(saa, axis=-1, keepdims=True), jnp.max(sab, axis=-1, keepdims=True)
        )
        mb = jnp.max(sbb, axis=-1, keepdims=True)
        paa, pab, pbb = jnp.exp(saa - ma), jnp.exp(sab - ma), jnp.exp(sbb - mb)
        la = jnp.sum(paa, axis=-1, keepdims=True) + jnp.sum(pab, axis=-1, keepdims=True)
        lb = jnp.sum(pbb, axis=-1, keepdims=True)
        oa = jnp.dot(paa.astype(jnp.bfloat16), va, preferred_element_type=jnp.float32)
        oa = oa + jnp.dot(pab.astype(jnp.bfloat16), vb, preferred_element_type=jnp.float32)
        ob = jnp.dot(pbb.astype(jnp.bfloat16), vb, preferred_element_type=jnp.float32)
        out_ref[:256, h * 64 : h * 64 + 64] = (oa / la).astype(jnp.bfloat16)
        out_ref[256:, h * 64 : h * 64 + 64] = (ob / lb).astype(jnp.bfloat16)


def attention(place, reach, gain, x, own, other):
    vmem = pl.BlockSpec(memory_space=pltpu.VMEM)
    smem = pl.BlockSpec(memory_space=pltpu.SMEM)
    return pl.pallas_call(
        attention_kernel,
        out_shape=jax.ShapeDtypeStruct((2 * STRIDE, HALF), jnp.bfloat16),
        in_specs=[smem, smem, vmem, vmem, vmem, vmem],
        out_specs=vmem,
        scratch_shapes=[
            pltpu.VMEM((FEATURES, WIDTH), jnp.bfloat16),
            pltpu.VMEM((2 * STRIDE, FEATURES), jnp.bfloat16),
            pltpu.VMEM((2 * STRIDE, WIDTH), jnp.bfloat16),
        ],
        compiler_params=pltpu.CompilerParams(vmem_limit_bytes=40 * 1024 * 1024),
        cost_estimate=pl.CostEstimate(
            flops=2 * 512 * 1024 * 1536 + 16 * 3 * 256 * 256 * 128,
            bytes_accessed=6 << 20,
            transcendentals=8 * 3 * 256 * 256,
        ),
        name="attention",
    )(place, reach, gain, x, own, other)


def body(tokens, norm_gain, w_qkv, w_out, row_blocks, col_rows):
    xh, c = lax.axis_index("xh"), lax.axis_index("c")
    by_column = xh == 1
    rows = tokens.reshape(STRIDE, FEATURES)

    block = jnp.concatenate([w_qkv, w_out], axis=1)
    block = lax.ppermute(block, ("xl", "xh"), [(0, 0), (1, 2), (2, 1), (3, 3)])

    send = jnp.concatenate(
        [rows.reshape(Z, 16, FEATURES), jnp.broadcast_to(block, (Z, 16, 512))], axis=2
    )
    recv = lax.all_to_all(send, "z", split_axis=0, concat_axis=0)
    turned = recv[:, :, :FEATURES]
    part = recv[:, :, FEATURES:].reshape(Z * 16, 512)

    own = lax.all_to_all(
        jnp.broadcast_to(part, (XL * Y, Z * 16, 512)), ("xl", "y"), split_axis=0, concat_axis=0
    )
    other = lax.ppermute(own, "c", SWAP)

    straight = rows.reshape(Z, 16, FEATURES)
    mine = jnp.where(by_column, turned, straight)
    given = jnp.where(by_column, straight, turned)
    both = jnp.stack([mine, lax.ppermute(given, "xh", SWAP)])
    low, high = both[:, :, :8], both[:, :, 8:]
    keep = jnp.where(c == 0, low, high)
    got = lax.ppermute(jnp.where(c == 0, high, low), "c", SWAP)
    even, odd = jnp.where(c == 0, keep, got), jnp.where(c == 0, got, keep)
    columns = jnp.stack([even, odd], axis=2).reshape(2 * STRIDE, FEATURES)
    x = jnp.where(by_column, columns, both.reshape(2 * STRIDE, FEATURES))

    place = jnp.stack([xh, c]).astype(jnp.int32)
    reach = jnp.stack([row_blocks, col_rows])
    out = attention(place, reach, norm_gain.reshape(1, FEATURES), x, own, other)

    back = lax.ppermute(out[STRIDE:], "xh", SWAP)
    row_out = jnp.where(by_column, back, out[:STRIDE])
    col_mid = jnp.where(by_column, out[:STRIDE], back)
    col_out = lax.all_to_all(
        col_mid.reshape(Z * C, 8, HALF), ("z", "c"), split_axis=0, concat_axis=0
    ).reshape(STRIDE, HALF)

    out_own, out_other = own[:, :, 384:], other[:, :, 384:]
    far_own = lax.ppermute(out_own, "xh", SWAP)
    far_other = lax.ppermute(far_own, "c", SWAP)

    def ordered(where, mine, theirs):
        return jnp.where(where == 0, jnp.stack([mine, theirs]), jnp.stack([theirs, mine]))

    pair = ordered(c, ordered(xh, out_own, far_own), ordered(xh, out_other, far_other))
    full_out = pair.reshape(C, XH, XL, Y, Z, 16, 128).transpose(2, 4, 0, 5, 1, 3, 6)
    full_out = full_out.reshape(FEATURES, FEATURES)

    joined = jnp.concatenate([row_out, col_out], axis=1)
    mixed = rows.astype(jnp.float32) + jnp.dot(joined, full_out, preferred_element_type=jnp.float32)
    return mixed.astype(jnp.bfloat16).reshape(tokens.shape)


def solution(mesh):
    fine = Mesh(mesh.devices.reshape(XL, Y, XH, Z, C), ("xl", "y", "xh", "z", "c"))
    fsdp, seq = ("xl", "y"), ("xh", "z", "c")
    return jax.shard_map(
        body,
        mesh=fine,
        in_specs=(P(fsdp, seq, None, None), P(), P(seq, fsdp), P(seq, fsdp), P(), P()),
        out_specs=P(fsdp, seq, None, None),
        check_vma=False,
    )
```

```python
import functools

import jax
import jax.numpy as jnp
from jax import lax
from jax.experimental import pallas as pl
from jax.experimental.pallas import tpu as pltpu
from jax.sharding import Mesh
from jax.sharding import PartitionSpec as P

XL, Y, XH, Z, C = 2, 4, 2, 16, 2
X = XH * XL
FEATURES, STRIDE, HEADS, HEAD_DIM = 1024, 256, 8, 64
HALF = HEADS * HEAD_DIM
WIDTH = 3 * HALF
PART = 384
SEQ = ("xh", "z", "c")
FAR = 1 << 20


def blocks(place, odd):
    x, y, core = place[0], place[1], place[2]
    for t in range(X):
        there = (x + t) & 3
        xh, xl = there >> 1, there & 1
        turn = (1 - xl) if odd else xl
        for s in range(Y):
            for zz in range(Z // 2):
                row = xh * 512 + 64 * zz + 32 * turn
                yield t * Y + s, zz, row, (y + s) & 3


def assemble(place, odd, own_ref, other_ref, lanes, w_ref, first, width):
    core = place[2]
    for block, zz, row, y in blocks(place, odd):
        cols = pl.ds(pl.multiple_of(first + width * y, 128), width)
        for ref, c in ((own_ref, core), (other_ref, 1 - core)):
            at = pl.multiple_of(row + 16 * c, 16)
            w_ref[pl.ds(at, 16), cols] = ref[block, pl.ds(16 * zz, 16), lanes]


def attend(reach_ref, gain_ref, x_ref, w_ref, n_ref, qkv_ref, out_ref, dist):
    def norm(i, _):
        rows = pl.ds(pl.multiple_of(i * 64, 64), 64)
        x = x_ref[rows, :].astype(jnp.float32)
        scale = lax.rsqrt(jnp.mean(x * x, axis=-1, keepdims=True) + 1e-05)
        n_ref[rows, :] = (x * scale * gain_ref[...]).astype(jnp.bfloat16)
        return 0

    lax.fori_loop(0, STRIDE // 64, norm, 0)

    def project(i, _):
        cols = pl.ds(pl.multiple_of(i * 256, 256), 256)
        qkv_ref[:, cols] = jnp.dot(
            n_ref[...], w_ref[:, cols], preferred_element_type=jnp.float32
        ).astype(jnp.bfloat16)
        return 0

    lax.fori_loop(0, WIDTH // 256, project, 0)

    for h in range(HEADS):
        q = qkv_ref[:, h * 64 : h * 64 + 64]
        k = qkv_ref[:, HALF + h * 64 : HALF + h * 64 + 64]
        v = qkv_ref[:, 2 * HALF + h * 64 : 2 * HALF + h * 64 + 64]
        s = lax.dot_general(
            q, k, (((1,), (1,)), ((), ())), preferred_element_type=jnp.float32
        )
        s = jnp.where(dist < reach_ref[h], s * 0.125, -1e30)
        p = jnp.exp(s - jnp.max(s, axis=-1, keepdims=True))
        o = jnp.dot(p.astype(jnp.bfloat16), v, preferred_element_type=jnp.float32)
        o = o / jnp.sum(p, axis=-1, keepdims=True)
        out_ref[:, h * 64 : h * 64 + 64] = o.astype(jnp.bfloat16)


def pairs():
    i = lax.broadcasted_iota(jnp.int32, (STRIDE, STRIDE), 0)
    return i, lax.broadcasted_iota(jnp.int32, (STRIDE, STRIDE), 1)


def column_kernel(place, reach_ref, gain_ref, x_ref, own_ref, other_ref, out_ref, done_ref, w_ref, n_ref, qkv_ref):
    done_ref[0] = 0
    assemble(place, True, own_ref, other_ref, slice(0, PART), w_ref, 0, PART)
    i, j = pairs()
    back = (i >> 2) - (j >> 2)
    dist = jnp.where((((i ^ j) & 3) == 0) & (back >= 0), back, FAR)
    attend(reach_ref, gain_ref, x_ref, w_ref, n_ref, qkv_ref, out_ref, dist)


def row_kernel(
    place, reach_ref, gain_ref, x_ref, own_ref, other_ref, base_ref, low_ref, done_ref, w_ref, n_ref, qkv_ref, a_ref, o_ref
):
    done_ref[0] = 0
    assemble(place, False, own_ref, other_ref, slice(0, PART), w_ref, 0, PART)
    i, j = pairs()
    dist = jnp.where(j <= i, (i >> 5) - (j >> 5), FAR)
    attend(reach_ref, gain_ref, x_ref, w_ref, n_ref, qkv_ref, a_ref, dist)
    assemble(place, False, own_ref, other_ref, slice(PART, PART + 128), o_ref, 0, 128)
    assemble(place, True, own_ref, other_ref, slice(PART + 128, PART + 256), o_ref, 512, 128)
    for n in range(0, FEATURES, 256):
        base_ref[:, n : n + 256] = x_ref[:, n : n + 256].astype(jnp.float32) + jnp.dot(
            a_ref[...], o_ref[:HALF, n : n + 256], preferred_element_type=jnp.float32
        )
    low_ref[...] = o_ref[HALF:, :]


def last_kernel(base_ref, col_ref, low_ref, out_ref):
    for n in range(0, FEATURES, 256):
        out_ref[:, n : n + 256] = (
            base_ref[:, n : n + 256]
            + jnp.dot(col_ref[...], low_ref[:, n : n + 256], preferred_element_type=jnp.float32)
        ).astype(jnp.bfloat16)


VMEM = pl.BlockSpec(memory_space=pltpu.VMEM)
SMEM = pl.BlockSpec(memory_space=pltpu.SMEM)
WORK = [
    pltpu.VMEM((FEATURES, WIDTH), jnp.bfloat16),
    pltpu.VMEM((STRIDE, FEATURES), jnp.bfloat16),
    pltpu.VMEM((STRIDE, WIDTH), jnp.bfloat16),
]
PARAMS = pltpu.CompilerParams(vmem_limit_bytes=40 * 1024 * 1024)
COST = pl.CostEstimate(
    flops=2 * 256 * 1024 * 1536 + 16 * 256 * 256 * 128,
    bytes_accessed=6 << 20,
    transcendentals=8 * 256 * 256,
)


def column_attention(place, reach, gain, x, own, other):
    return pl.pallas_call(
        column_kernel,
        out_shape=[
            jax.ShapeDtypeStruct((STRIDE, HALF), jnp.bfloat16),
            jax.ShapeDtypeStruct((1,), jnp.int32),
        ],
        in_specs=[SMEM, SMEM, VMEM, VMEM, VMEM, VMEM],
        out_specs=[VMEM, SMEM],
        scratch_shapes=WORK,
        compiler_params=PARAMS,
        cost_estimate=COST,
        name="columns",
    )(place, reach, gain, x, own, other)


def row_attention(place, reach, gain, x, own, other):
    return pl.pallas_call(
        row_kernel,
        out_shape=[
            jax.ShapeDtypeStruct((STRIDE, FEATURES), jnp.float32),
            jax.ShapeDtypeStruct((HALF, FEATURES), jnp.bfloat16),
            jax.ShapeDtypeStruct((1,), jnp.int32),
        ],
        in_specs=[SMEM, SMEM, VMEM, VMEM, VMEM, VMEM],
        out_specs=[VMEM, VMEM, SMEM],
        scratch_shapes=WORK
        + [
            pltpu.VMEM((STRIDE, HALF), jnp.bfloat16),
            pltpu.VMEM((FEATURES, FEATURES), jnp.bfloat16),
        ],
        compiler_params=PARAMS,
        cost_estimate=COST,
        name="rows",
    )(place, reach, gain, x, own, other)


def ring(part, axes, order):
    size = len(order)
    return [
        lax.ppermute(part, axes, [(order[i], order[(i - t) % size]) for i in range(size)])
        for t in range(1, size)
    ]


def body(tokens, norm_gain, w_qkv, w_out, row_blocks, col_rows):
    xl, y, xh, c = (lax.axis_index(a) for a in ("xl", "y", "xh", "c"))
    rows = tokens.reshape(STRIDE, FEATURES)
    gain = norm_gain.reshape(1, FEATURES)
    place = jnp.stack([2 * xh + xl, y, c]).astype(jnp.int32)

    block = jnp.concatenate([w_qkv, w_out], axis=1)
    change = [(a * Z + z, (a ^ (z & 1)) * Z + z) for a in range(XL) for z in range(Z)]
    block = lax.ppermute(block, ("xl", "z"), change)
    column = lax.all_to_all(jnp.broadcast_to(block, (Z, 16, 512)), "z", split_axis=0, concat_axis=0)

    sent, column = lax.optimization_barrier((rows, column))
    turned = lax.all_to_all(sent.reshape(64, 4, FEATURES), SEQ, split_axis=0, concat_axis=0)
    turned = turned.reshape(STRIDE, FEATURES)

    halves = column.reshape(Z // 2, 2, 16, 512)
    row_part = jnp.where(xl == 0, halves[:, 0], halves[:, 1]).reshape(128, 512)
    col_part = jnp.where(xl == 0, halves[:, 1], halves[:, 0]).reshape(128, 512)
    part = jnp.concatenate([col_part[:, :PART], row_part, col_part[:, PART:]], axis=1)
    near = jnp.stack([part, *ring(part, "y", range(Y))])

    def plane(part):
        return [part, *ring(part, ("xl", "xh"), [0, 2, 1, 3])]

    def both_cores(parts):
        own = jnp.stack(parts).reshape(X * Y, *parts[0].shape[1:])
        return own, lax.ppermute(own, "c", [(0, 1), (1, 0)])

    col_plane = plane(near[:, :, :PART])
    col_own, col_other = both_cores(col_plane)
    col_mid, done = column_attention(place, col_rows, gain, turned, col_own, col_other)
    col_out = lax.all_to_all(col_mid.reshape(64, 4, HALF), SEQ, split_axis=0, concat_axis=0)

    near_rest, _ = lax.optimization_barrier((near[:, :, PART:], col_plane))
    rest = [jnp.where(done[0] == 0, a, 0) for a in plane(near_rest)]
    rest_own, rest_other = both_cores(rest)
    base, low, last = row_attention(place, row_blocks, gain, rows, rest_own, rest_other)
    col_out = jnp.where(last[0] == 0, col_out, 0).reshape(STRIDE, HALF)

    mixed = pl.pallas_call(
        last_kernel,
        out_shape=jax.ShapeDtypeStruct((STRIDE, FEATURES), jnp.bfloat16),
        in_specs=[VMEM, VMEM, VMEM],
        out_specs=VMEM,
        compiler_params=PARAMS,
        name="mixed",
    )(base, col_out, low)
    return mixed.reshape(tokens.shape)


def solution(mesh):
    fine = Mesh(mesh.devices.reshape(XL, Y, XH, Z, C), ("xl", "y", "xh", "z", "c"))
    fsdp = ("xl", "y")
    return jax.shard_map(
        body,
        mesh=fine,
        in_specs=(P(fsdp, SEQ, None, None), P(), P(SEQ, fsdp), P(SEQ, fsdp), P(), P()),
        out_specs=P(fsdp, SEQ, None, None),
        check_vma=False,
    )
```

```python
import jax
import jax.numpy as jnp
from jax import lax
from jax.experimental import pallas as pl
from jax.experimental.pallas import tpu as pltpu
from jax.sharding import Mesh
from jax.sharding import PartitionSpec as P

XL, Y, XH, Z, C = 2, 4, 2, 16, 2
X = XH * XL
FEATURES, STRIDE, HEADS, HEAD_DIM = 1024, 256, 8, 64
HALF = HEADS * HEAD_DIM
WIDTH = 3 * HALF
PART = 384
SEQ = ("xh", "z", "c")
FAR = 1 << 20


def blocks(place, odd):
    x, y, core = place[0], place[1], place[2]
    for t in range(X):
        there = (x + t) & 3
        xh, xl = there >> 1, there & 1
        turn = (1 - xl) if odd else xl
        for s in range(Y):
            for zz in range(Z // 2):
                row = xh * 512 + 64 * zz + 32 * turn
                yield t * Y + s, zz, row, (y + s) & 3


def assemble(place, odd, own_ref, other_ref, lanes, w_ref, first, width):
    core = place[2]
    for block, zz, row, y in blocks(place, odd):
        cols = pl.ds(pl.multiple_of(first + width * y, 128), width)
        for ref, c in ((own_ref, core), (other_ref, 1 - core)):
            at = pl.multiple_of(row + 16 * c, 16)
            w_ref[pl.ds(at, 16), cols] = ref[block, pl.ds(16 * zz, 16), lanes]


def attend(reach_ref, gain_ref, x_ref, w_ref, n_ref, qkv_ref, out_ref, dist):
    def norm(i, _):
        rows = pl.ds(pl.multiple_of(i * 64, 64), 64)
        x = x_ref[rows, :].astype(jnp.float32)
        scale = lax.rsqrt(jnp.mean(x * x, axis=-1, keepdims=True) + 1e-05)
        n_ref[rows, :] = (x * scale * gain_ref[...]).astype(jnp.bfloat16)
        return 0

    lax.fori_loop(0, STRIDE // 64, norm, 0)

    def project(i, _):
        cols = pl.ds(pl.multiple_of(i * 256, 256), 256)
        qkv_ref[:, cols] = jnp.dot(
            n_ref[...], w_ref[:, cols], preferred_element_type=jnp.float32
        ).astype(jnp.bfloat16)
        return 0

    lax.fori_loop(0, WIDTH // 256, project, 0)

    for h in range(HEADS):
        q = qkv_ref[:, h * 64 : h * 64 + 64]
        k = qkv_ref[:, HALF + h * 64 : HALF + h * 64 + 64]
        v = qkv_ref[:, 2 * HALF + h * 64 : 2 * HALF + h * 64 + 64]
        s = lax.dot_general(
            q, k, (((1,), (1,)), ((), ())), preferred_element_type=jnp.float32
        )
        s = jnp.where(dist < reach_ref[h], s * 0.125, -1e30)
        p = jnp.exp(s - jnp.max(s, axis=-1, keepdims=True))
        o = jnp.dot(p.astype(jnp.bfloat16), v, preferred_element_type=jnp.float32)
        o = o / jnp.sum(p, axis=-1, keepdims=True)
        out_ref[:, h * 64 : h * 64 + 64] = o.astype(jnp.bfloat16)


def pairs():
    i = lax.broadcasted_iota(jnp.int32, (STRIDE, STRIDE), 0)
    return i, lax.broadcasted_iota(jnp.int32, (STRIDE, STRIDE), 1)


def column_kernel(place, reach_ref, gain_ref, x_ref, own_ref, other_ref, out_ref, done_ref, w_ref, n_ref, qkv_ref):
    done_ref[0] = 0
    core = place[2]
    for a in range(XL):
        for y in range(Y):
            for b in range(XH):
                for zz in range(Z // 2):
                    for ref, c in ((own_ref, core), (other_ref, 1 - core)):
                        row = b * 512 + 64 * zz + 32 * (1 - a) + 16 * c
                        w_ref[pl.ds(pl.multiple_of(row, 16), 16), pl.ds(PART * y, PART)] = ref[
                            (a * Y + y) * XH + b, pl.ds(16 * zz, 16), :
                        ]
    i, j = pairs()
    back = (i >> 2) - (j >> 2)
    dist = jnp.where((((i ^ j) & 3) == 0) & (back >= 0), back, FAR)
    attend(reach_ref, gain_ref, x_ref, w_ref, n_ref, qkv_ref, out_ref, dist)


def pack_kernel(after, *refs):
    *parts, out_ref, sems = refs
    copies = [pltpu.make_async_copy(p, out_ref.at[i], sems.at[i]) for i, p in enumerate(parts)]
    for copy in copies:
        copy.start()
    for copy in copies:
        copy.wait()


def row_kernel(
    place, reach_ref, gain_ref, x_ref, own_ref, other_ref, base_ref, low_ref, done_ref, w_ref, n_ref, qkv_ref, a_ref, o_ref
):
    done_ref[0] = 0
    assemble(place, False, own_ref, other_ref, slice(0, PART), w_ref, 0, PART)
    i, j = pairs()
    dist = jnp.where(j <= i, (i >> 5) - (j >> 5), FAR)
    attend(reach_ref, gain_ref, x_ref, w_ref, n_ref, qkv_ref, a_ref, dist)
    assemble(place, False, own_ref, other_ref, slice(PART, PART + 128), o_ref, 0, 128)
    assemble(place, True, own_ref, other_ref, slice(PART + 128, PART + 256), o_ref, 512, 128)
    for n in range(0, FEATURES, 256):
        base_ref[:, n : n + 256] = x_ref[:, n : n + 256].astype(jnp.float32) + jnp.dot(
            a_ref[...], o_ref[:HALF, n : n + 256], preferred_element_type=jnp.float32
        )
    low_ref[...] = o_ref[HALF:, :]


def last_kernel(base_ref, col_ref, low_ref, out_ref):
    for n in range(0, FEATURES, 256):
        out_ref[:, n : n + 256] = (
            base_ref[:, n : n + 256]
            + jnp.dot(col_ref[...], low_ref[:, n : n + 256], preferred_element_type=jnp.float32)
        ).astype(jnp.bfloat16)


VMEM = pl.BlockSpec(memory_space=pltpu.VMEM)
SMEM = pl.BlockSpec(memory_space=pltpu.SMEM)
WORK = [
    pltpu.VMEM((FEATURES, WIDTH), jnp.bfloat16),
    pltpu.VMEM((STRIDE, FEATURES), jnp.bfloat16),
    pltpu.VMEM((STRIDE, WIDTH), jnp.bfloat16),
]
PARAMS = pltpu.CompilerParams(vmem_limit_bytes=40 * 1024 * 1024)
COST = pl.CostEstimate(
    flops=2 * 256 * 1024 * 1536 + 16 * 256 * 256 * 128,
    bytes_accessed=6 << 20,
    transcendentals=8 * 256 * 256,
)


def column_attention(place, reach, gain, x, own, other):
    return pl.pallas_call(
        column_kernel,
        out_shape=[
            jax.ShapeDtypeStruct((STRIDE, HALF), jnp.bfloat16),
            jax.ShapeDtypeStruct((1,), jnp.int32),
        ],
        in_specs=[SMEM, SMEM, VMEM, VMEM, VMEM, VMEM],
        out_specs=[VMEM, SMEM],
        scratch_shapes=WORK,
        compiler_params=PARAMS,
        cost_estimate=COST,
        name="columns",
    )(place, reach, gain, x, own, other)


def pack(after, parts):
    return pl.pallas_call(
        pack_kernel,
        out_shape=jax.ShapeDtypeStruct((len(parts), *parts[0].shape), jnp.bfloat16),
        in_specs=[SMEM] + [pl.BlockSpec(memory_space=pl.ANY)] * len(parts),
        out_specs=pl.BlockSpec(memory_space=pl.ANY),
        scratch_shapes=[pltpu.SemaphoreType.DMA((len(parts),))],
        name="pack",
    )(after, *parts)


def row_attention(place, reach, gain, x, own, other):
    return pl.pallas_call(
        row_kernel,
        out_shape=[
            jax.ShapeDtypeStruct((STRIDE, FEATURES), jnp.float32),
            jax.ShapeDtypeStruct((HALF, FEATURES), jnp.bfloat16),
            jax.ShapeDtypeStruct((1,), jnp.int32),
        ],
        in_specs=[SMEM, SMEM, VMEM, VMEM, VMEM, VMEM],
        out_specs=[VMEM, VMEM, SMEM],
        scratch_shapes=WORK
        + [
            pltpu.VMEM((STRIDE, HALF), jnp.bfloat16),
            pltpu.VMEM((FEATURES, FEATURES), jnp.bfloat16),
        ],
        compiler_params=PARAMS,
        cost_estimate=pl.CostEstimate(flops=1 << 20, bytes_accessed=1 << 20, transcendentals=0),
        name="rows",
    )(place, reach, gain, x, own, other)


def ring(part, axes, order):
    size = len(order)
    return [
        lax.ppermute(part, axes, [(order[i], order[(i - t) % size]) for i in range(size)])
        for t in range(1, size)
    ]


def body(tokens, norm_gain, w_qkv, w_out, row_blocks, col_rows):
    xl, y, xh, c = (lax.axis_index(a) for a in ("xl", "y", "xh", "c"))
    rows = tokens.reshape(STRIDE, FEATURES)
    gain = norm_gain.reshape(1, FEATURES)
    place = jnp.stack([2 * xh + xl, y, c]).astype(jnp.int32)

    block = jnp.concatenate([w_qkv, w_out], axis=1)
    change = [(a * Z + z, (a ^ (z & 1)) * Z + z) for a in range(XL) for z in range(Z)]
    block = lax.ppermute(block, ("xl", "z"), change)

    column = lax.all_to_all(jnp.broadcast_to(block, (Z, 16, 512)), "z", split_axis=0, concat_axis=0)
    halves = column.reshape(Z // 2, 2, 16, 512)
    row_part = jnp.where(xl == 0, halves[:, 0], halves[:, 1]).reshape(128, 512)
    col_part = jnp.where(xl == 0, halves[:, 1], halves[:, 0]).reshape(128, 512)
    rest_part = jnp.concatenate([row_part, col_part[:, PART:]], axis=1)

    col_own = lax.all_to_all(
        jnp.broadcast_to(col_part[:, :PART], (X * Y, 128, PART)),
        ("xl", "y", "xh"),
        split_axis=0,
        concat_axis=0,
    )

    near = jnp.stack([rest_part, *ring(rest_part, "y", range(Y))])

    sent, col_own, near = lax.optimization_barrier((rows, col_own, near))
    turned = lax.all_to_all(sent.reshape(64, 4, FEATURES), SEQ, split_axis=0, concat_axis=0)
    turned = turned.reshape(STRIDE, FEATURES)

    swap = [(0, 1), (1, 0)]
    col_other = lax.ppermute(col_own, "c", swap)
    near, col_other = lax.optimization_barrier((near, col_other))
    plane = [near, *ring(near, ("xl", "xh"), [0, 2, 1, 3])]
    col_mid, done = column_attention(place, col_rows, gain, turned, col_own, col_other)
    col_out = lax.all_to_all(col_mid.reshape(64, 4, HALF), SEQ, split_axis=0, concat_axis=0)

    rest_own = pack(done, plane).reshape(X * Y, 128, 640)
    rest_other = lax.ppermute(rest_own, "c", swap)
    base, low, last = row_attention(place, row_blocks, gain, rows, rest_own, rest_other)
    col_out = jnp.where(last[0] == 0, col_out, 0).reshape(STRIDE, HALF)

    mixed = pl.pallas_call(
        last_kernel,
        out_shape=jax.ShapeDtypeStruct((STRIDE, FEATURES), jnp.bfloat16),
        in_specs=[VMEM, VMEM, VMEM],
        out_specs=VMEM,
        compiler_params=PARAMS,
        name="mixed",
    )(base, col_out, low)
    return mixed.reshape(tokens.shape)


def solution(mesh):
    fine = Mesh(mesh.devices.reshape(XL, Y, XH, Z, C), ("xl", "y", "xh", "z", "c"))
    fsdp = ("xl", "y")
    return jax.shard_map(
        body,
        mesh=fine,
        in_specs=(P(fsdp, SEQ, None, None), P(), P(SEQ, fsdp), P(SEQ, fsdp), P(), P()),
        out_specs=P(fsdp, SEQ, None, None),
        check_vma=False,
    )
```

```python
import jax
import jax.numpy as jnp
from jax import lax
from jax.experimental import pallas as pl
from jax.experimental.pallas import tpu as pltpu
from jax.sharding import Mesh
from jax.sharding import PartitionSpec as P

XL, Y, XH, Z, C = 2, 4, 2, 16, 2
X = XH * XL
FEATURES, STRIDE, HEADS, HEAD_DIM = 1024, 256, 8, 64
HALF = HEADS * HEAD_DIM
WIDTH = 3 * HALF
PART = 384
SEQ = ("xh", "z", "c")
FAR = 1 << 20


def assemble(place, odd, refs, lanes, w_ref, first, width):
    x, y, core = place[0], place[1], place[2]
    for t in range(X):
        there = (x + t) & 3
        xh, xl = there >> 1, there & 1
        base = 512 * xh + 32 * ((1 - xl) if odd else xl)
        for s in range(Y):
            cols = pl.ds(pl.multiple_of(first + width * ((y + s) & 3), 128), width)
            for ref, c in ((refs[t], core), (refs[X + t], 1 - core)):
                for zz in range(Z // 2):
                    row = pl.multiple_of(base + 16 * c + 64 * zz, 16)
                    w_ref[pl.ds(row, 16), cols] = ref[s, pl.ds(16 * zz, 16), lanes]


def attend(reach_ref, gain_ref, x_ref, w_ref, n_ref, qkv_ref, out_ref, dist):
    def norm(i, _):
        rows = pl.ds(pl.multiple_of(i * 64, 64), 64)
        x = x_ref[rows, :].astype(jnp.float32)
        scale = lax.rsqrt(jnp.mean(x * x, axis=-1, keepdims=True) + 1e-05)
        n_ref[rows, :] = (x * scale * gain_ref[...]).astype(jnp.bfloat16)
        return 0

    lax.fori_loop(0, STRIDE // 64, norm, 0)

    def project(i, _):
        cols = pl.ds(pl.multiple_of(i * 256, 256), 256)
        qkv_ref[:, cols] = jnp.dot(
            n_ref[...], w_ref[:, cols], preferred_element_type=jnp.float32
        ).astype(jnp.bfloat16)
        return 0

    lax.fori_loop(0, WIDTH // 256, project, 0)

    for h in range(HEADS):
        q = qkv_ref[:, h * 64 : h * 64 + 64]
        k = qkv_ref[:, HALF + h * 64 : HALF + h * 64 + 64]
        v = qkv_ref[:, 2 * HALF + h * 64 : 2 * HALF + h * 64 + 64]
        s = lax.dot_general(
            q, k, (((1,), (1,)), ((), ())), preferred_element_type=jnp.float32
        )
        s = jnp.where(dist < reach_ref[h], s * 0.125, -1e30)
        p = jnp.exp(s - jnp.max(s, axis=-1, keepdims=True))
        o = jnp.dot(p.astype(jnp.bfloat16), v, preferred_element_type=jnp.float32)
        o = o / jnp.sum(p, axis=-1, keepdims=True)
        out_ref[:, h * 64 : h * 64 + 64] = o.astype(jnp.bfloat16)


def pairs():
    i = lax.broadcasted_iota(jnp.int32, (STRIDE, STRIDE), 0)
    return i, lax.broadcasted_iota(jnp.int32, (STRIDE, STRIDE), 1)


def column_kernel(place, reach_ref, gain_ref, x_ref, *refs):
    parts, (out_ref, w_ref, n_ref, qkv_ref) = refs[: 2 * X], refs[2 * X :]
    assemble(place, True, parts, slice(0, PART), w_ref, 0, PART)
    i, j = pairs()
    back = (i >> 2) - (j >> 2)
    dist = jnp.where((((i ^ j) & 3) == 0) & (back >= 0), back, FAR)
    attend(reach_ref, gain_ref, x_ref, w_ref, n_ref, qkv_ref, out_ref, dist)


def row_kernel(place, reach_ref, gain_ref, x_ref, *refs):
    parts = refs[: 2 * X]
    base_ref, low_ref, done_ref, w_ref, n_ref, qkv_ref, a_ref, o_ref = refs[2 * X :]
    done_ref[0] = 0
    assemble(place, False, parts, slice(0, PART), w_ref, 0, PART)
    i, j = pairs()
    dist = jnp.where(j <= i, (i >> 5) - (j >> 5), FAR)
    attend(reach_ref, gain_ref, x_ref, w_ref, n_ref, qkv_ref, a_ref, dist)
    assemble(place, False, parts, slice(PART, PART + 128), o_ref, 0, 128)
    assemble(place, True, parts, slice(PART + 128, PART + 256), o_ref, 512, 128)
    for n in range(0, FEATURES, 256):
        base_ref[:, n : n + 256] = x_ref[:, n : n + 256].astype(jnp.float32) + jnp.dot(
            a_ref[...], o_ref[:HALF, n : n + 256], preferred_element_type=jnp.float32
        )
    low_ref[...] = o_ref[HALF:, :]


def last_kernel(base_ref, col_ref, low_ref, out_ref):
    for n in range(0, FEATURES, 256):
        out_ref[:, n : n + 256] = (
            base_ref[:, n : n + 256]
            + jnp.dot(col_ref[...], low_ref[:, n : n + 256], preferred_element_type=jnp.float32)
        ).astype(jnp.bfloat16)


VMEM = pl.BlockSpec(memory_space=pltpu.VMEM)
SMEM = pl.BlockSpec(memory_space=pltpu.SMEM)
WORK = [
    pltpu.VMEM((FEATURES, WIDTH), jnp.bfloat16),
    pltpu.VMEM((STRIDE, FEATURES), jnp.bfloat16),
    pltpu.VMEM((STRIDE, WIDTH), jnp.bfloat16),
]
PARAMS = pltpu.CompilerParams(vmem_limit_bytes=40 * 1024 * 1024)
COST = pl.CostEstimate(
    flops=2 * 256 * 1024 * 1536 + 16 * 256 * 256 * 128,
    bytes_accessed=6 << 20,
    transcendentals=8 * 256 * 256,
)


def column_attention(place, reach, gain, x, parts):
    return pl.pallas_call(
        column_kernel,
        out_shape=jax.ShapeDtypeStruct((STRIDE, HALF), jnp.bfloat16),
        in_specs=[SMEM, SMEM] + [VMEM] * (2 + len(parts)),
        out_specs=VMEM,
        scratch_shapes=WORK,
        compiler_params=PARAMS,
        cost_estimate=COST,
        name="columns",
    )(place, reach, gain, x, *parts)


def row_attention(place, reach, gain, x, parts):
    return pl.pallas_call(
        row_kernel,
        out_shape=[
            jax.ShapeDtypeStruct((STRIDE, FEATURES), jnp.float32),
            jax.ShapeDtypeStruct((HALF, FEATURES), jnp.bfloat16),
            jax.ShapeDtypeStruct((1,), jnp.int32),
        ],
        in_specs=[SMEM, SMEM] + [VMEM] * (2 + len(parts)),
        out_specs=[VMEM, VMEM, SMEM],
        scratch_shapes=WORK
        + [
            pltpu.VMEM((STRIDE, HALF), jnp.bfloat16),
            pltpu.VMEM((FEATURES, FEATURES), jnp.bfloat16),
        ],
        compiler_params=PARAMS,
        cost_estimate=pl.CostEstimate(flops=1 << 20, bytes_accessed=1 << 20, transcendentals=0),
        name="rows",
    )(place, reach, gain, x, *parts)


def ring(part, axes, order):
    size = len(order)
    return [
        lax.ppermute(part, axes, [(order[i], order[(i - t) % size]) for i in range(size)])
        for t in range(1, size)
    ]


def body(tokens, norm_gain, w_qkv, w_out, row_blocks, col_rows):
    xl, y, xh, c = (lax.axis_index(a) for a in ("xl", "y", "xh", "c"))
    rows = tokens.reshape(STRIDE, FEATURES)
    gain = norm_gain.reshape(1, FEATURES)
    place = jnp.stack([2 * xh + xl, y, c]).astype(jnp.int32)

    block = jnp.concatenate([w_qkv, w_out], axis=1)
    change = [(a * Z + z, (a ^ (z & 1)) * Z + z) for a in range(XL) for z in range(Z)]
    block = lax.ppermute(block, ("xl", "z"), change)
    column = lax.all_to_all(jnp.broadcast_to(block, (Z, 16, 512)), "z", split_axis=0, concat_axis=0)

    sent, column = lax.optimization_barrier((rows, column))
    turned = lax.all_to_all(sent.reshape(64, 4, FEATURES), SEQ, split_axis=0, concat_axis=0)
    turned = turned.reshape(STRIDE, FEATURES)

    halves = column.reshape(Z // 2, 2, 16, 512)
    row_part = jnp.where(xl == 0, halves[:, 0], halves[:, 1]).reshape(128, 512)
    col_part = jnp.where(xl == 0, halves[:, 1], halves[:, 0]).reshape(128, 512)
    part = jnp.concatenate([col_part[:, :PART], row_part, col_part[:, PART:]], axis=1)
    near = jnp.stack([part, *ring(part, "y", range(Y))])

    def plane(part):
        return [part, *ring(part, ("xl", "xh"), [0, 2, 1, 3])]

    def both_cores(parts):
        return [*parts, *(lax.ppermute(a, "c", [(0, 1), (1, 0)]) for a in parts)]

    col_plane = plane(near[:, :, :PART])
    col_mid = column_attention(place, col_rows, gain, turned, both_cores(col_plane))
    col_out = lax.all_to_all(col_mid.reshape(64, 4, HALF), SEQ, split_axis=0, concat_axis=0)

    near_rest, _ = lax.optimization_barrier((near[:, :, PART:], col_plane))
    rest, _ = lax.optimization_barrier((plane(near_rest), col_mid))
    base, low, last = row_attention(place, row_blocks, gain, rows, both_cores(rest))
    col_out = jnp.where(last[0] == 0, col_out, 0).reshape(STRIDE, HALF)

    mixed = pl.pallas_call(
        last_kernel,
        out_shape=jax.ShapeDtypeStruct((STRIDE, FEATURES), jnp.bfloat16),
        in_specs=[VMEM, VMEM, VMEM],
        out_specs=VMEM,
        compiler_params=PARAMS,
        name="mixed",
    )(base, col_out, low)
    return mixed.reshape(tokens.shape)


def solution(mesh):
    fine = Mesh(mesh.devices.reshape(XL, Y, XH, Z, C), ("xl", "y", "xh", "z", "c"))
    fsdp = ("xl", "y")
    return jax.shard_map(
        body,
        mesh=fine,
        in_specs=(P(fsdp, SEQ, None, None), P(), P(SEQ, fsdp), P(SEQ, fsdp), P(), P()),
        out_specs=P(fsdp, SEQ, None, None),
        check_vma=False,
    )
```

```python
import jax
import jax.numpy as jnp
from jax import lax
from jax.experimental import pallas as pl
from jax.experimental.pallas import tpu as pltpu
from jax.sharding import Mesh
from jax.sharding import PartitionSpec as P

XL, Y, XH, Z, C = 2, 4, 2, 16, 2
X = XH * XL
FEATURES, STRIDE, HEADS, HEAD_DIM = 1024, 256, 8, 64
HALF = HEADS * HEAD_DIM
WIDTH = 3 * HALF
PART = 384
SEQ = ("xh", "z", "c")
FAR = 1 << 20


def assemble(place, odd, refs, lanes, w_ref, first, width):
    x, y, core = place[0], place[1], place[2]
    for t in range(X):
        there = (x + t) & 3
        xh, xl = there >> 1, there & 1
        base = 512 * xh + 32 * ((1 - xl) if odd else xl)
        for s in range(Y):
            cols = pl.ds(pl.multiple_of(first + width * ((y + s) & 3), 128), width)
            piece, at = divmod(t * Y + s, X * Y // (len(refs) // 2))
            for ref, c in ((refs[piece], core), (refs[len(refs) // 2 + piece], 1 - core)):
                for zz in range(Z // 2):
                    row = pl.multiple_of(base + 16 * c + 64 * zz, 16)
                    w_ref[pl.ds(row, 16), cols] = ref[at, pl.ds(16 * zz, 16), lanes]


def attend(reach_ref, gain_ref, x_ref, w_ref, n_ref, qkv_ref, out_ref, dist):
    def norm(i, _):
        rows = pl.ds(pl.multiple_of(i * 64, 64), 64)
        x = x_ref[rows, :].astype(jnp.float32)
        scale = lax.rsqrt(jnp.mean(x * x, axis=-1, keepdims=True) + 1e-05)
        n_ref[rows, :] = (x * scale * gain_ref[...]).astype(jnp.bfloat16)
        return 0

    lax.fori_loop(0, STRIDE // 64, norm, 0)

    def project(i, _):
        cols = pl.ds(pl.multiple_of(i * 256, 256), 256)
        qkv_ref[:, cols] = jnp.dot(
            n_ref[...], w_ref[:, cols], preferred_element_type=jnp.float32
        ).astype(jnp.bfloat16)
        return 0

    lax.fori_loop(0, WIDTH // 256, project, 0)

    for h in range(HEADS):
        q = qkv_ref[:, h * 64 : h * 64 + 64]
        k = qkv_ref[:, HALF + h * 64 : HALF + h * 64 + 64]
        v = qkv_ref[:, 2 * HALF + h * 64 : 2 * HALF + h * 64 + 64]
        s = lax.dot_general(
            q, k, (((1,), (1,)), ((), ())), preferred_element_type=jnp.float32
        )
        s = jnp.where(dist < reach_ref[h], s * 0.125, -1e30)
        p = jnp.exp(s - jnp.max(s, axis=-1, keepdims=True))
        o = jnp.dot(p.astype(jnp.bfloat16), v, preferred_element_type=jnp.float32)
        o = o / jnp.sum(p, axis=-1, keepdims=True)
        out_ref[:, h * 64 : h * 64 + 64] = o.astype(jnp.bfloat16)


def pairs():
    i = lax.broadcasted_iota(jnp.int32, (STRIDE, STRIDE), 0)
    return i, lax.broadcasted_iota(jnp.int32, (STRIDE, STRIDE), 1)


def column_kernel(place, reach_ref, gain_ref, x_ref, *refs):
    *parts, out_ref, w_ref, n_ref, qkv_ref = refs
    assemble(place, True, parts, slice(0, PART), w_ref, 0, PART)
    i, j = pairs()
    back = (i >> 2) - (j >> 2)
    dist = jnp.where((((i ^ j) & 3) == 0) & (back >= 0), back, FAR)
    attend(reach_ref, gain_ref, x_ref, w_ref, n_ref, qkv_ref, out_ref, dist)


def row_kernel(place, reach_ref, gain_ref, x_ref, *refs):
    *parts, base_ref, low_ref, done_ref, w_ref, n_ref, qkv_ref, a_ref, o_ref = refs
    done_ref[0] = 0
    assemble(place, False, parts, slice(0, PART), w_ref, 0, PART)
    i, j = pairs()
    dist = jnp.where(j <= i, (i >> 5) - (j >> 5), FAR)
    attend(reach_ref, gain_ref, x_ref, w_ref, n_ref, qkv_ref, a_ref, dist)
    assemble(place, False, parts, slice(PART, PART + 128), o_ref, 0, 128)
    assemble(place, True, parts, slice(PART + 128, PART + 256), o_ref, 512, 128)
    for n in range(0, FEATURES, 256):
        base_ref[:, n : n + 256] = x_ref[:, n : n + 256].astype(jnp.float32) + jnp.dot(
            a_ref[...], o_ref[:HALF, n : n + 256], preferred_element_type=jnp.float32
        )
    low_ref[...] = o_ref[HALF:, :]


def last_kernel(base_ref, col_ref, low_ref, out_ref):
    for n in range(0, FEATURES, 256):
        out_ref[:, n : n + 256] = (
            base_ref[:, n : n + 256]
            + jnp.dot(col_ref[...], low_ref[:, n : n + 256], preferred_element_type=jnp.float32)
        ).astype(jnp.bfloat16)


VMEM = pl.BlockSpec(memory_space=pltpu.VMEM)
SMEM = pl.BlockSpec(memory_space=pltpu.SMEM)
WORK = [
    pltpu.VMEM((FEATURES, WIDTH), jnp.bfloat16),
    pltpu.VMEM((STRIDE, FEATURES), jnp.bfloat16),
    pltpu.VMEM((STRIDE, WIDTH), jnp.bfloat16),
]
PARAMS = pltpu.CompilerParams(vmem_limit_bytes=24 * 1024 * 1024)
COST = pl.CostEstimate(
    flops=2 * 256 * 1024 * 1536 + 16 * 256 * 256 * 128,
    bytes_accessed=6 << 20,
    transcendentals=8 * 256 * 256,
)


def column_attention(place, reach, gain, x, parts):
    return pl.pallas_call(
        column_kernel,
        out_shape=jax.ShapeDtypeStruct((STRIDE, HALF), jnp.bfloat16),
        in_specs=[SMEM, SMEM] + [VMEM] * (2 + len(parts)),
        out_specs=VMEM,
        scratch_shapes=WORK,
        compiler_params=PARAMS,
        cost_estimate=COST,
        name="columns",
    )(place, reach, gain, x, *parts)


def row_attention(place, reach, gain, x, parts):
    return pl.pallas_call(
        row_kernel,
        out_shape=[
            jax.ShapeDtypeStruct((STRIDE, FEATURES), jnp.float32),
            jax.ShapeDtypeStruct((HALF, FEATURES), jnp.bfloat16),
            jax.ShapeDtypeStruct((1,), jnp.int32),
        ],
        in_specs=[SMEM, SMEM] + [VMEM] * (2 + len(parts)),
        out_specs=[VMEM, VMEM, SMEM],
        scratch_shapes=WORK
        + [
            pltpu.VMEM((STRIDE, HALF), jnp.bfloat16),
            pltpu.VMEM((FEATURES, FEATURES), jnp.bfloat16),
        ],
        compiler_params=PARAMS,
        cost_estimate=pl.CostEstimate(flops=1 << 20, bytes_accessed=1 << 20, transcendentals=0),
        name="rows",
    )(place, reach, gain, x, *parts)


def ring(part, axes, order):
    size = len(order)
    return [
        lax.ppermute(part, axes, [(order[i], order[(i - t) % size]) for i in range(size)])
        for t in range(1, size)
    ]


def body(tokens, norm_gain, w_qkv, w_out, row_blocks, col_rows):
    xl, y, xh, c = (lax.axis_index(a) for a in ("xl", "y", "xh", "c"))
    rows = tokens.reshape(STRIDE, FEATURES)
    gain = norm_gain.reshape(1, FEATURES)
    place = jnp.stack([2 * xh + xl, y, c]).astype(jnp.int32)

    block = jnp.concatenate([w_qkv, w_out], axis=1)
    change = [(a * Z + z, (a ^ (z & 1)) * Z + z) for a in range(XL) for z in range(Z)]
    block = lax.ppermute(block, ("xl", "z"), change)
    column = lax.all_to_all(jnp.broadcast_to(block, (Z, 16, 512)), "z", split_axis=0, concat_axis=0)

    sent, column = lax.optimization_barrier((rows.reshape(64, 4, FEATURES), column))
    turned = lax.all_to_all(sent, SEQ, split_axis=0, concat_axis=0)
    turned = turned.reshape(STRIDE, FEATURES)

    halves = column.reshape(Z // 2, 2, 16, 512)
    row_part = jnp.where(xl == 0, halves[:, 0], halves[:, 1]).reshape(128, 512)
    col_part = jnp.where(xl == 0, halves[:, 1], halves[:, 0]).reshape(128, 512)
    rest_part = jnp.concatenate([row_part, col_part[:, PART:]], axis=1)

    def near(part):
        return jnp.stack([part, *ring(part, "y", range(Y))])

    def plane(part):
        return [part, *ring(part, ("xl", "xh"), [0, 2, 1, 3])]

    def both_cores(parts, pieces):
        size = X // pieces
        if size > 1:
            parts = [jnp.concatenate(parts[i : i + size]) for i in range(0, X, size)]
        return [*parts, *(lax.ppermute(a, "c", [(0, 1), (1, 0)]) for a in parts)]

    col_near = near(col_part[:, :PART])
    rest_part, _ = lax.optimization_barrier((rest_part, col_near))
    col_plane, rest_near = lax.optimization_barrier((plane(col_near), near(rest_part)))
    col_mid = column_attention(place, col_rows, gain, turned, both_cores(col_plane, 2))
    col_out = lax.all_to_all(col_mid.reshape(64, 4, HALF), SEQ, split_axis=0, concat_axis=0)

    rest, _ = lax.optimization_barrier((plane(rest_near), col_mid))
    base, low, last = row_attention(place, row_blocks, gain, rows, both_cores(rest, 4))
    col_out = jnp.where(last[0] == 0, col_out, 0).reshape(STRIDE, HALF)

    mixed = pl.pallas_call(
        last_kernel,
        out_shape=jax.ShapeDtypeStruct((STRIDE, FEATURES), jnp.bfloat16),
        in_specs=[VMEM, VMEM, VMEM],
        out_specs=VMEM,
        compiler_params=PARAMS,
        name="mixed",
    )(base, col_out, low)
    return mixed.reshape(tokens.shape)


def solution(mesh):
    fine = Mesh(mesh.devices.reshape(XL, Y, XH, Z, C), ("xl", "y", "xh", "z", "c"))
    fsdp = ("xl", "y")
    return jax.shard_map(
        body,
        mesh=fine,
        in_specs=(P(fsdp, SEQ, None, None), P(), P(SEQ, fsdp), P(SEQ, fsdp), P(), P()),
        out_specs=P(fsdp, SEQ, None, None),
        check_vma=False,
    )
```

```python
import math

import jax
import jax.numpy as jnp
from jax import lax
from jax.experimental import pallas as pl
from jax.experimental.pallas import tpu as pltpu
from jax.sharding import Mesh
from jax.sharding import PartitionSpec as P

XL, Y, XH, Z, C = 2, 4, 2, 16, 2
X = XH * XL
FEATURES, STRIDE, HEADS, HEAD_DIM = 1024, 256, 8, 64
HALF = HEADS * HEAD_DIM
WIDTH = 3 * HALF
PART = 384
SEQ = ("xh", "z", "c")
FAR = 1 << 20
COLUMN_PIECES = (1, 3)
REST_PIECES = (1, 1, 1, 1)


def assemble(place, odd, refs, sizes, lanes, w_ref, first, width):
    x, y, core = place[0], place[1], place[2]
    pieces = [(i, j) for i, size in enumerate(sizes) for j in range(size)]
    for t in range(X):
        there = (x + t) & 3
        xh, xl = there >> 1, there & 1
        turn = 32 * ((1 - xl) if odd else xl)
        piece, at = pieces[t]
        for s in range(Y):
            cols = pl.ds(pl.multiple_of(first + width * ((y + s) & 3), 128), width)
            for ref, c in ((refs[piece], core), (refs[len(sizes) + piece], 1 - core)):
                rows = pl.ds(pl.multiple_of(turn + 16 * c, 16), 16)
                block = ref[at * Y + s, :, lanes].reshape(Z // 2, 16, width)
                w_ref[pl.ds(Z // 2 * xh, Z // 2), rows, cols] = block


def attend(reach_ref, gain_ref, x_ref, w_ref, n_ref, qkv_ref, out_ref, dist):
    def norm(i, _):
        rows = pl.ds(pl.multiple_of(i * 64, 64), 64)
        x = x_ref[rows, :].astype(jnp.float32)
        scale = lax.rsqrt(jnp.mean(x * x, axis=-1, keepdims=True) + 1e-05)
        n_ref[rows, :] = (x * scale * gain_ref[...]).astype(jnp.bfloat16)
        return 0

    lax.fori_loop(0, STRIDE // 64, norm, 0)

    def project(i, _):
        cols = pl.ds(pl.multiple_of(i * 256, 256), 256)
        qkv_ref[:, cols] = jnp.dot(
            n_ref[...],
            w_ref[:, :, cols].reshape(FEATURES, 256),
            preferred_element_type=jnp.float32,
        ).astype(jnp.bfloat16)
        return 0

    lax.fori_loop(0, WIDTH // 256, project, 0)

    lane = lax.broadcasted_iota(jnp.int32, (STRIDE, 128), 1)
    low = (lane < 64).astype(jnp.float32)
    masks = [low.astype(jnp.bfloat16), (1.0 - low).astype(jnp.bfloat16)]
    scale = 0.125 * math.log2(math.e)
    mid = STRIDE // 2
    for h in range(0, HEADS, 2):
        q, k, v = (qkv_ref[:, n * HALF + h * 64 : n * HALF + h * 64 + 128] for n in range(3))
        done = []
        for e in range(2):
            reach = reach_ref[h + e]
            qe = q * masks[e]
            ve = v * masks[e] + masks[1 - e]
            for first, seen in ((0, mid), (mid, STRIDE)):
                s = lax.dot_general(
                    qe[first : first + mid],
                    k[:seen],
                    (((1,), (1,)), ((), ())),
                    preferred_element_type=jnp.float32,
                )
                s = jnp.where(dist[first : first + mid, :seen] < reach, s * scale, -1e30)
                p = jnp.exp2(s - jnp.max(s, axis=-1, keepdims=True)).astype(jnp.bfloat16)
                o = jnp.dot(p, ve[:seen], preferred_element_type=jnp.float32)
                done.append(o / pltpu.roll(o, 64, 1))
        for i, first in enumerate((0, mid)):
            both = jnp.where(lane[:mid] < 64, done[i], done[2 + i])
            out_ref[first : first + mid, h * 64 : h * 64 + 128] = both.astype(jnp.bfloat16)


def pairs():
    i = lax.broadcasted_iota(jnp.int32, (STRIDE, STRIDE), 0)
    return i, lax.broadcasted_iota(jnp.int32, (STRIDE, STRIDE), 1)


def column_kernel(place, reach_ref, gain_ref, x_ref, *refs):
    *parts, out_ref, w_ref, n_ref, qkv_ref = refs
    assemble(place, True, parts, COLUMN_PIECES, slice(0, PART), w_ref, 0, PART)
    i, j = pairs()
    back = (i >> 2) - (j >> 2)
    dist = jnp.where((((i ^ j) & 3) == 0) & (back >= 0), back, FAR)
    attend(reach_ref, gain_ref, x_ref, w_ref, n_ref, qkv_ref, out_ref, dist)


def row_kernel(place, reach_ref, gain_ref, x_ref, *refs):
    *parts, base_ref, low_ref, done_ref, w_ref, n_ref, qkv_ref, a_ref, o_ref = refs
    done_ref[0] = 0
    assemble(place, False, parts, REST_PIECES, slice(0, PART), w_ref, 0, PART)
    i, j = pairs()
    dist = jnp.where(j <= i, (i >> 5) - (j >> 5), FAR)
    attend(reach_ref, gain_ref, x_ref, w_ref, n_ref, qkv_ref, a_ref, dist)
    assemble(place, False, parts, REST_PIECES, slice(PART, PART + 128), o_ref, 0, 128)
    assemble(place, True, parts, REST_PIECES, slice(PART + 128, PART + 256), o_ref, 512, 128)
    for n in range(0, FEATURES, 256):
        base_ref[:, n : n + 256] = x_ref[:, n : n + 256].astype(jnp.float32) + jnp.dot(
            a_ref[...],
            o_ref[: Z // 2, :, n : n + 256].reshape(HALF, 256),
            preferred_element_type=jnp.float32,
        )
    low_ref[...] = o_ref[Z // 2 :].reshape(HALF, FEATURES)


def last_kernel(base_ref, col_ref, low_ref, out_ref):
    for n in range(0, FEATURES, 256):
        out_ref[:, n : n + 256] = (
            base_ref[:, n : n + 256]
            + jnp.dot(col_ref[...], low_ref[:, n : n + 256], preferred_element_type=jnp.float32)
        ).astype(jnp.bfloat16)


VMEM = pl.BlockSpec(memory_space=pltpu.VMEM)
SMEM = pl.BlockSpec(memory_space=pltpu.SMEM)
WORK = [
    pltpu.VMEM((Z, 64, WIDTH), jnp.bfloat16),
    pltpu.VMEM((STRIDE, FEATURES), jnp.bfloat16),
    pltpu.VMEM((STRIDE, WIDTH), jnp.bfloat16),
]
PARAMS = pltpu.CompilerParams(vmem_limit_bytes=24 * 1024 * 1024)
COST = pl.CostEstimate(
    flops=2 * 256 * 1024 * 1536 + 16 * 256 * 256 * 128,
    bytes_accessed=6 << 20,
    transcendentals=8 * 256 * 256,
)


def column_attention(place, reach, gain, x, parts):
    return pl.pallas_call(
        column_kernel,
        out_shape=jax.ShapeDtypeStruct((STRIDE, HALF), jnp.bfloat16),
        in_specs=[SMEM, SMEM] + [VMEM] * (2 + len(parts)),
        out_specs=VMEM,
        scratch_shapes=WORK,
        compiler_params=PARAMS,
        cost_estimate=COST,
        name="columns",
    )(place, reach, gain, x, *parts)


def row_attention(place, reach, gain, x, parts):
    return pl.pallas_call(
        row_kernel,
        out_shape=[
            jax.ShapeDtypeStruct((STRIDE, FEATURES), jnp.float32),
            jax.ShapeDtypeStruct((HALF, FEATURES), jnp.bfloat16),
            jax.ShapeDtypeStruct((1,), jnp.int32),
        ],
        in_specs=[SMEM, SMEM] + [VMEM] * (2 + len(parts)),
        out_specs=[VMEM, VMEM, SMEM],
        scratch_shapes=WORK
        + [
            pltpu.VMEM((STRIDE, HALF), jnp.bfloat16),
            pltpu.VMEM((Z, 64, FEATURES), jnp.bfloat16),
        ],
        compiler_params=PARAMS,
        cost_estimate=pl.CostEstimate(flops=1 << 20, bytes_accessed=1 << 20, transcendentals=0),
        name="rows",
    )(place, reach, gain, x, *parts)


def ring(part, axes, order):
    size = len(order)
    return [
        lax.ppermute(part, axes, [(order[i], order[(i - t) % size]) for i in range(size)])
        for t in range(1, size)
    ]


def body(tokens, norm_gain, w_qkv, w_out, row_blocks, col_rows):
    xl, y, xh, c = (lax.axis_index(a) for a in ("xl", "y", "xh", "c"))
    rows = tokens.reshape(STRIDE, FEATURES)
    gain = norm_gain.reshape(1, FEATURES)
    place = jnp.stack([2 * xh + xl, y, c]).astype(jnp.int32)

    block = jnp.concatenate([w_qkv, w_out], axis=1)
    change = [(a * Z + z, (a ^ (z & 1)) * Z + z) for a in range(XL) for z in range(Z)]
    block = lax.ppermute(block, ("xl", "z"), change)
    column = lax.all_to_all(jnp.broadcast_to(block, (Z, 16, 512)), "z", split_axis=0, concat_axis=0)

    sent, column = lax.optimization_barrier((rows.reshape(64, 4, FEATURES), column))
    turned = lax.all_to_all(sent, SEQ, split_axis=0, concat_axis=0)
    turned = turned.reshape(STRIDE, FEATURES)

    halves = column.reshape(Z // 2, 2, 16, 512)
    row_part = jnp.where(xl == 0, halves[:, 0], halves[:, 1]).reshape(128, 512)
    col_part = jnp.where(xl == 0, halves[:, 1], halves[:, 0]).reshape(128, 512)
    part = jnp.concatenate([col_part[:, :PART], row_part, col_part[:, PART:]], axis=1)
    near = jnp.stack([part, *ring(part, "y", range(Y))])

    def plane(part):
        return [part, *ring(part, ("xl", "xh"), [0, 2, 1, 3])]

    def both_cores(parts, sizes):
        ends = [sum(sizes[: i + 1]) for i in range(len(sizes))]
        joined = [
            parts[e - n] if n == 1 else jnp.concatenate(parts[e - n : e])
            for e, n in zip(ends, sizes, strict=True)
        ]
        return [*joined, *(lax.ppermute(a, "c", [(0, 1), (1, 0)]) for a in joined)]

    col_plane = plane(near[:, :, :PART])
    col_mid = column_attention(place, col_rows, gain, turned, both_cores(col_plane, COLUMN_PIECES))
    col_out = lax.all_to_all(col_mid.reshape(64, 4, HALF), SEQ, split_axis=0, concat_axis=0)

    near_rest, _ = lax.optimization_barrier((near[:, :, PART:], col_plane))
    rest, _ = lax.optimization_barrier((plane(near_rest), col_mid))
    base, low, last = row_attention(place, row_blocks, gain, rows, both_cores(rest, REST_PIECES))
    col_out = jnp.where(last[0] == 0, col_out, 0).reshape(STRIDE, HALF)

    mixed = pl.pallas_call(
        last_kernel,
        out_shape=jax.ShapeDtypeStruct((STRIDE, FEATURES), jnp.bfloat16),
        in_specs=[VMEM, VMEM, VMEM],
        out_specs=VMEM,
        compiler_params=PARAMS,
        name="mixed",
    )(base, col_out, low)
    return mixed.reshape(tokens.shape)


def solution(mesh):
    fine = Mesh(mesh.devices.reshape(XL, Y, XH, Z, C), ("xl", "y", "xh", "z", "c"))
    fsdp = ("xl", "y")
    return jax.shard_map(
        body,
        mesh=fine,
        in_specs=(P(fsdp, SEQ, None, None), P(), P(SEQ, fsdp), P(SEQ, fsdp), P(), P()),
        out_specs=P(fsdp, SEQ, None, None),
        check_vma=False,
    )
```

```python
import math

import jax
import jax.numpy as jnp
from jax import lax
from jax.experimental import pallas as pl
from jax.experimental.pallas import tpu as pltpu
from jax.sharding import Mesh
from jax.sharding import PartitionSpec as P

XL, Y, XH, Z, C = 2, 4, 2, 16, 2
X = XH * XL
FEATURES, STRIDE, HEADS, HEAD_DIM = 1024, 256, 8, 64
HALF = HEADS * HEAD_DIM
WIDTH = 3 * HALF
PART = 384
SEQ = ("xh", "z", "c")
FAR = 1 << 20
COLUMN_PIECES = (1, 3)
REST_PIECES = (1, 1, 1, 1)


def assemble(place, odd, refs, sizes, lanes, w_ref, first, width):
    x, y, core = place[0], place[1], place[2]
    pieces = [(i, j) for i, size in enumerate(sizes) for j in range(size)]
    for t in range(Y):
        cols = pl.ds(pl.multiple_of(first + width * ((y + t) & 3), 128), width)
        piece, at = pieces[t]
        for s in range(X):
            there = (x + s) & 3
            xh, xl = there >> 1, there & 1
            turn = 32 * ((1 - xl) if odd else xl)
            for ref, c in ((refs[piece], core), (refs[len(sizes) + piece], 1 - core)):
                rows = pl.ds(pl.multiple_of(turn + 16 * c, 16), 16)
                block = ref[at * X + s, :, lanes].reshape(Z // 2, 16, width)
                w_ref[pl.ds(Z // 2 * xh, Z // 2), rows, cols] = block


def attend(reach_ref, gain_ref, x_ref, w_ref, n_ref, qkv_ref, out_ref, dist):
    def norm(i, _):
        rows = pl.ds(pl.multiple_of(i * 64, 64), 64)
        x = x_ref[rows, :].astype(jnp.float32)
        scale = lax.rsqrt(jnp.mean(x * x, axis=-1, keepdims=True) + 1e-05)
        n_ref[rows, :] = (x * scale * gain_ref[...]).astype(jnp.bfloat16)
        return 0

    lax.fori_loop(0, STRIDE // 64, norm, 0)

    def project(i, _):
        cols = pl.ds(pl.multiple_of(i * 256, 256), 256)
        qkv_ref[:, cols] = jnp.dot(
            n_ref[...],
            w_ref[:, :, cols].reshape(FEATURES, 256),
            preferred_element_type=jnp.float32,
        ).astype(jnp.bfloat16)
        return 0

    lax.fori_loop(0, WIDTH // 256, project, 0)

    lane = lax.broadcasted_iota(jnp.int32, (STRIDE, 128), 1)
    low = (lane < 64).astype(jnp.float32)
    masks = [low.astype(jnp.bfloat16), (1.0 - low).astype(jnp.bfloat16)]
    scale = 0.125 * math.log2(math.e)
    mid = STRIDE // 2
    for h in range(0, HEADS, 2):
        q, k, v = (qkv_ref[:, n * HALF + h * 64 : n * HALF + h * 64 + 128] for n in range(3))
        done = []
        for e in range(2):
            reach = reach_ref[h + e]
            qe = q * masks[e]
            ve = v * masks[e] + masks[1 - e]
            for first, seen in ((0, mid), (mid, STRIDE)):
                s = lax.dot_general(
                    qe[first : first + mid],
                    k[:seen],
                    (((1,), (1,)), ((), ())),
                    preferred_element_type=jnp.float32,
                )
                s = jnp.where(dist[first : first + mid, :seen] < reach, s * scale, -1e30)
                p = jnp.exp2(s - jnp.max(s, axis=-1, keepdims=True)).astype(jnp.bfloat16)
                o = jnp.dot(p, ve[:seen], preferred_element_type=jnp.float32)
                done.append(o / pltpu.roll(o, 64, 1))
        for i, first in enumerate((0, mid)):
            both = jnp.where(lane[:mid] < 64, done[i], done[2 + i])
            out_ref[first : first + mid, h * 64 : h * 64 + 128] = both.astype(jnp.bfloat16)


def pairs():
    i = lax.broadcasted_iota(jnp.int32, (STRIDE, STRIDE), 0)
    return i, lax.broadcasted_iota(jnp.int32, (STRIDE, STRIDE), 1)


def column_kernel(place, reach_ref, gain_ref, x_ref, *refs):
    *parts, out_ref, w_ref, n_ref, qkv_ref = refs
    assemble(place, True, parts, COLUMN_PIECES, slice(0, PART), w_ref, 0, PART)
    i, j = pairs()
    back = (i >> 2) - (j >> 2)
    dist = jnp.where((((i ^ j) & 3) == 0) & (back >= 0), back, FAR)
    attend(reach_ref, gain_ref, x_ref, w_ref, n_ref, qkv_ref, out_ref, dist)


def row_kernel(place, reach_ref, gain_ref, x_ref, *refs):
    *parts, base_ref, low_ref, done_ref, w_ref, n_ref, qkv_ref, a_ref, o_ref = refs
    done_ref[0] = 0
    assemble(place, False, parts, REST_PIECES, slice(0, PART), w_ref, 0, PART)
    i, j = pairs()
    dist = jnp.where(j <= i, (i >> 5) - (j >> 5), FAR)
    attend(reach_ref, gain_ref, x_ref, w_ref, n_ref, qkv_ref, a_ref, dist)
    assemble(place, False, parts, REST_PIECES, slice(PART, PART + 128), o_ref, 0, 128)
    assemble(place, True, parts, REST_PIECES, slice(PART + 128, PART + 256), o_ref, 512, 128)
    for n in range(0, FEATURES, 256):
        base_ref[:, n : n + 256] = x_ref[:, n : n + 256].astype(jnp.float32) + jnp.dot(
            a_ref[...],
            o_ref[: Z // 2, :, n : n + 256].reshape(HALF, 256),
            preferred_element_type=jnp.float32,
        )
    low_ref[...] = o_ref[Z // 2 :].reshape(HALF, FEATURES)


def last_kernel(base_ref, col_ref, low_ref, out_ref):
    for n in range(0, FEATURES, 256):
        out_ref[:, n : n + 256] = (
            base_ref[:, n : n + 256]
            + jnp.dot(col_ref[...], low_ref[:, n : n + 256], preferred_element_type=jnp.float32)
        ).astype(jnp.bfloat16)


VMEM = pl.BlockSpec(memory_space=pltpu.VMEM)
SMEM = pl.BlockSpec(memory_space=pltpu.SMEM)
WORK = [
    pltpu.VMEM((Z, 64, WIDTH), jnp.bfloat16),
    pltpu.VMEM((STRIDE, FEATURES), jnp.bfloat16),
    pltpu.VMEM((STRIDE, WIDTH), jnp.bfloat16),
]
PARAMS = pltpu.CompilerParams(vmem_limit_bytes=24 * 1024 * 1024)
COST = pl.CostEstimate(
    flops=2 * 256 * 1024 * 1536 + 16 * 256 * 256 * 128,
    bytes_accessed=6 << 20,
    transcendentals=8 * 256 * 256,
)


def column_attention(place, reach, gain, x, parts):
    return pl.pallas_call(
        column_kernel,
        out_shape=jax.ShapeDtypeStruct((STRIDE, HALF), jnp.bfloat16),
        in_specs=[SMEM, SMEM] + [VMEM] * (2 + len(parts)),
        out_specs=VMEM,
        scratch_shapes=WORK,
        compiler_params=PARAMS,
        cost_estimate=COST,
        name="columns",
    )(place, reach, gain, x, *parts)


def row_attention(place, reach, gain, x, parts):
    return pl.pallas_call(
        row_kernel,
        out_shape=[
            jax.ShapeDtypeStruct((STRIDE, FEATURES), jnp.float32),
            jax.ShapeDtypeStruct((HALF, FEATURES), jnp.bfloat16),
            jax.ShapeDtypeStruct((1,), jnp.int32),
        ],
        in_specs=[SMEM, SMEM] + [VMEM] * (2 + len(parts)),
        out_specs=[VMEM, VMEM, SMEM],
        scratch_shapes=WORK
        + [
            pltpu.VMEM((STRIDE, HALF), jnp.bfloat16),
            pltpu.VMEM((Z, 64, FEATURES), jnp.bfloat16),
        ],
        compiler_params=PARAMS,
        cost_estimate=pl.CostEstimate(flops=1 << 20, bytes_accessed=1 << 20, transcendentals=0),
        name="rows",
    )(place, reach, gain, x, *parts)


def ring(part, axes, order):
    size = len(order)
    return [
        lax.ppermute(part, axes, [(order[i], order[(i - t) % size]) for i in range(size)])
        for t in range(1, size)
    ]


def body(tokens, norm_gain, w_qkv, w_out, row_blocks, col_rows):
    xl, y, xh, c = (lax.axis_index(a) for a in ("xl", "y", "xh", "c"))
    rows = tokens.reshape(STRIDE, FEATURES)
    gain = norm_gain.reshape(1, FEATURES)
    place = jnp.stack([2 * xh + xl, y, c]).astype(jnp.int32)

    block = jnp.concatenate([w_qkv, w_out], axis=1)
    change = [(a * Z + z, (a ^ (z & 1)) * Z + z) for a in range(XL) for z in range(Z)]
    block = lax.ppermute(block, ("xl", "z"), change)
    column = lax.all_to_all(jnp.broadcast_to(block, (Z, 16, 512)), "z", split_axis=0, concat_axis=0)

    sent, column = lax.optimization_barrier((rows.reshape(64, 4, FEATURES), column))
    turned = lax.all_to_all(sent, SEQ, split_axis=0, concat_axis=0)
    turned = turned.reshape(STRIDE, FEATURES)

    halves = column.reshape(Z // 2, 2, 16, 512)
    row_part = jnp.where(xl == 0, halves[:, 0], halves[:, 1]).reshape(128, 512)
    col_part = jnp.where(xl == 0, halves[:, 1], halves[:, 0]).reshape(128, 512)
    part = jnp.concatenate([col_part[:, :PART], row_part, col_part[:, PART:]], axis=1)
    near = jnp.stack([part, *ring(part, ("xl", "xh"), [0, 2, 1, 3])])

    def plane(part):
        return [part, *ring(part, "y", range(Y))]

    def both_cores(parts, sizes):
        ends = [sum(sizes[: i + 1]) for i in range(len(sizes))]
        joined = [
            parts[e - n] if n == 1 else jnp.concatenate(parts[e - n : e])
            for e, n in zip(ends, sizes, strict=True)
        ]
        return [*joined, *(lax.ppermute(a, "c", [(0, 1), (1, 0)]) for a in joined)]

    col_plane = plane(near[:, :, :PART])
    col_mid = column_attention(place, col_rows, gain, turned, both_cores(col_plane, COLUMN_PIECES))
    col_out = lax.all_to_all(col_mid.reshape(64, 4, HALF), SEQ, split_axis=0, concat_axis=0)

    near_rest, _ = lax.optimization_barrier((near[:, :, PART:], col_plane))
    rest, _ = lax.optimization_barrier((plane(near_rest), col_mid))
    base, low, last = row_attention(place, row_blocks, gain, rows, both_cores(rest, REST_PIECES))
    col_out = jnp.where(last[0] == 0, col_out, 0).reshape(STRIDE, HALF)

    mixed = pl.pallas_call(
        last_kernel,
        out_shape=jax.ShapeDtypeStruct((STRIDE, FEATURES), jnp.bfloat16),
        in_specs=[VMEM, VMEM, VMEM],
        out_specs=VMEM,
        compiler_params=PARAMS,
        name="mixed",
    )(base, col_out, low)
    return mixed.reshape(tokens.shape)


def solution(mesh):
    fine = Mesh(mesh.devices.reshape(XL, Y, XH, Z, C), ("xl", "y", "xh", "z", "c"))
    fsdp = ("xl", "y")
    return jax.shard_map(
        body,
        mesh=fine,
        in_specs=(P(fsdp, SEQ, None, None), P(), P(SEQ, fsdp), P(SEQ, fsdp), P(), P()),
        out_specs=P(fsdp, SEQ, None, None),
        check_vma=False,
    )
```

```python
import math

import jax
import jax.numpy as jnp
from jax import lax
from jax.experimental import pallas as pl
from jax.experimental.pallas import tpu as pltpu
from jax.sharding import Mesh
from jax.sharding import PartitionSpec as P

XL, Y, XH, Z, C = 2, 4, 2, 16, 2
X = XH * XL
FEATURES, STRIDE, HEADS, HEAD_DIM = 1024, 256, 8, 64
HALF = HEADS * HEAD_DIM
WIDTH = 3 * HALF
PART = 384
SEQ = ("xh", "z", "c")
FAR = 1 << 20
COLUMN_PIECES = (1, 3)
REST_PIECES = (1, 1, 1, 1)


def assemble(place, odd, refs, sizes, lanes, w_ref, first, width):
    x, y, core = place[0], place[1], place[2]
    pieces = [(i, j) for i, size in enumerate(sizes) for j in range(size)]
    for t in range(Y):
        cols = pl.ds(pl.multiple_of(first + width * ((y + t) & 3), 128), width)
        piece, at = pieces[t]
        for s in range(X):
            there = (x + s) & 3
            xh, xl = there >> 1, there & 1
            turn = 32 * ((1 - xl) if odd else xl)
            for ref, c in ((refs[piece], core), (refs[len(sizes) + piece], 1 - core)):
                rows = pl.ds(pl.multiple_of(turn + 16 * c, 16), 16)
                block = ref[at * X + s, :, lanes].reshape(Z // 2, 16, width)
                w_ref[pl.ds(Z // 2 * xh, Z // 2), rows, cols] = block


def attend(reach_ref, gain_ref, x_ref, w_ref, n_ref, qkv_ref, out_ref, dist):
    def norm(i, _):
        rows = pl.ds(pl.multiple_of(i * 64, 64), 64)
        x = x_ref[rows, :].astype(jnp.float32)
        scale = lax.rsqrt(jnp.mean(x * x, axis=-1, keepdims=True) + 1e-05)
        n_ref[rows, :] = (x * scale * gain_ref[...]).astype(jnp.bfloat16)
        return 0

    lax.fori_loop(0, STRIDE // 64, norm, 0)

    for n in range(0, WIDTH, 512):
        qkv_ref[:, n : n + 512] = jnp.dot(
            n_ref[...],
            w_ref[:, :, n : n + 512].reshape(FEATURES, 512),
            preferred_element_type=jnp.float32,
        ).astype(jnp.bfloat16)

    lane = lax.broadcasted_iota(jnp.int32, (STRIDE // 2, 128), 1)
    low = (lane < 64).astype(jnp.float32)
    masks = [low.astype(jnp.bfloat16), (1.0 - low).astype(jnp.bfloat16)]
    scale = 0.125 * math.log2(math.e)
    mid = STRIDE // 2
    for h in range(0, HEADS, 2):
        for first, seen in ((0, mid), (mid, STRIDE)):
            q, k, v = (qkv_ref[:, n * HALF + h * 64 : n * HALF + h * 64 + 128] for n in range(3))
            q = q[first : first + mid]
            s = lax.dot_general(
                jnp.concatenate([q * masks[0], q * masks[1]]),
                k[:seen],
                (((1,), (1,)), ((), ())),
                preferred_element_type=jnp.float32,
            )
            near = dist[first : first + mid, :seen]
            ps, sums = [], []
            for e in range(2):
                se = jnp.where(near < reach_ref[h + e], s[e * mid : e * mid + mid] * scale, -1e30)
                p = jnp.exp2(se - jnp.max(se, axis=-1, keepdims=True))
                sums.append(jnp.sum(p, axis=-1, keepdims=True))
                ps.append(p.astype(jnp.bfloat16))
            o = jnp.dot(jnp.concatenate(ps), v[:seen], preferred_element_type=jnp.float32)
            both = jnp.where(lane < 64, o[:mid] / sums[0], o[mid:] / sums[1])
            out_ref[first : first + mid, h * 64 : h * 64 + 128] = both.astype(jnp.bfloat16)


def pairs():
    i = lax.broadcasted_iota(jnp.int32, (STRIDE, STRIDE), 0)
    return i, lax.broadcasted_iota(jnp.int32, (STRIDE, STRIDE), 1)


def column_kernel(place, reach_ref, gain_ref, x_ref, *refs):
    *parts, out_ref, w_ref, n_ref, qkv_ref = refs
    assemble(place, True, parts, COLUMN_PIECES, slice(0, PART), w_ref, 0, PART)
    i, j = pairs()
    back = (i >> 2) - (j >> 2)
    dist = jnp.where((((i ^ j) & 3) == 0) & (back >= 0), back, FAR)
    attend(reach_ref, gain_ref, x_ref, w_ref, n_ref, qkv_ref, out_ref, dist)


def row_kernel(place, reach_ref, gain_ref, x_ref, *refs):
    *parts, base_ref, low_ref, done_ref, w_ref, n_ref, qkv_ref, a_ref, o_ref = refs
    done_ref[0] = 0
    assemble(place, False, parts, REST_PIECES, slice(0, PART), w_ref, 0, PART)
    i, j = pairs()
    dist = jnp.where(j <= i, (i >> 5) - (j >> 5), FAR)
    attend(reach_ref, gain_ref, x_ref, w_ref, n_ref, qkv_ref, a_ref, dist)
    assemble(place, False, parts, REST_PIECES, slice(PART, PART + 128), o_ref, 0, 128)
    assemble(place, True, parts, REST_PIECES, slice(PART + 128, PART + 256), o_ref, 512, 128)
    for n in range(0, FEATURES, 256):
        base_ref[:, n : n + 256] = x_ref[:, n : n + 256].astype(jnp.float32) + jnp.dot(
            a_ref[...],
            o_ref[: Z // 2, :, n : n + 256].reshape(HALF, 256),
            preferred_element_type=jnp.float32,
        )
    low_ref[...] = o_ref[Z // 2 :].reshape(HALF, FEATURES)


def last_kernel(base_ref, col_ref, low_ref, out_ref):
    for n in range(0, FEATURES, 256):
        out_ref[:, n : n + 256] = (
            base_ref[:, n : n + 256]
            + jnp.dot(col_ref[...], low_ref[:, n : n + 256], preferred_element_type=jnp.float32)
        ).astype(jnp.bfloat16)


VMEM = pl.BlockSpec(memory_space=pltpu.VMEM)
SMEM = pl.BlockSpec(memory_space=pltpu.SMEM)
WORK = [
    pltpu.VMEM((Z, 64, WIDTH), jnp.bfloat16),
    pltpu.VMEM((STRIDE, FEATURES), jnp.bfloat16),
    pltpu.VMEM((STRIDE, WIDTH), jnp.bfloat16),
]
PARAMS = pltpu.CompilerParams(vmem_limit_bytes=24 * 1024 * 1024)
COST = pl.CostEstimate(
    flops=2 * 256 * 1024 * 1536 + 16 * 256 * 256 * 128,
    bytes_accessed=6 << 20,
    transcendentals=8 * 256 * 256,
)


def column_attention(place, reach, gain, x, parts):
    return pl.pallas_call(
        column_kernel,
        out_shape=jax.ShapeDtypeStruct((STRIDE, HALF), jnp.bfloat16),
        in_specs=[SMEM, SMEM] + [VMEM] * (2 + len(parts)),
        out_specs=VMEM,
        scratch_shapes=WORK,
        compiler_params=PARAMS,
        cost_estimate=COST,
        name="columns",
    )(place, reach, gain, x, *parts)


def row_attention(place, reach, gain, x, parts):
    return pl.pallas_call(
        row_kernel,
        out_shape=[
            jax.ShapeDtypeStruct((STRIDE, FEATURES), jnp.float32),
            jax.ShapeDtypeStruct((HALF, FEATURES), jnp.bfloat16),
            jax.ShapeDtypeStruct((1,), jnp.int32),
        ],
        in_specs=[SMEM, SMEM] + [VMEM] * (2 + len(parts)),
        out_specs=[VMEM, VMEM, SMEM],
        scratch_shapes=WORK
        + [
            pltpu.VMEM((STRIDE, HALF), jnp.bfloat16),
            pltpu.VMEM((Z, 64, FEATURES), jnp.bfloat16),
        ],
        compiler_params=PARAMS,
        cost_estimate=pl.CostEstimate(flops=1 << 20, bytes_accessed=1 << 20, transcendentals=0),
        name="rows",
    )(place, reach, gain, x, *parts)


def ring(part, axes, order):
    size = len(order)
    return [
        lax.ppermute(part, axes, [(order[i], order[(i - t) % size]) for i in range(size)])
        for t in range(1, size)
    ]


def body(tokens, norm_gain, w_qkv, w_out, row_blocks, col_rows):
    xl, y, xh, c = (lax.axis_index(a) for a in ("xl", "y", "xh", "c"))
    rows = tokens.reshape(STRIDE, FEATURES)
    gain = norm_gain.reshape(1, FEATURES)
    place = jnp.stack([2 * xh + xl, y, c]).astype(jnp.int32)

    block = jnp.concatenate([w_qkv, w_out], axis=1)
    change = [(a * Z + z, (a ^ (z & 1)) * Z + z) for a in range(XL) for z in range(Z)]
    block = lax.ppermute(block, ("xl", "z"), change)
    column = lax.all_to_all(jnp.broadcast_to(block, (Z, 16, 512)), "z", split_axis=0, concat_axis=0)

    sent, column = lax.optimization_barrier((rows.reshape(64, 4, FEATURES), column))
    turned = lax.all_to_all(sent, SEQ, split_axis=0, concat_axis=0)
    turned = turned.reshape(STRIDE, FEATURES)

    halves = column.reshape(Z // 2, 2, 16, 512)
    row_part = jnp.where(xl == 0, halves[:, 0], halves[:, 1]).reshape(128, 512)
    col_part = jnp.where(xl == 0, halves[:, 1], halves[:, 0]).reshape(128, 512)
    part = jnp.concatenate([col_part[:, :PART], row_part, col_part[:, PART:]], axis=1)
    near = jnp.stack([part, *ring(part, ("xl", "xh"), [0, 2, 1, 3])])

    def plane(part):
        return [part, *ring(part, "y", range(Y))]

    def both_cores(parts, sizes):
        ends = [sum(sizes[: i + 1]) for i in range(len(sizes))]
        joined = [
            parts[e - n] if n == 1 else jnp.concatenate(parts[e - n : e])
            for e, n in zip(ends, sizes, strict=True)
        ]
        return [*joined, *(lax.ppermute(a, "c", [(0, 1), (1, 0)]) for a in joined)]

    col_plane = plane(near[:, :, :PART])
    col_mid = column_attention(place, col_rows, gain, turned, both_cores(col_plane, COLUMN_PIECES))
    col_out = lax.all_to_all(col_mid.reshape(64, 4, HALF), SEQ, split_axis=0, concat_axis=0)

    near_rest, _ = lax.optimization_barrier((near[:, :, PART:], col_plane[1]))
    rest, _ = lax.optimization_barrier((plane(near_rest), col_mid))
    base, low, last = row_attention(place, row_blocks, gain, rows, both_cores(rest, REST_PIECES))
    col_out = jnp.where(last[0] == 0, col_out, 0).reshape(STRIDE, HALF)

    mixed = pl.pallas_call(
        last_kernel,
        out_shape=jax.ShapeDtypeStruct((STRIDE, FEATURES), jnp.bfloat16),
        in_specs=[VMEM, VMEM, VMEM],
        out_specs=VMEM,
        compiler_params=PARAMS,
        name="mixed",
    )(base, col_out, low)
    return mixed.reshape(tokens.shape)


def solution(mesh):
    fine = Mesh(mesh.devices.reshape(XL, Y, XH, Z, C), ("xl", "y", "xh", "z", "c"))
    fsdp = ("xl", "y")
    return jax.shard_map(
        body,
        mesh=fine,
        in_specs=(P(fsdp, SEQ, None, None), P(), P(SEQ, fsdp), P(SEQ, fsdp), P(), P()),
        out_specs=P(fsdp, SEQ, None, None),
        check_vma=False,
    )
```

```python
import math

import jax
import jax.numpy as jnp
from jax import lax
from jax.experimental import pallas as pl
from jax.experimental.pallas import tpu as pltpu
from jax.sharding import Mesh
from jax.sharding import PartitionSpec as P

XL, Y, XH, Z, C = 2, 4, 2, 16, 2
X = XH * XL
FEATURES, STRIDE, HEADS, HEAD_DIM = 1024, 256, 8, 64
HALF = HEADS * HEAD_DIM
WIDTH = 3 * HALF
PART = 384
SEQ = ("xh", "z", "c")
FAR = 1 << 20
COLUMN_PIECES = (1, 3)
REST_PIECES = (1, 1, 1, 1)


def assemble(place, odd, refs, sizes, lanes, w_ref, first, width):
    x, y, core = place[0], place[1], place[2]
    pieces = [(i, j) for i, size in enumerate(sizes) for j in range(size)]
    for t in range(Y):
        cols = pl.ds(pl.multiple_of(first + width * ((y + t) & 3), 128), width)
        piece, at = pieces[t]
        for s in range(X):
            there = (x + s) & 3
            xh, xl = there >> 1, there & 1
            turn = 32 * ((1 - xl) if odd else xl)
            for ref, c in ((refs[piece], core), (refs[len(sizes) + piece], 1 - core)):
                rows = pl.ds(pl.multiple_of(turn + 16 * c, 16), 16)
                block = ref[at * X + s, :, lanes].reshape(Z // 2, 16, width)
                w_ref[pl.ds(Z // 2 * xh, Z // 2), rows, cols] = block


def attend(reach_ref, gain_ref, x_ref, w_ref, n_ref, qkv_ref, out_ref, dist):
    def norm(i, _):
        rows = pl.ds(pl.multiple_of(i * 64, 64), 64)
        x = x_ref[rows, :].astype(jnp.float32)
        scale = lax.rsqrt(jnp.mean(x * x, axis=-1, keepdims=True) + 1e-05)
        n_ref[rows, :] = (x * scale * gain_ref[...]).astype(jnp.bfloat16)
        return 0

    lax.fori_loop(0, STRIDE // 64, norm, 0)

    for n in range(0, WIDTH, 512):
        qkv_ref[:, n : n + 512] = jnp.dot(
            n_ref[...],
            w_ref[:, :, n : n + 512].reshape(FEATURES, 512),
            preferred_element_type=jnp.float32,
        ).astype(jnp.bfloat16)

    lane = lax.broadcasted_iota(jnp.int32, (STRIDE // 2, 128), 1)
    low = (lane < 64).astype(jnp.float32)
    masks = [low.astype(jnp.bfloat16), (1.0 - low).astype(jnp.bfloat16)]
    scale = 0.125 * math.log2(math.e)
    mid = STRIDE // 2
    for h in range(0, HEADS, 2):
        for first, seen in ((0, mid), (mid, STRIDE)):
            q, k, v = (qkv_ref[:, n * HALF + h * 64 : n * HALF + h * 64 + 128] for n in range(3))
            q = q[first : first + mid]
            s = lax.dot_general(
                jnp.concatenate([q * masks[0], q * masks[1]]),
                k[:seen],
                (((1,), (1,)), ((), ())),
                preferred_element_type=jnp.float32,
            )
            near = dist[first : first + mid, :seen]
            ps, sums = [], []
            for e in range(2):
                se = jnp.where(near < reach_ref[h + e], s[e * mid : e * mid + mid] * scale, -1e30)
                p = jnp.exp2(se - jnp.max(se, axis=-1, keepdims=True))
                sums.append(jnp.sum(p, axis=-1, keepdims=True))
                ps.append(p.astype(jnp.bfloat16))
            o = jnp.dot(jnp.concatenate(ps), v[:seen], preferred_element_type=jnp.float32)
            both = jnp.where(lane < 64, o[:mid] / sums[0], o[mid:] / sums[1])
            out_ref[first : first + mid, h * 64 : h * 64 + 128] = both.astype(jnp.bfloat16)


def pairs():
    i = lax.broadcasted_iota(jnp.int32, (STRIDE, STRIDE), 0)
    return i, lax.broadcasted_iota(jnp.int32, (STRIDE, STRIDE), 1)


def column_kernel(place, reach_ref, gain_ref, x_ref, *refs):
    *parts, out_ref, w_ref, n_ref, qkv_ref = refs
    assemble(place, True, parts, COLUMN_PIECES, slice(0, PART), w_ref, 0, PART)
    i, j = pairs()
    back = (i >> 2) - (j >> 2)
    dist = jnp.where((((i ^ j) & 3) == 0) & (back >= 0), back, FAR)
    attend(reach_ref, gain_ref, x_ref, w_ref, n_ref, qkv_ref, out_ref, dist)


def row_kernel(place, reach_ref, gain_ref, x_ref, *refs):
    *parts, base_ref, low_ref, done_ref, w_ref, n_ref, qkv_ref, a_ref, o_ref = refs
    done_ref[0] = 0
    assemble(place, False, parts, REST_PIECES, slice(0, PART), w_ref, 0, PART)
    i, j = pairs()
    dist = jnp.where(j <= i, (i >> 5) - (j >> 5), FAR)
    attend(reach_ref, gain_ref, x_ref, w_ref, n_ref, qkv_ref, a_ref, dist)
    assemble(place, False, parts, REST_PIECES, slice(PART, PART + 128), o_ref, 0, 128)
    assemble(place, True, parts, REST_PIECES, slice(PART + 128, PART + 256), o_ref, 512, 128)
    for n in range(0, FEATURES, 256):
        base_ref[:, n : n + 256] = x_ref[:, n : n + 256].astype(jnp.float32) + jnp.dot(
            a_ref[...],
            o_ref[: Z // 2, :, n : n + 256].reshape(HALF, 256),
            preferred_element_type=jnp.float32,
        )
    low_ref[...] = o_ref[Z // 2 :].reshape(HALF, FEATURES)


def last_kernel(base_ref, col_ref, low_ref, out_ref):
    for n in range(0, FEATURES, 256):
        out_ref[:, n : n + 256] = (
            base_ref[:, n : n + 256]
            + jnp.dot(col_ref[...], low_ref[:, n : n + 256], preferred_element_type=jnp.float32)
        ).astype(jnp.bfloat16)


VMEM = pl.BlockSpec(memory_space=pltpu.VMEM)
SMEM = pl.BlockSpec(memory_space=pltpu.SMEM)
WORK = [
    pltpu.VMEM((Z, 64, WIDTH), jnp.bfloat16),
    pltpu.VMEM((STRIDE, FEATURES), jnp.bfloat16),
    pltpu.VMEM((STRIDE, WIDTH), jnp.bfloat16),
]
PARAMS = pltpu.CompilerParams(vmem_limit_bytes=24 * 1024 * 1024)
COST = pl.CostEstimate(
    flops=2 * 256 * 1024 * 1536 + 16 * 256 * 256 * 128,
    bytes_accessed=6 << 20,
    transcendentals=8 * 256 * 256,
)


def column_attention(place, reach, gain, x, parts):
    return pl.pallas_call(
        column_kernel,
        out_shape=jax.ShapeDtypeStruct((STRIDE, HALF), jnp.bfloat16),
        in_specs=[SMEM, SMEM] + [VMEM] * (2 + len(parts)),
        out_specs=VMEM,
        scratch_shapes=WORK,
        compiler_params=PARAMS,
        cost_estimate=COST,
        name="columns",
    )(place, reach, gain, x, *parts)


def row_attention(place, reach, gain, x, parts):
    return pl.pallas_call(
        row_kernel,
        out_shape=[
            jax.ShapeDtypeStruct((STRIDE, FEATURES), jnp.float32),
            jax.ShapeDtypeStruct((HALF, FEATURES), jnp.bfloat16),
            jax.ShapeDtypeStruct((1,), jnp.int32),
        ],
        in_specs=[SMEM, SMEM] + [VMEM] * (2 + len(parts)),
        out_specs=[VMEM, VMEM, SMEM],
        scratch_shapes=WORK
        + [
            pltpu.VMEM((STRIDE, HALF), jnp.bfloat16),
            pltpu.VMEM((Z, 64, FEATURES), jnp.bfloat16),
        ],
        compiler_params=PARAMS,
        cost_estimate=pl.CostEstimate(flops=1 << 20, bytes_accessed=1 << 20, transcendentals=0),
        name="rows",
    )(place, reach, gain, x, *parts)


def ring(part, axes, order):
    size = len(order)
    return [
        lax.ppermute(part, axes, [(order[i], order[(i - t) % size]) for i in range(size)])
        for t in range(1, size)
    ]


def body(tokens, norm_gain, w_qkv, w_out, row_blocks, col_rows):
    xl, y, xh, c = (lax.axis_index(a) for a in ("xl", "y", "xh", "c"))
    rows = tokens.reshape(STRIDE, FEATURES)
    gain = norm_gain.reshape(1, FEATURES)
    place = jnp.stack([2 * xh + xl, y, c]).astype(jnp.int32)

    block = jnp.concatenate([w_qkv, w_out], axis=1)
    change = [(a * Z + z, (a ^ (z & 1)) * Z + z) for a in range(XL) for z in range(Z)]
    block = lax.ppermute(block, ("xl", "z"), change)
    column = lax.all_to_all(jnp.broadcast_to(block, (Z, 16, 512)), "z", split_axis=0, concat_axis=0)

    sent, column = lax.optimization_barrier((rows.reshape(64, 4, FEATURES), column))
    turned = lax.all_to_all(sent, SEQ, split_axis=0, concat_axis=0)
    turned = turned.reshape(STRIDE, FEATURES)

    halves = column.reshape(Z // 2, 2, 16, 512)
    row_part = jnp.where(xl == 0, halves[:, 0], halves[:, 1]).reshape(128, 512)
    col_part = jnp.where(xl == 0, halves[:, 1], halves[:, 0]).reshape(128, 512)
    part = jnp.concatenate([col_part[:, :PART], row_part, col_part[:, PART:]], axis=1)
    near = jnp.stack([part, *ring(part, ("xl", "xh"), [0, 2, 1, 3])])

    def plane(part):
        return [part, *ring(part, "y", range(Y))]

    def swap(part):
        return lax.ppermute(part, "c", [(0, 1), (1, 0)])

    held, *came = plane(near[:, :, :PART])
    rest, beside = near[:, :, PART:], came[0]
    came = jnp.concatenate(came)
    col_mid = column_attention(
        place, col_rows, gain, turned, [held, came, swap(held), swap(came)]
    )
    col_out = lax.all_to_all(col_mid.reshape(64, 4, HALF), SEQ, split_axis=0, concat_axis=0)

    rest, _ = lax.optimization_barrier((rest, beside))
    rest, *later = plane(rest)
    rest = [rest, *(lax.optimization_barrier((a, col_mid))[0] for a in later)]
    rest = [*rest, *(swap(a) for a in rest)]
    base, low, last = row_attention(place, row_blocks, gain, rows, rest)
    col_out = jnp.where(last[0] == 0, col_out, 0).reshape(STRIDE, HALF)

    mixed = pl.pallas_call(
        last_kernel,
        out_shape=jax.ShapeDtypeStruct((STRIDE, FEATURES), jnp.bfloat16),
        in_specs=[VMEM, VMEM, VMEM],
        out_specs=VMEM,
        compiler_params=PARAMS,
        name="mixed",
    )(base, col_out, low)
    return mixed.reshape(tokens.shape)


def solution(mesh):
    fine = Mesh(mesh.devices.reshape(XL, Y, XH, Z, C), ("xl", "y", "xh", "z", "c"))
    fsdp = ("xl", "y")
    return jax.shard_map(
        body,
        mesh=fine,
        in_specs=(P(fsdp, SEQ, None, None), P(), P(SEQ, fsdp), P(SEQ, fsdp), P(), P()),
        out_specs=P(fsdp, SEQ, None, None),
        check_vma=False,
    )
```

```python
import math

import jax
import jax.numpy as jnp
from jax import lax
from jax.experimental import pallas as pl
from jax.experimental.pallas import tpu as pltpu
from jax.sharding import Mesh
from jax.sharding import PartitionSpec as P

XL, Y, XH, Z, C = 2, 4, 2, 16, 2
X = XH * XL
FEATURES, STRIDE, HEADS, HEAD_DIM = 1024, 256, 8, 64
HALF = HEADS * HEAD_DIM
WIDTH = 3 * HALF
PART = 384
SEQ = ("xh", "z", "c")
FAR = 1 << 20
REST_PIECES = (1, 1, 1, 1)


def assemble(place, odd, refs, sizes, lanes, w_ref, first, width):
    x, y, core = place[0], place[1], place[2]
    pieces = [(i, j) for i, size in enumerate(sizes) for j in range(size)]
    for t in range(Y):
        cols = pl.ds(pl.multiple_of(first + width * ((y + t) & 3), 128), width)
        piece, at = pieces[t]
        for s in range(X):
            there = (x + s) & 3
            xh, xl = there >> 1, there & 1
            turn = 32 * ((1 - xl) if odd else xl)
            for ref, c in ((refs[piece], core), (refs[len(sizes) + piece], 1 - core)):
                rows = pl.ds(pl.multiple_of(turn + 16 * c, 16), 16)
                block = ref[at * X + s, :, lanes].reshape(Z // 2, 16, width)
                w_ref[pl.ds(Z // 2 * xh, Z // 2), rows, cols] = block


def attend(reach_ref, gain_ref, x_ref, w_ref, n_ref, qkv_ref, out_ref, dist):
    def norm(i, _):
        rows = pl.ds(pl.multiple_of(i * 64, 64), 64)
        x = x_ref[rows, :].astype(jnp.float32)
        scale = lax.rsqrt(jnp.mean(x * x, axis=-1, keepdims=True) + 1e-05)
        n_ref[rows, :] = (x * scale * gain_ref[...]).astype(jnp.bfloat16)
        return 0

    lax.fori_loop(0, STRIDE // 64, norm, 0)

    for n in range(0, WIDTH, 512):
        qkv_ref[:, n : n + 512] = jnp.dot(
            n_ref[...],
            w_ref[:, :, n : n + 512].reshape(FEATURES, 512),
            preferred_element_type=jnp.float32,
        ).astype(jnp.bfloat16)

    lane = lax.broadcasted_iota(jnp.int32, (STRIDE // 2, 128), 1)
    low = (lane < 64).astype(jnp.float32)
    masks = [low.astype(jnp.bfloat16), (1.0 - low).astype(jnp.bfloat16)]
    scale = 0.125 * math.log2(math.e)
    mid = STRIDE // 2
    for h in range(0, HEADS, 2):
        for first, seen in ((0, mid), (mid, STRIDE)):
            q, k, v = (qkv_ref[:, n * HALF + h * 64 : n * HALF + h * 64 + 128] for n in range(3))
            q = q[first : first + mid]
            s = lax.dot_general(
                jnp.concatenate([q * masks[0], q * masks[1]]),
                k[:seen],
                (((1,), (1,)), ((), ())),
                preferred_element_type=jnp.float32,
            )
            near = dist[first : first + mid, :seen]
            ps, sums = [], []
            for e in range(2):
                se = jnp.where(near < reach_ref[h + e], s[e * mid : e * mid + mid] * scale, -1e30)
                p = jnp.exp2(se - jnp.max(se, axis=-1, keepdims=True))
                sums.append(jnp.sum(p, axis=-1, keepdims=True))
                ps.append(p.astype(jnp.bfloat16))
            o = jnp.dot(jnp.concatenate(ps), v[:seen], preferred_element_type=jnp.float32)
            both = jnp.where(lane < 64, o[:mid] / sums[0], o[mid:] / sums[1])
            out_ref[first : first + mid, h * 64 : h * 64 + 128] = both.astype(jnp.bfloat16)


def pairs():
    i = lax.broadcasted_iota(jnp.int32, (STRIDE, STRIDE), 0)
    return i, lax.broadcasted_iota(jnp.int32, (STRIDE, STRIDE), 1)


def column_kernel(place, reach_ref, gain_ref, here_ref, there_ref, other_ref, w0_ref, w1_ref, *refs):
    out_ref, w_ref, n_ref, qkv_ref, x_ref = refs
    core, half = place[2], place[3]
    for a in range(XL):
        for y in range(Y):
            for b in range(XH):
                for ref, c in ((w0_ref, core), (w1_ref, 1 - core)):
                    rows = pl.ds(pl.multiple_of(32 * (1 - a) + 16 * c, 16), 16)
                    block = ref[(a * Y + y) * XH + b].reshape(Z // 2, 16, PART)
                    w_ref[Z // 2 * b : Z // 2 * (b + 1), rows, PART * y : PART * (y + 1)] = block
    i, j = pairs()
    row = 32 * ((j >> 7) ^ half) + 2 * ((j >> 2) & 15) + (((j >> 6) & 1) ^ core)
    move = (4 * row + (j & 3) == i).astype(jnp.float32).astype(jnp.bfloat16)
    n_ref[0:64, :] = here_ref[...]
    n_ref[64:128, :] = other_ref[0:64, :]
    n_ref[128:192, :] = there_ref[...]
    n_ref[192:256, :] = other_ref[64:128, :]
    for n in range(0, FEATURES, 512):
        x_ref[:, n : n + 512] = jnp.dot(
            move, n_ref[:, n : n + 512], preferred_element_type=jnp.float32
        ).astype(jnp.bfloat16)
    back = (i >> 2) - (j >> 2)
    dist = jnp.where((((i ^ j) & 3) == 0) & (back >= 0), back, FAR)
    attend(reach_ref, gain_ref, x_ref, w_ref, n_ref, qkv_ref, out_ref, dist)


def row_kernel(place, reach_ref, gain_ref, x_ref, *refs):
    *parts, base_ref, low_ref, done_ref, w_ref, n_ref, qkv_ref, a_ref, o_ref = refs
    done_ref[0] = 0
    assemble(place, False, parts, REST_PIECES, slice(0, PART), w_ref, 0, PART)
    i, j = pairs()
    dist = jnp.where(j <= i, (i >> 5) - (j >> 5), FAR)
    attend(reach_ref, gain_ref, x_ref, w_ref, n_ref, qkv_ref, a_ref, dist)
    assemble(place, False, parts, REST_PIECES, slice(PART, PART + 128), o_ref, 0, 128)
    assemble(place, True, parts, REST_PIECES, slice(PART + 128, PART + 256), o_ref, 512, 128)
    for n in range(0, FEATURES, 256):
        base_ref[:, n : n + 256] = x_ref[:, n : n + 256].astype(jnp.float32) + jnp.dot(
            a_ref[...],
            o_ref[: Z // 2, :, n : n + 256].reshape(HALF, 256),
            preferred_element_type=jnp.float32,
        )
    low_ref[...] = o_ref[Z // 2 :].reshape(HALF, FEATURES)


def last_kernel(base_ref, col_ref, low_ref, out_ref):
    for n in range(0, FEATURES, 256):
        out_ref[:, n : n + 256] = (
            base_ref[:, n : n + 256]
            + jnp.dot(col_ref[...], low_ref[:, n : n + 256], preferred_element_type=jnp.float32)
        ).astype(jnp.bfloat16)


VMEM = pl.BlockSpec(memory_space=pltpu.VMEM)
SMEM = pl.BlockSpec(memory_space=pltpu.SMEM)
WORK = [
    pltpu.VMEM((Z, 64, WIDTH), jnp.bfloat16),
    pltpu.VMEM((STRIDE, FEATURES), jnp.bfloat16),
    pltpu.VMEM((STRIDE, WIDTH), jnp.bfloat16),
]
PARAMS = pltpu.CompilerParams(vmem_limit_bytes=24 * 1024 * 1024)
COST = pl.CostEstimate(
    flops=2 * 256 * 1024 * 1536 + 16 * 256 * 256 * 128,
    bytes_accessed=6 << 20,
    transcendentals=8 * 256 * 256,
)


def column_attention(place, reach, gain, *arrays):
    return pl.pallas_call(
        column_kernel,
        out_shape=jax.ShapeDtypeStruct((STRIDE, HALF), jnp.bfloat16),
        in_specs=[SMEM, SMEM] + [VMEM] * (1 + len(arrays)),
        out_specs=VMEM,
        scratch_shapes=WORK + [pltpu.VMEM((STRIDE, FEATURES), jnp.bfloat16)],
        compiler_params=PARAMS,
        cost_estimate=COST,
        name="columns",
    )(place, reach, gain, *arrays)


def row_attention(place, reach, gain, x, parts):
    return pl.pallas_call(
        row_kernel,
        out_shape=[
            jax.ShapeDtypeStruct((STRIDE, FEATURES), jnp.float32),
            jax.ShapeDtypeStruct((HALF, FEATURES), jnp.bfloat16),
            jax.ShapeDtypeStruct((1,), jnp.int32),
        ],
        in_specs=[SMEM, SMEM] + [VMEM] * (2 + len(parts)),
        out_specs=[VMEM, VMEM, SMEM],
        scratch_shapes=WORK
        + [
            pltpu.VMEM((STRIDE, HALF), jnp.bfloat16),
            pltpu.VMEM((Z, 64, FEATURES), jnp.bfloat16),
        ],
        compiler_params=PARAMS,
        cost_estimate=pl.CostEstimate(flops=1 << 20, bytes_accessed=1 << 20, transcendentals=0),
        name="rows",
    )(place, reach, gain, x, *parts)


def ring(part, axes, order):
    size = len(order)
    return [
        lax.ppermute(part, axes, [(order[i], order[(i - t) % size]) for i in range(size)])
        for t in range(1, size)
    ]


def body(tokens, norm_gain, w_qkv, w_out, row_blocks, col_rows):
    xl, y, xh, c = (lax.axis_index(a) for a in ("xl", "y", "xh", "c"))
    rows = tokens.reshape(STRIDE, FEATURES)
    gain = norm_gain.reshape(1, FEATURES)
    place = jnp.stack([2 * xh + xl, y, c, xh]).astype(jnp.int32)

    block = jnp.concatenate([w_qkv, w_out], axis=1)
    change = [(a * Z + z, (a ^ (z & 1)) * Z + z) for a in range(XL) for z in range(Z)]
    block = lax.ppermute(block, ("xl", "z"), change)

    tokens_out = rows.reshape(XH, Z, C, 4, FEATURES).transpose(1, 0, 2, 3, 4)
    block = jnp.broadcast_to(block.reshape(XH, C, 4, 512), (Z, XH, C, 4, 512))
    column = lax.all_to_all(
        jnp.concatenate([tokens_out, block], axis=4), "z", split_axis=0, concat_axis=0
    )
    turned = column[..., :FEATURES]
    halves = column[..., FEATURES:].reshape(Z // 2, 2, 16, 512)
    row_part = jnp.where(xl == 0, halves[:, 0], halves[:, 1]).reshape(128, 512)
    col_part = jnp.where(xl == 0, halves[:, 1], halves[:, 0]).reshape(128, 512)
    rest_part = jnp.concatenate([row_part, col_part[:, PART:]], axis=1)

    def swap(part, axis="c"):
        return lax.ppermute(part, axis, [(0, 1), (1, 0)])

    col_own = lax.all_to_all(
        jnp.broadcast_to(col_part[:, :PART], (X * Y, 128, PART)),
        ("xl", "y", "xh"),
        split_axis=0,
        concat_axis=0,
    )

    here = jnp.where(xh == 0, turned[:, 0], turned[:, 1])
    there = swap(jnp.where(xh == 0, turned[:, 1], turned[:, 0]), "xh")
    others = swap(jnp.stack([jnp.where(c == 0, a[:, 1], a[:, 0]) for a in (here, there)]))
    here, there = (
        jnp.where(c == 0, a[:, 0], a[:, 1]).reshape(64, FEATURES) for a in (here, there)
    )
    near = jnp.stack([rest_part, *ring(rest_part, ("xl", "xh"), [0, 2, 1, 3])])
    col_own, others, near = lax.optimization_barrier((col_own, others, near))

    col_mid = column_attention(
        place, col_rows, gain, here, there, others.reshape(128, FEATURES), col_own, swap(col_own)
    )
    col_out = lax.all_to_all(col_mid.reshape(64, 4, HALF), SEQ, split_axis=0, concat_axis=0)

    rest, *later = [near, *ring(near, "y", range(Y))]
    rest = [rest, *(lax.optimization_barrier((a, col_mid))[0] for a in later)]
    rest = [*rest, *(swap(a) for a in rest)]
    base, low, last = row_attention(place, row_blocks, gain, rows, rest)
    col_out = jnp.where(last[0] == 0, col_out, 0).reshape(STRIDE, HALF)

    mixed = pl.pallas_call(
        last_kernel,
        out_shape=jax.ShapeDtypeStruct((STRIDE, FEATURES), jnp.bfloat16),
        in_specs=[VMEM, VMEM, VMEM],
        out_specs=VMEM,
        compiler_params=PARAMS,
        name="mixed",
    )(base, col_out, low)
    return mixed.reshape(tokens.shape)


def solution(mesh):
    fine = Mesh(mesh.devices.reshape(XL, Y, XH, Z, C), ("xl", "y", "xh", "z", "c"))
    fsdp = ("xl", "y")
    return jax.shard_map(
        body,
        mesh=fine,
        in_specs=(P(fsdp, SEQ, None, None), P(), P(SEQ, fsdp), P(SEQ, fsdp), P(), P()),
        out_specs=P(fsdp, SEQ, None, None),
        check_vma=False,
    )
```

```python
import math

import jax
import jax.numpy as jnp
from jax import lax
from jax.experimental import pallas as pl
from jax.experimental.pallas import tpu as pltpu
from jax.sharding import Mesh
from jax.sharding import PartitionSpec as P

XL, Y, XH, Z, C = 2, 4, 2, 16, 2
X = XH * XL
FEATURES, STRIDE, HEADS, HEAD_DIM = 1024, 256, 8, 64
HALF = HEADS * HEAD_DIM
WIDTH = 3 * HALF
PART = 384
SEQ = ("xh", "z", "c")
FAR = 1 << 20
COLUMN_PIECES = (1, 3)
REST_PIECES = (1, 1, 1, 1)


def assemble(place, refs, sizes, lanes, w_ref, first, width):
    xh, y, core = place[0], place[1], place[2]
    pieces = [(i, j) for i, size in enumerate(sizes) for j in range(size)]
    for t in range(Y):
        cols = pl.ds(pl.multiple_of(first + width * ((y + t) & 3), 128), width)
        piece, at = pieces[t]
        for u in range(XH):
            for ref, c in ((refs[piece], core), (refs[len(sizes) + piece], 1 - core)):
                rows = pl.ds(pl.multiple_of(16 * c, 16), 16)
                block = ref[at * XH + u, :, lanes].reshape(Z, 16, width)
                w_ref[pl.ds(Z * ((xh + u) & 1), Z), rows, cols] = block


def attend(reach_ref, gain_ref, x_ref, w_ref, n_ref, qkv_ref, out_ref, dist):
    def norm(i, _):
        rows = pl.ds(pl.multiple_of(i * 64, 64), 64)
        x = x_ref[rows, :].astype(jnp.float32)
        scale = lax.rsqrt(jnp.mean(x * x, axis=-1, keepdims=True) + 1e-05)
        n_ref[rows, :] = (x * scale * gain_ref[...]).astype(jnp.bfloat16)
        return 0

    lax.fori_loop(0, STRIDE // 64, norm, 0)

    for n in range(0, WIDTH, 512):
        qkv_ref[:, n : n + 512] = jnp.dot(
            n_ref[...],
            w_ref[:, :, n : n + 512].reshape(FEATURES, 512),
            preferred_element_type=jnp.float32,
        ).astype(jnp.bfloat16)

    lane = lax.broadcasted_iota(jnp.int32, (STRIDE // 2, 128), 1)
    low = (lane < 64).astype(jnp.float32)
    masks = [low.astype(jnp.bfloat16), (1.0 - low).astype(jnp.bfloat16)]
    scale = 0.125 * math.log2(math.e)
    mid = STRIDE // 2
    for h in range(0, HEADS, 2):
        for first, seen in ((0, mid), (mid, STRIDE)):
            q, k, v = (qkv_ref[:, n * HALF + h * 64 : n * HALF + h * 64 + 128] for n in range(3))
            q = q[first : first + mid]
            s = lax.dot_general(
                jnp.concatenate([q * masks[0], q * masks[1]]),
                k[:seen],
                (((1,), (1,)), ((), ())),
                preferred_element_type=jnp.float32,
            )
            near = dist[first : first + mid, :seen]
            ps, sums = [], []
            for e in range(2):
                se = jnp.where(near < reach_ref[h + e], s[e * mid : e * mid + mid] * scale, -1e30)
                p = jnp.exp2(se - jnp.max(se, axis=-1, keepdims=True))
                sums.append(jnp.sum(p, axis=-1, keepdims=True))
                ps.append(p.astype(jnp.bfloat16))
            o = jnp.dot(jnp.concatenate(ps), v[:seen], preferred_element_type=jnp.float32)
            both = jnp.where(lane < 64, o[:mid] / sums[0], o[mid:] / sums[1])
            out_ref[first : first + mid, h * 64 : h * 64 + 128] = both.astype(jnp.bfloat16)


def pairs():
    i = lax.broadcasted_iota(jnp.int32, (STRIDE, STRIDE), 0)
    return i, lax.broadcasted_iota(jnp.int32, (STRIDE, STRIDE), 1)


def column_kernel(place, reach_ref, gain_ref, x_ref, *refs):
    *parts, out_ref, w_ref, n_ref, qkv_ref = refs
    assemble(place, parts, COLUMN_PIECES, slice(0, PART), w_ref, 0, PART)
    i, j = pairs()
    back = (i >> 2) - (j >> 2)
    dist = jnp.where((((i ^ j) & 3) == 0) & (back >= 0), back, FAR)
    attend(reach_ref, gain_ref, x_ref, w_ref, n_ref, qkv_ref, out_ref, dist)


def row_kernel(place, reach_ref, gain_ref, x_ref, *refs):
    *parts, base_ref, low_ref, done_ref, w_ref, n_ref, qkv_ref, a_ref, o_ref = refs
    done_ref[0] = 0
    assemble(place, parts, REST_PIECES, slice(0, PART), w_ref, 0, PART)
    i, j = pairs()
    dist = jnp.where(j <= i, (i >> 5) - (j >> 5), FAR)
    attend(reach_ref, gain_ref, x_ref, w_ref, n_ref, qkv_ref, a_ref, dist)
    assemble(place, parts, REST_PIECES, slice(PART, PART + 128), o_ref, 0, 128)
    assemble(place, parts, REST_PIECES, slice(PART + 128, PART + 256), o_ref, 512, 128)
    for n in range(0, FEATURES, 256):
        base_ref[:, n : n + 256] = x_ref[:, n : n + 256].astype(jnp.float32) + jnp.dot(
            a_ref[...],
            o_ref[:Z, :, n : n + 256].reshape(HALF, 256),
            preferred_element_type=jnp.float32,
        )
    low_ref[...] = o_ref[Z:].reshape(HALF, FEATURES)


def last_kernel(base_ref, col_ref, low_ref, out_ref):
    for n in range(0, FEATURES, 256):
        out_ref[:, n : n + 256] = (
            base_ref[:, n : n + 256]
            + jnp.dot(col_ref[...], low_ref[:, n : n + 256], preferred_element_type=jnp.float32)
        ).astype(jnp.bfloat16)


VMEM = pl.BlockSpec(memory_space=pltpu.VMEM)
SMEM = pl.BlockSpec(memory_space=pltpu.SMEM)
WORK = [
    pltpu.VMEM((2 * Z, 32, WIDTH), jnp.bfloat16),
    pltpu.VMEM((STRIDE, FEATURES), jnp.bfloat16),
    pltpu.VMEM((STRIDE, WIDTH), jnp.bfloat16),
]
PARAMS = pltpu.CompilerParams(vmem_limit_bytes=24 * 1024 * 1024)
COST = pl.CostEstimate(
    flops=2 * 256 * 1024 * 1536 + 16 * 256 * 256 * 128,
    bytes_accessed=6 << 20,
    transcendentals=8 * 256 * 256,
)


def column_attention(place, reach, gain, x, parts):
    return pl.pallas_call(
        column_kernel,
        out_shape=jax.ShapeDtypeStruct((STRIDE, HALF), jnp.bfloat16),
        in_specs=[SMEM, SMEM] + [VMEM] * (2 + len(parts)),
        out_specs=VMEM,
        scratch_shapes=WORK,
        compiler_params=PARAMS,
        cost_estimate=COST,
        name="columns",
    )(place, reach, gain, x, *parts)


def row_attention(place, reach, gain, x, parts):
    return pl.pallas_call(
        row_kernel,
        out_shape=[
            jax.ShapeDtypeStruct((STRIDE, FEATURES), jnp.float32),
            jax.ShapeDtypeStruct((HALF, FEATURES), jnp.bfloat16),
            jax.ShapeDtypeStruct((1,), jnp.int32),
        ],
        in_specs=[SMEM, SMEM] + [VMEM] * (2 + len(parts)),
        out_specs=[VMEM, VMEM, SMEM],
        scratch_shapes=WORK
        + [
            pltpu.VMEM((STRIDE, HALF), jnp.bfloat16),
            pltpu.VMEM((2 * Z, 32, FEATURES), jnp.bfloat16),
        ],
        compiler_params=PARAMS,
        cost_estimate=pl.CostEstimate(flops=1 << 20, bytes_accessed=1 << 20, transcendentals=0),
        name="rows",
    )(place, reach, gain, x, *parts)


def ring(part, axes, order):
    size = len(order)
    return [
        lax.ppermute(part, axes, [(order[i], order[(i - t) % size]) for i in range(size)])
        for t in range(1, size)
    ]


def body(tokens, norm_gain, w_qkv, w_out, row_blocks, col_rows):
    xl, y, xh, c = (lax.axis_index(a) for a in ("xl", "y", "xh", "c"))
    rows = tokens.reshape(STRIDE, FEATURES)
    gain = norm_gain.reshape(1, FEATURES)
    place = jnp.stack([xh, y, c]).astype(jnp.int32)

    block = jnp.concatenate([w_qkv, w_out], axis=1)
    column = lax.all_to_all(jnp.broadcast_to(block, (Z, 16, 512)), "z", split_axis=0, concat_axis=0)

    sent, column = lax.optimization_barrier((rows.reshape(64, 4, FEATURES), column))
    turned = lax.all_to_all(sent, SEQ, split_axis=0, concat_axis=0)
    turned = turned.reshape(STRIDE, FEATURES)

    part = column.reshape(Z * 16, 512)
    ahead, across, behind = ring(part, ("xl", "xh"), [0, 2, 1, 3])
    for_rows = [jnp.where(xl == 0, part, behind), jnp.where(xl == 0, across, ahead)]
    for_columns = [jnp.where(xl == 0, ahead, part), jnp.where(xl == 0, behind, across)]
    near = jnp.stack([a[:, :PART] for a in for_columns])
    rest = jnp.stack(
        [jnp.concatenate([a, b[:, PART:]], axis=1) for a, b in zip(for_rows, for_columns, strict=True)]
    )

    def plane(part):
        return [part, *ring(part, "y", range(Y))]

    def swap(part):
        return lax.ppermute(part, "c", [(0, 1), (1, 0)])

    held, *came = plane(near)
    beside = came[0]
    came = jnp.concatenate(came)
    col_mid = column_attention(
        place, col_rows, gain, turned, [held, came, swap(held), swap(came)]
    )
    col_out = lax.all_to_all(col_mid.reshape(64, 4, HALF), SEQ, split_axis=0, concat_axis=0)

    rest, _ = lax.optimization_barrier((rest, beside))
    rest, *later = plane(rest)
    rest = [rest, *(lax.optimization_barrier((a, col_mid))[0] for a in later)]
    rest = [*rest, *(swap(a) for a in rest)]
    base, low, last = row_attention(place, row_blocks, gain, rows, rest)
    col_out = jnp.where(last[0] == 0, col_out, 0).reshape(STRIDE, HALF)

    mixed = pl.pallas_call(
        last_kernel,
        out_shape=jax.ShapeDtypeStruct((STRIDE, FEATURES), jnp.bfloat16),
        in_specs=[VMEM, VMEM, VMEM],
        out_specs=VMEM,
        compiler_params=PARAMS,
        name="mixed",
    )(base, col_out, low)
    return mixed.reshape(tokens.shape)


def solution(mesh):
    fine = Mesh(mesh.devices.reshape(XL, Y, XH, Z, C), ("xl", "y", "xh", "z", "c"))
    fsdp = ("xl", "y")
    return jax.shard_map(
        body,
        mesh=fine,
        in_specs=(P(fsdp, SEQ, None, None), P(), P(SEQ, fsdp), P(SEQ, fsdp), P(), P()),
        out_specs=P(fsdp, SEQ, None, None),
        check_vma=False,
    )
```

```python
import math

import jax
import jax.numpy as jnp
from jax import lax
from jax.experimental import pallas as pl
from jax.experimental.pallas import tpu as pltpu
from jax.sharding import Mesh
from jax.sharding import PartitionSpec as P

XL, Y, XH, Z, C = 2, 4, 2, 16, 2
X = XH * XL
FEATURES, STRIDE, HEADS, HEAD_DIM = 1024, 256, 8, 64
HALF = HEADS * HEAD_DIM
WIDTH = 3 * HALF
PART = 384
SEQ = ("xh", "z", "c")
FAR = 1 << 20
COLUMN_PIECES = (1, 3)
REST_PIECES = (1, 1, 1, 1)
COLUMN_ORDER = (0, 2, 1, 3)
REST_ORDER = (0, 1, 2, 3)


def assemble(place, refs, sizes, order, lanes, w_ref, first, width):
    xh, y, core = place[0], place[1], place[2]
    pieces = [(i, j) for i, size in enumerate(sizes) for j in range(size)]
    for t in range(Y):
        cols = pl.ds(pl.multiple_of(first + width * ((y + t) & 3), 128), width)
        piece, at = pieces[order.index(t)]
        for u in range(XH):
            for ref, c in ((refs[piece], core), (refs[len(sizes) + piece], 1 - core)):
                rows = pl.ds(pl.multiple_of(16 * c, 16), 16)
                block = ref[at * XH + u, :, lanes].reshape(Z, 16, width)
                w_ref[pl.ds(Z * ((xh + u) & 1), Z), rows, cols] = block


def attend(reach_ref, gain_ref, x_ref, w_ref, n_ref, qkv_ref, out_ref, dist):
    def norm(i, _):
        rows = pl.ds(pl.multiple_of(i * 64, 64), 64)
        x = x_ref[rows, :].astype(jnp.float32)
        scale = lax.rsqrt(jnp.mean(x * x, axis=-1, keepdims=True) + 1e-05)
        n_ref[rows, :] = (x * scale * gain_ref[...]).astype(jnp.bfloat16)
        return 0

    lax.fori_loop(0, STRIDE // 64, norm, 0)

    for n in range(0, WIDTH, 512):
        qkv_ref[:, n : n + 512] = jnp.dot(
            n_ref[...],
            w_ref[:, :, n : n + 512].reshape(FEATURES, 512),
            preferred_element_type=jnp.float32,
        ).astype(jnp.bfloat16)

    lane = lax.broadcasted_iota(jnp.int32, (STRIDE // 2, 128), 1)
    low = (lane < 64).astype(jnp.float32)
    masks = [low.astype(jnp.bfloat16), (1.0 - low).astype(jnp.bfloat16)]
    scale = 0.125 * math.log2(math.e)
    mid = STRIDE // 2
    for h in range(0, HEADS, 2):
        for first, seen in ((0, mid), (mid, STRIDE)):
            q, k, v = (qkv_ref[:, n * HALF + h * 64 : n * HALF + h * 64 + 128] for n in range(3))
            q = q[first : first + mid]
            s = lax.dot_general(
                jnp.concatenate([q * masks[0], q * masks[1]]),
                k[:seen],
                (((1,), (1,)), ((), ())),
                preferred_element_type=jnp.float32,
            )
            near = dist[first : first + mid, :seen]
            ps, sums = [], []
            for e in range(2):
                se = jnp.where(near < reach_ref[h + e], s[e * mid : e * mid + mid] * scale, -1e30)
                p = jnp.exp2(se - jnp.max(se, axis=-1, keepdims=True))
                sums.append(jnp.sum(p, axis=-1, keepdims=True))
                ps.append(p.astype(jnp.bfloat16))
            o = jnp.dot(jnp.concatenate(ps), v[:seen], preferred_element_type=jnp.float32)
            both = jnp.where(lane < 64, o[:mid] / sums[0], o[mid:] / sums[1])
            out_ref[first : first + mid, h * 64 : h * 64 + 128] = both.astype(jnp.bfloat16)


def pairs():
    i = lax.broadcasted_iota(jnp.int32, (STRIDE, STRIDE), 0)
    return i, lax.broadcasted_iota(jnp.int32, (STRIDE, STRIDE), 1)


def column_kernel(place, reach_ref, gain_ref, x_ref, *refs):
    *parts, out_ref, w_ref, n_ref, qkv_ref = refs
    assemble(place, parts, COLUMN_PIECES, COLUMN_ORDER, slice(0, PART), w_ref, 0, PART)
    i, j = pairs()
    back = (i >> 2) - (j >> 2)
    dist = jnp.where((((i ^ j) & 3) == 0) & (back >= 0), back, FAR)
    attend(reach_ref, gain_ref, x_ref, w_ref, n_ref, qkv_ref, out_ref, dist)


def row_kernel(place, reach_ref, gain_ref, x_ref, *refs):
    *parts, base_ref, low_ref, done_ref, w_ref, n_ref, qkv_ref, a_ref, o_ref = refs
    done_ref[0] = 0
    assemble(place, parts, REST_PIECES, REST_ORDER, slice(0, PART), w_ref, 0, PART)
    i, j = pairs()
    dist = jnp.where(j <= i, (i >> 5) - (j >> 5), FAR)
    attend(reach_ref, gain_ref, x_ref, w_ref, n_ref, qkv_ref, a_ref, dist)
    assemble(place, parts, REST_PIECES, REST_ORDER, slice(PART, PART + 128), o_ref, 0, 128)
    assemble(place, parts, REST_PIECES, REST_ORDER, slice(PART + 128, PART + 256), o_ref, 512, 128)
    for n in range(0, FEATURES, 256):
        base_ref[:, n : n + 256] = x_ref[:, n : n + 256].astype(jnp.float32) + jnp.dot(
            a_ref[...],
            o_ref[:Z, :, n : n + 256].reshape(HALF, 256),
            preferred_element_type=jnp.float32,
        )
    low_ref[...] = o_ref[Z:].reshape(HALF, FEATURES)


def last_kernel(base_ref, col_ref, low_ref, out_ref):
    for n in range(0, FEATURES, 256):
        out_ref[:, n : n + 256] = (
            base_ref[:, n : n + 256]
            + jnp.dot(col_ref[...], low_ref[:, n : n + 256], preferred_element_type=jnp.float32)
        ).astype(jnp.bfloat16)


VMEM = pl.BlockSpec(memory_space=pltpu.VMEM)
SMEM = pl.BlockSpec(memory_space=pltpu.SMEM)
WORK = [
    pltpu.VMEM((2 * Z, 32, WIDTH), jnp.bfloat16),
    pltpu.VMEM((STRIDE, FEATURES), jnp.bfloat16),
    pltpu.VMEM((STRIDE, WIDTH), jnp.bfloat16),
]
PARAMS = pltpu.CompilerParams(vmem_limit_bytes=24 * 1024 * 1024)
COST = pl.CostEstimate(
    flops=2 * 256 * 1024 * 1536 + 16 * 256 * 256 * 128,
    bytes_accessed=6 << 20,
    transcendentals=8 * 256 * 256,
)


def column_attention(place, reach, gain, x, parts):
    return pl.pallas_call(
        column_kernel,
        out_shape=jax.ShapeDtypeStruct((STRIDE, HALF), jnp.bfloat16),
        in_specs=[SMEM, SMEM] + [VMEM] * (2 + len(parts)),
        out_specs=VMEM,
        scratch_shapes=WORK,
        compiler_params=PARAMS,
        cost_estimate=COST,
        name="columns",
    )(place, reach, gain, x, *parts)


def row_attention(place, reach, gain, x, parts):
    return pl.pallas_call(
        row_kernel,
        out_shape=[
            jax.ShapeDtypeStruct((STRIDE, FEATURES), jnp.float32),
            jax.ShapeDtypeStruct((HALF, FEATURES), jnp.bfloat16),
            jax.ShapeDtypeStruct((1,), jnp.int32),
        ],
        in_specs=[SMEM, SMEM] + [VMEM] * (2 + len(parts)),
        out_specs=[VMEM, VMEM, SMEM],
        scratch_shapes=WORK
        + [
            pltpu.VMEM((STRIDE, HALF), jnp.bfloat16),
            pltpu.VMEM((2 * Z, 32, FEATURES), jnp.bfloat16),
        ],
        compiler_params=PARAMS,
        cost_estimate=pl.CostEstimate(flops=1 << 20, bytes_accessed=1 << 20, transcendentals=0),
        name="rows",
    )(place, reach, gain, x, *parts)


def ring(part, axes, order):
    size = len(order)
    got = {
        t: lax.ppermute(part, axes, [(order[i], order[(i - t) % size]) for i in range(size)])
        for t in sorted(range(1, size), key=lambda t: -min(t, size - t))
    }
    return [got[t] for t in range(1, size)]


def body(tokens, norm_gain, w_qkv, w_out, row_blocks, col_rows):
    xl, y, xh, c = (lax.axis_index(a) for a in ("xl", "y", "xh", "c"))
    rows = tokens.reshape(STRIDE, FEATURES)
    gain = norm_gain.reshape(1, FEATURES)
    place = jnp.stack([xh, y, c]).astype(jnp.int32)

    block = [jnp.broadcast_to(w, (Z, *w.shape)) for w in (w_qkv, w_out)]
    column = lax.all_to_all(jnp.concatenate(block, axis=2), "z", split_axis=0, concat_axis=0)

    sent, column = lax.optimization_barrier((rows.reshape(64, 4, FEATURES), column))
    turned = lax.all_to_all(sent, SEQ, split_axis=0, concat_axis=0)
    turned = turned.reshape(STRIDE, FEATURES)

    part = column.reshape(Z * 16, 512)
    ahead, across, behind = ring(part, ("xl", "xh"), [0, 2, 1, 3])
    for_rows = [jnp.where(xl == 0, part, behind), jnp.where(xl == 0, across, ahead)]
    for_columns = [jnp.where(xl == 0, ahead, part), jnp.where(xl == 0, behind, across)]
    near = jnp.stack([a[:, :PART] for a in for_columns])
    rest = jnp.stack(
        [jnp.concatenate([a, b[:, PART:]], axis=1) for a, b in zip(for_rows, for_columns, strict=True)]
    )

    def plane(part):
        return [part, *ring(part, "y", range(Y))]

    def swap(part):
        return lax.ppermute(part, "c", [(0, 1), (1, 0)])

    held, *came = plane(near)
    beside = came[0]
    came = jnp.concatenate([came[t - 1] for t in COLUMN_ORDER[1:]])
    col_mid = column_attention(
        place, col_rows, gain, turned, [held, came, swap(held), swap(came)]
    )
    col_out = lax.all_to_all(col_mid.reshape(64, 4, HALF), SEQ, split_axis=0, concat_axis=0)

    rest, _ = lax.optimization_barrier((rest, beside))
    rest, *later = plane(rest)
    rest = [rest, *(lax.optimization_barrier((a, col_mid))[0] for a in later)]
    rest = [*rest, *(swap(a) for a in rest)]
    base, low, last = row_attention(place, row_blocks, gain, rows, rest)
    col_out = jnp.where(last[0] == 0, col_out, 0).reshape(STRIDE, HALF)

    mixed = pl.pallas_call(
        last_kernel,
        out_shape=jax.ShapeDtypeStruct((STRIDE, FEATURES), jnp.bfloat16),
        in_specs=[VMEM, VMEM, VMEM],
        out_specs=VMEM,
        compiler_params=PARAMS,
        name="mixed",
    )(base, col_out, low)
    return mixed.reshape(tokens.shape)


def solution(mesh):
    fine = Mesh(mesh.devices.reshape(XL, Y, XH, Z, C), ("xl", "y", "xh", "z", "c"))
    fsdp = ("xl", "y")
    return jax.shard_map(
        body,
        mesh=fine,
        in_specs=(P(fsdp, SEQ, None, None), P(), P(SEQ, fsdp), P(SEQ, fsdp), P(), P()),
        out_specs=P(fsdp, SEQ, None, None),
        check_vma=False,
    )
```

```python
import math

import jax
import jax.numpy as jnp
from jax import lax
from jax.experimental import pallas as pl
from jax.experimental.pallas import tpu as pltpu
from jax.sharding import Mesh
from jax.sharding import PartitionSpec as P

XL, Y, XH, Z, C = 2, 4, 2, 16, 2
X = XH * XL
FEATURES, STRIDE, HEADS, HEAD_DIM = 1024, 256, 8, 64
HALF = HEADS * HEAD_DIM
WIDTH = 3 * HALF
PART = 384
SEQ = ("xh", "z", "c")
FAR = 1 << 20
COLUMN_PIECES = (1, 3)
REST_PIECES = (1, 1, 1, 1)
COLUMN_ORDER = (0, 2, 1, 3)
REST_ORDER = (0, 1, 2, 3)


def assemble(place, refs, sizes, order, lanes, w_ref, first, width):
    xh, y, core = place[0], place[1], place[2]
    pieces = [(i, j) for i, size in enumerate(sizes) for j in range(size)]
    for t in range(Y):
        cols = pl.ds(pl.multiple_of(first + width * ((y + t) & 3), 128), width)
        piece, at = pieces[order.index(t)]
        for u in range(XH):
            for ref, c in ((refs[piece], core), (refs[len(sizes) + piece], 1 - core)):
                rows = pl.ds(pl.multiple_of(16 * c, 16), 16)
                block = ref[at * XH + u, :, lanes].reshape(Z, 16, width)
                w_ref[pl.ds(Z * ((xh + u) & 1), Z), rows, cols] = block


def attend(reach_ref, gain_ref, x_ref, w_ref, n_ref, qkv_ref, out_ref, dist):
    def norm(i, _):
        rows = pl.ds(pl.multiple_of(i * 64, 64), 64)
        x = x_ref[rows, :].astype(jnp.float32)
        scale = lax.rsqrt(jnp.mean(x * x, axis=-1, keepdims=True) + 1e-05)
        n_ref[rows, :] = (x * scale * gain_ref[...]).astype(jnp.bfloat16)
        return 0

    lax.fori_loop(0, STRIDE // 64, norm, 0)

    for n in range(0, WIDTH, 512):
        qkv_ref[:, n : n + 512] = jnp.dot(
            n_ref[...],
            w_ref[:, :, n : n + 512].reshape(FEATURES, 512),
            preferred_element_type=jnp.float32,
        ).astype(jnp.bfloat16)

    lane = lax.broadcasted_iota(jnp.int32, (STRIDE // 2, 128), 1)
    low = (lane < 64).astype(jnp.float32)
    masks = [low.astype(jnp.bfloat16), (1.0 - low).astype(jnp.bfloat16)]
    scale = 0.125 * math.log2(math.e)
    mid = STRIDE // 2
    for h in range(0, HEADS, 2):
        for first, seen in ((0, mid), (mid, STRIDE)):
            q, k, v = (qkv_ref[:, n * HALF + h * 64 : n * HALF + h * 64 + 128] for n in range(3))
            q = q[first : first + mid]
            s = lax.dot_general(
                jnp.concatenate([q * masks[0], q * masks[1]]),
                k[:seen],
                (((1,), (1,)), ((), ())),
                preferred_element_type=jnp.float32,
            )
            near = dist[first : first + mid, :seen]
            ps, sums = [], []
            for e in range(2):
                se = jnp.where(near < reach_ref[h + e], s[e * mid : e * mid + mid] * scale, -1e30)
                p = jnp.exp2(se - jnp.max(se, axis=-1, keepdims=True))
                sums.append(jnp.sum(p, axis=-1, keepdims=True))
                ps.append(p.astype(jnp.bfloat16))
            o = jnp.dot(jnp.concatenate(ps), v[:seen], preferred_element_type=jnp.float32)
            both = jnp.where(lane < 64, o[:mid] / sums[0], o[mid:] / sums[1])
            out_ref[first : first + mid, h * 64 : h * 64 + 128] = both.astype(jnp.bfloat16)


def pairs():
    i = lax.broadcasted_iota(jnp.int32, (STRIDE, STRIDE), 0)
    return i, lax.broadcasted_iota(jnp.int32, (STRIDE, STRIDE), 1)


def column_kernel(place, reach_ref, gain_ref, x_ref, *refs):
    *parts, out_ref, w_ref, n_ref, qkv_ref = refs
    assemble(place, parts, COLUMN_PIECES, COLUMN_ORDER, slice(0, PART), w_ref, 0, PART)
    i, j = pairs()
    back = (i >> 2) - (j >> 2)
    dist = jnp.where((((i ^ j) & 3) == 0) & (back >= 0), back, FAR)
    attend(reach_ref, gain_ref, x_ref, w_ref, n_ref, qkv_ref, out_ref, dist)


def row_kernel(place, reach_ref, gain_ref, x_ref, *refs):
    *parts, base_ref, low_ref, done_ref, w_ref, n_ref, qkv_ref, a_ref, o_ref = refs
    done_ref[0] = 0
    assemble(place, parts, REST_PIECES, REST_ORDER, slice(0, PART), w_ref, 0, PART)
    i, j = pairs()
    dist = jnp.where(j <= i, (i >> 5) - (j >> 5), FAR)
    attend(reach_ref, gain_ref, x_ref, w_ref, n_ref, qkv_ref, a_ref, dist)
    assemble(place, parts, REST_PIECES, REST_ORDER, slice(PART, PART + 128), o_ref, 0, 128)
    assemble(place, parts, REST_PIECES, REST_ORDER, slice(PART + 128, PART + 256), o_ref, 512, 128)
    for n in range(0, FEATURES, 256):
        base_ref[:, n : n + 256] = x_ref[:, n : n + 256].astype(jnp.float32) + jnp.dot(
            a_ref[...],
            o_ref[:Z, :, n : n + 256].reshape(HALF, 256),
            preferred_element_type=jnp.float32,
        )
    low_ref[...] = o_ref[Z:].reshape(HALF, FEATURES)


def copies_kernel(qkv_ref, out_ref, copies_ref):
    for z in range(Z):
        copies_ref[z, :, :PART] = qkv_ref[...]
        copies_ref[z, :, PART:] = out_ref[...]


def last_kernel(base_ref, col_ref, low_ref, out_ref):
    for n in range(0, FEATURES, 256):
        out_ref[:, n : n + 256] = (
            base_ref[:, n : n + 256]
            + jnp.dot(col_ref[...], low_ref[:, n : n + 256], preferred_element_type=jnp.float32)
        ).astype(jnp.bfloat16)


VMEM = pl.BlockSpec(memory_space=pltpu.VMEM)
SMEM = pl.BlockSpec(memory_space=pltpu.SMEM)
WORK = [
    pltpu.VMEM((2 * Z, 32, WIDTH), jnp.bfloat16),
    pltpu.VMEM((STRIDE, FEATURES), jnp.bfloat16),
    pltpu.VMEM((STRIDE, WIDTH), jnp.bfloat16),
]
PARAMS = pltpu.CompilerParams(vmem_limit_bytes=24 * 1024 * 1024)
COST = pl.CostEstimate(
    flops=2 * 256 * 1024 * 1536 + 16 * 256 * 256 * 128,
    bytes_accessed=6 << 20,
    transcendentals=8 * 256 * 256,
)


def column_attention(place, reach, gain, x, parts):
    return pl.pallas_call(
        column_kernel,
        out_shape=jax.ShapeDtypeStruct((STRIDE, HALF), jnp.bfloat16),
        in_specs=[SMEM, SMEM] + [VMEM] * (2 + len(parts)),
        out_specs=VMEM,
        scratch_shapes=WORK,
        compiler_params=PARAMS,
        cost_estimate=COST,
        name="columns",
    )(place, reach, gain, x, *parts)


def row_attention(place, reach, gain, x, parts):
    return pl.pallas_call(
        row_kernel,
        out_shape=[
            jax.ShapeDtypeStruct((STRIDE, FEATURES), jnp.float32),
            jax.ShapeDtypeStruct((HALF, FEATURES), jnp.bfloat16),
            jax.ShapeDtypeStruct((1,), jnp.int32),
        ],
        in_specs=[SMEM, SMEM] + [VMEM] * (2 + len(parts)),
        out_specs=[VMEM, VMEM, SMEM],
        scratch_shapes=WORK
        + [
            pltpu.VMEM((STRIDE, HALF), jnp.bfloat16),
            pltpu.VMEM((2 * Z, 32, FEATURES), jnp.bfloat16),
        ],
        compiler_params=PARAMS,
        cost_estimate=pl.CostEstimate(flops=1 << 20, bytes_accessed=1 << 20, transcendentals=0),
        name="rows",
    )(place, reach, gain, x, *parts)


def ring(part, axes, order):
    size = len(order)
    got = {
        t: lax.ppermute(part, axes, [(order[i], order[(i - t) % size]) for i in range(size)])
        for t in sorted(range(1, size), key=lambda t: -min(t, size - t))
    }
    return [got[t] for t in range(1, size)]


def body(tokens, norm_gain, w_qkv, w_out, row_blocks, col_rows):
    xl, y, xh, c = (lax.axis_index(a) for a in ("xl", "y", "xh", "c"))
    rows = tokens.reshape(STRIDE, FEATURES)
    gain = norm_gain.reshape(1, FEATURES)
    place = jnp.stack([xh, y, c]).astype(jnp.int32)

    block = pl.pallas_call(
        copies_kernel,
        out_shape=jax.ShapeDtypeStruct((Z, 16, 512), jnp.bfloat16),
        in_specs=[VMEM, VMEM],
        out_specs=VMEM,
        name="copies",
    )(w_qkv, w_out)
    column = lax.all_to_all(block, "z", split_axis=0, concat_axis=0)

    sent, column = lax.optimization_barrier((rows.reshape(64, 4, FEATURES), column))
    turned = lax.all_to_all(sent, SEQ, split_axis=0, concat_axis=0)
    turned = turned.reshape(STRIDE, FEATURES)

    part = column.reshape(Z * 16, 512)
    ahead, across, behind = ring(part, ("xl", "xh"), [0, 2, 1, 3])
    for_rows = [jnp.where(xl == 0, part, behind), jnp.where(xl == 0, across, ahead)]
    for_columns = [jnp.where(xl == 0, ahead, part), jnp.where(xl == 0, behind, across)]
    near = jnp.stack([a[:, :PART] for a in for_columns])
    rest = jnp.stack(
        [jnp.concatenate([a, b[:, PART:]], axis=1) for a, b in zip(for_rows, for_columns, strict=True)]
    )

    def plane(part):
        return [part, *ring(part, "y", range(Y))]

    def swap(part):
        return lax.ppermute(part, "c", [(0, 1), (1, 0)])

    held, *came = plane(near)
    beside = came[0]
    held, came[1] = lax.optimization_barrier((held, came[1]))
    first = swap(held)
    came = jnp.concatenate([came[t - 1] for t in COLUMN_ORDER[1:]])
    came, first = lax.optimization_barrier((came, first))
    col_mid = column_attention(
        place, col_rows, gain, turned, [held, came, first, swap(came)]
    )
    col_out = lax.all_to_all(col_mid.reshape(64, 4, HALF), SEQ, split_axis=0, concat_axis=0)

    rest, _ = lax.optimization_barrier((rest, beside))
    rest, *later = plane(rest)
    rest = [rest, *(lax.optimization_barrier((a, col_mid))[0] for a in later)]
    rest = [*rest, *(swap(a) for a in rest)]
    base, low, last = row_attention(place, row_blocks, gain, rows, rest)
    col_out = jnp.where(last[0] == 0, col_out, 0).reshape(STRIDE, HALF)

    mixed = pl.pallas_call(
        last_kernel,
        out_shape=jax.ShapeDtypeStruct((STRIDE, FEATURES), jnp.bfloat16),
        in_specs=[VMEM, VMEM, VMEM],
        out_specs=VMEM,
        compiler_params=PARAMS,
        name="mixed",
    )(base, col_out, low)
    return mixed.reshape(tokens.shape)


def solution(mesh):
    fine = Mesh(mesh.devices.reshape(XL, Y, XH, Z, C), ("xl", "y", "xh", "z", "c"))
    fsdp = ("xl", "y")
    return jax.shard_map(
        body,
        mesh=fine,
        in_specs=(P(fsdp, SEQ, None, None), P(), P(SEQ, fsdp), P(SEQ, fsdp), P(), P()),
        out_specs=P(fsdp, SEQ, None, None),
        check_vma=False,
    )
```

```python
import math

import jax
import jax.numpy as jnp
from jax import lax
from jax.experimental import pallas as pl
from jax.experimental.pallas import tpu as pltpu
from jax.sharding import Mesh
from jax.sharding import PartitionSpec as P

XL, Y, XH, Z, C = 2, 4, 2, 16, 2
X = XH * XL
FEATURES, STRIDE, HEADS, HEAD_DIM = 1024, 256, 8, 64
HALF = HEADS * HEAD_DIM
WIDTH = 3 * HALF
PART = 384
SEQ = ("xh", "z", "c")
FAR = 1 << 20
COLUMN_PIECES = (1, 3)
REST_PIECES = (1, 1, 1, 1)
COLUMN_ORDER = (0, 2, 1, 3)
REST_ORDER = (0, 1, 2, 3)


def assemble(place, refs, sizes, order, lanes, w_ref, first, width):
    xh, y, core = place[0], place[1], place[2]
    pieces = [(i, j) for i, size in enumerate(sizes) for j in range(size)]
    for t in range(Y):
        cols = pl.ds(pl.multiple_of(first + width * ((y + t) & 3), 128), width)
        piece, at = pieces[order.index(t)]
        for u in range(XH):
            for ref, c in ((refs[piece], core), (refs[len(sizes) + piece], 1 - core)):
                rows = pl.ds(pl.multiple_of(16 * c, 16), 16)
                block = ref[at * XH + u, :, lanes].reshape(Z, 16, width)
                w_ref[pl.ds(Z * ((xh + u) & 1), Z), rows, cols] = block


def attend(reach_ref, gain_ref, x_ref, w_ref, n_ref, qkv_ref, out_ref, dist):
    def norm(i, _):
        rows = pl.ds(pl.multiple_of(i * 64, 64), 64)
        if len(x_ref.shape) == 3:
            x = x_ref[pl.ds(pl.multiple_of(i * 16, 16), 16)].astype(jnp.float32)
            x = x.reshape(64, FEATURES)
        else:
            x = x_ref[rows, :].astype(jnp.float32)
        scale = lax.rsqrt(jnp.mean(x * x, axis=-1, keepdims=True) + 1e-05)
        n_ref[rows, :] = (x * scale * gain_ref[...]).astype(jnp.bfloat16)
        return 0

    lax.fori_loop(0, STRIDE // 64, norm, 0)

    for n in range(0, WIDTH, 512):
        qkv_ref[:, n : n + 512] = jnp.dot(
            n_ref[...],
            w_ref[:, :, n : n + 512].reshape(FEATURES, 512),
            preferred_element_type=jnp.float32,
        ).astype(jnp.bfloat16)

    lane = lax.broadcasted_iota(jnp.int32, (STRIDE // 2, 128), 1)
    low = (lane < 64).astype(jnp.float32)
    masks = [low.astype(jnp.bfloat16), (1.0 - low).astype(jnp.bfloat16)]
    scale = 0.125 * math.log2(math.e)
    mid = STRIDE // 2
    for h in range(0, HEADS, 2):
        for first, seen in ((0, mid), (mid, STRIDE)):
            q, k, v = (qkv_ref[:, n * HALF + h * 64 : n * HALF + h * 64 + 128] for n in range(3))
            q = q[first : first + mid]
            s = lax.dot_general(
                jnp.concatenate([q * masks[0], q * masks[1]]),
                k[:seen],
                (((1,), (1,)), ((), ())),
                preferred_element_type=jnp.float32,
            )
            near = dist[first : first + mid, :seen]
            ps, sums = [], []
            for e in range(2):
                se = jnp.where(near < reach_ref[h + e], s[e * mid : e * mid + mid] * scale, -1e30)
                p = jnp.exp2(se - jnp.max(se, axis=-1, keepdims=True))
                sums.append(jnp.sum(p, axis=-1, keepdims=True))
                ps.append(p.astype(jnp.bfloat16))
            o = jnp.dot(jnp.concatenate(ps), v[:seen], preferred_element_type=jnp.float32)
            both = jnp.where(lane < 64, o[:mid] / sums[0], o[mid:] / sums[1])
            lanes = slice(h * 64, h * 64 + 128)
            if len(out_ref.shape) == 3:
                both = both.reshape(mid // 4, 4, 128).astype(jnp.bfloat16)
                out_ref[first // 4 : (first + mid) // 4, :, lanes] = both
            else:
                out_ref[first : first + mid, lanes] = both.astype(jnp.bfloat16)


def pairs():
    i = lax.broadcasted_iota(jnp.int32, (STRIDE, STRIDE), 0)
    return i, lax.broadcasted_iota(jnp.int32, (STRIDE, STRIDE), 1)


def column_kernel(place, reach_ref, gain_ref, x_ref, *refs):
    *parts, out_ref, w_ref, n_ref, qkv_ref = refs
    assemble(place, parts, COLUMN_PIECES, COLUMN_ORDER, slice(0, PART), w_ref, 0, PART)
    i, j = pairs()
    back = (i >> 2) - (j >> 2)
    dist = jnp.where((((i ^ j) & 3) == 0) & (back >= 0), back, FAR)
    attend(reach_ref, gain_ref, x_ref, w_ref, n_ref, qkv_ref, out_ref, dist)


def row_kernel(place, reach_ref, gain_ref, x_ref, *refs):
    *parts, base_ref, low_ref, done_ref, w_ref, n_ref, qkv_ref, a_ref, o_ref = refs
    done_ref[0] = 0
    assemble(place, parts, REST_PIECES, REST_ORDER, slice(0, PART), w_ref, 0, PART)
    i, j = pairs()
    dist = jnp.where(j <= i, (i >> 5) - (j >> 5), FAR)
    attend(reach_ref, gain_ref, x_ref, w_ref, n_ref, qkv_ref, a_ref, dist)
    assemble(place, parts, REST_PIECES, REST_ORDER, slice(PART, PART + 128), o_ref, 0, 128)
    assemble(place, parts, REST_PIECES, REST_ORDER, slice(PART + 128, PART + 256), o_ref, 512, 128)
    for n in range(0, FEATURES, 256):
        base_ref[:, n : n + 256] = x_ref[:, n : n + 256].astype(jnp.float32) + jnp.dot(
            a_ref[...],
            o_ref[:Z, :, n : n + 256].reshape(HALF, 256),
            preferred_element_type=jnp.float32,
        )
    low_ref[...] = o_ref[Z:].reshape(HALF, FEATURES)


def copies_kernel(qkv_ref, out_ref, copies_ref):
    for z in range(Z):
        copies_ref[z, :, :PART] = qkv_ref[...]
        copies_ref[z, :, PART:] = out_ref[...]


def last_kernel(base_ref, col_ref, low_ref, out_ref):
    for n in range(0, FEATURES, 256):
        out_ref[:, n : n + 256] = (
            base_ref[:, n : n + 256]
            + jnp.dot(col_ref[...], low_ref[:, n : n + 256], preferred_element_type=jnp.float32)
        ).astype(jnp.bfloat16)


VMEM = pl.BlockSpec(memory_space=pltpu.VMEM)
SMEM = pl.BlockSpec(memory_space=pltpu.SMEM)
WORK = [
    pltpu.VMEM((2 * Z, 32, WIDTH), jnp.bfloat16),
    pltpu.VMEM((STRIDE, FEATURES), jnp.bfloat16),
    pltpu.VMEM((STRIDE, WIDTH), jnp.bfloat16),
]
PARAMS = pltpu.CompilerParams(vmem_limit_bytes=24 * 1024 * 1024)
COST = pl.CostEstimate(
    flops=2 * 256 * 1024 * 1536 + 16 * 256 * 256 * 128,
    bytes_accessed=6 << 20,
    transcendentals=8 * 256 * 256,
)


def column_attention(place, reach, gain, x, parts):
    return pl.pallas_call(
        column_kernel,
        out_shape=jax.ShapeDtypeStruct((STRIDE // 4, 4, HALF), jnp.bfloat16),
        in_specs=[SMEM, SMEM] + [VMEM] * (2 + len(parts)),
        out_specs=VMEM,
        scratch_shapes=WORK,
        compiler_params=PARAMS,
        cost_estimate=COST,
        name="columns",
    )(place, reach, gain, x, *parts)


def row_attention(place, reach, gain, x, parts):
    return pl.pallas_call(
        row_kernel,
        out_shape=[
            jax.ShapeDtypeStruct((STRIDE, FEATURES), jnp.float32),
            jax.ShapeDtypeStruct((HALF, FEATURES), jnp.bfloat16),
            jax.ShapeDtypeStruct((1,), jnp.int32),
        ],
        in_specs=[SMEM, SMEM] + [VMEM] * (2 + len(parts)),
        out_specs=[VMEM, VMEM, SMEM],
        scratch_shapes=WORK
        + [
            pltpu.VMEM((STRIDE, HALF), jnp.bfloat16),
            pltpu.VMEM((2 * Z, 32, FEATURES), jnp.bfloat16),
        ],
        compiler_params=PARAMS,
        cost_estimate=pl.CostEstimate(flops=1 << 20, bytes_accessed=1 << 20, transcendentals=0),
        name="rows",
    )(place, reach, gain, x, *parts)


def ring(part, axes, order):
    size = len(order)
    got = {
        t: lax.ppermute(part, axes, [(order[i], order[(i - t) % size]) for i in range(size)])
        for t in sorted(range(1, size), key=lambda t: -min(t, size - t))
    }
    return [got[t] for t in range(1, size)]


def body(tokens, norm_gain, w_qkv, w_out, row_blocks, col_rows):
    xl, y, xh, c = (lax.axis_index(a) for a in ("xl", "y", "xh", "c"))
    rows = tokens.reshape(STRIDE, FEATURES)
    gain = norm_gain.reshape(1, FEATURES)
    place = jnp.stack([xh, y, c]).astype(jnp.int32)

    block = pl.pallas_call(
        copies_kernel,
        out_shape=jax.ShapeDtypeStruct((Z, 16, 512), jnp.bfloat16),
        in_specs=[VMEM, VMEM],
        out_specs=VMEM,
        name="copies",
    )(w_qkv, w_out)
    column = lax.all_to_all(block, "z", split_axis=0, concat_axis=0)

    sent, column = lax.optimization_barrier((rows.reshape(64, 4, FEATURES), column))
    turned = lax.all_to_all(sent, SEQ, split_axis=0, concat_axis=0)

    part = column.reshape(Z * 16, 512)
    ahead, across, behind = ring(part, ("xl", "xh"), [0, 2, 1, 3])
    for_rows = [jnp.where(xl == 0, part, behind), jnp.where(xl == 0, across, ahead)]
    for_columns = [jnp.where(xl == 0, ahead, part), jnp.where(xl == 0, behind, across)]
    near = jnp.stack([a[:, :PART] for a in for_columns])
    rest = jnp.stack(
        [jnp.concatenate([a, b[:, PART:]], axis=1) for a, b in zip(for_rows, for_columns, strict=True)]
    )

    def plane(part):
        return [part, *ring(part, "y", range(Y))]

    def swap(part):
        return lax.ppermute(part, "c", [(0, 1), (1, 0)])

    held, *came = plane(near)
    beside = came[0]
    held, came[1] = lax.optimization_barrier((held, came[1]))
    first = swap(held)
    came = jnp.concatenate([came[t - 1] for t in COLUMN_ORDER[1:]])
    came, first = lax.optimization_barrier((came, first))
    col_mid = column_attention(
        place, col_rows, gain, turned, [held, came, first, swap(came)]
    )
    col_out = lax.all_to_all(col_mid, SEQ, split_axis=0, concat_axis=0)

    rest, _ = lax.optimization_barrier((rest, beside))
    rest, *later = plane(rest)
    rest = [rest, *(lax.optimization_barrier((a, col_mid))[0] for a in later)]
    rest = [*rest, *(swap(a) for a in rest)]
    base, low, last = row_attention(place, row_blocks, gain, rows, rest)
    col_out = jnp.where(last[0] == 0, col_out, 0).reshape(STRIDE, HALF)

    mixed = pl.pallas_call(
        last_kernel,
        out_shape=jax.ShapeDtypeStruct((STRIDE, FEATURES), jnp.bfloat16),
        in_specs=[VMEM, VMEM, VMEM],
        out_specs=VMEM,
        compiler_params=PARAMS,
        name="mixed",
    )(base, col_out, low)
    return mixed.reshape(tokens.shape)


def solution(mesh):
    fine = Mesh(mesh.devices.reshape(XL, Y, XH, Z, C), ("xl", "y", "xh", "z", "c"))
    fsdp = ("xl", "y")
    return jax.shard_map(
        body,
        mesh=fine,
        in_specs=(P(fsdp, SEQ, None, None), P(), P(SEQ, fsdp), P(SEQ, fsdp), P(), P()),
        out_specs=P(fsdp, SEQ, None, None),
        check_vma=False,
    )
```

```python
import math

import jax
import jax.numpy as jnp
from jax import lax
from jax.experimental import pallas as pl
from jax.experimental.pallas import tpu as pltpu
from jax.sharding import Mesh
from jax.sharding import PartitionSpec as P

XL, Y, XH, Z, C = 2, 4, 2, 16, 2
X = XH * XL
FEATURES, STRIDE, HEADS, HEAD_DIM = 1024, 256, 8, 64
HALF = HEADS * HEAD_DIM
WIDTH = 3 * HALF
PART = 384
SEQ = ("xh", "z", "c")
FAR = 1 << 20
COLUMN_PIECES = (1, 1, 2)
REST_PIECES = (1, 1, 1, 1)
COLUMN_ORDER = (0, 2, 1, 3)
REST_ORDER = (0, 1, 2, 3)


def assemble(place, refs, sizes, order, lanes, w_ref, first, width):
    xh, y, core = place[0], place[1], place[2]
    pieces = [(i, j) for i, size in enumerate(sizes) for j in range(size)]
    for t in range(Y):
        cols = pl.ds(pl.multiple_of(first + width * ((y + t) & 3), 128), width)
        piece, at = pieces[order.index(t)]
        for u in range(XH):
            for ref, c in ((refs[piece], core), (refs[len(sizes) + piece], 1 - core)):
                rows = pl.ds(pl.multiple_of(16 * c, 16), 16)
                block = ref[at * XH + u, :, lanes].reshape(Z, 16, width)
                w_ref[pl.ds(Z * ((xh + u) & 1), Z), rows, cols] = block


def attend(reach_ref, gain_ref, x_ref, w_ref, n_ref, qkv_ref, out_ref, dist):
    def norm(i, _):
        rows = pl.ds(pl.multiple_of(i * 64, 64), 64)
        x = x_ref[rows, :].astype(jnp.float32)
        scale = lax.rsqrt(jnp.mean(x * x, axis=-1, keepdims=True) + 1e-05)
        n_ref[rows, :] = (x * scale * gain_ref[...]).astype(jnp.bfloat16)
        return 0

    lax.fori_loop(0, STRIDE // 64, norm, 0)

    for n in range(0, WIDTH, 512):
        qkv_ref[:, n : n + 512] = jnp.dot(
            n_ref[...],
            w_ref[:, :, n : n + 512].reshape(FEATURES, 512),
            preferred_element_type=jnp.float32,
        ).astype(jnp.bfloat16)

    lane = lax.broadcasted_iota(jnp.int32, (STRIDE // 2, 128), 1)
    low = (lane < 64).astype(jnp.float32)
    masks = [low.astype(jnp.bfloat16), (1.0 - low).astype(jnp.bfloat16)]
    scale = 0.125 * math.log2(math.e)
    mid = STRIDE // 2
    for h in range(0, HEADS, 2):
        for first, seen in ((0, mid), (mid, STRIDE)):
            q, k, v = (qkv_ref[:, n * HALF + h * 64 : n * HALF + h * 64 + 128] for n in range(3))
            q = q[first : first + mid]
            s = lax.dot_general(
                jnp.concatenate([q * masks[0], q * masks[1]]),
                k[:seen],
                (((1,), (1,)), ((), ())),
                preferred_element_type=jnp.float32,
            )
            near = dist[first : first + mid, :seen]
            ps, sums = [], []
            for e in range(2):
                se = jnp.where(near < reach_ref[h + e], s[e * mid : e * mid + mid] * scale, -1e30)
                p = jnp.exp2(se - jnp.max(se, axis=-1, keepdims=True))
                sums.append(jnp.sum(p, axis=-1, keepdims=True))
                ps.append(p.astype(jnp.bfloat16))
            o = jnp.dot(jnp.concatenate(ps), v[:seen], preferred_element_type=jnp.float32)
            both = jnp.where(lane < 64, o[:mid] / sums[0], o[mid:] / sums[1])
            out_ref[first : first + mid, h * 64 : h * 64 + 128] = both.astype(jnp.bfloat16)


def pairs():
    i = lax.broadcasted_iota(jnp.int32, (STRIDE, STRIDE), 0)
    return i, lax.broadcasted_iota(jnp.int32, (STRIDE, STRIDE), 1)


def column_kernel(place, reach_ref, gain_ref, x_ref, *refs):
    *parts, out_ref, w_ref, n_ref, qkv_ref = refs
    assemble(place, parts, COLUMN_PIECES, COLUMN_ORDER, slice(0, PART), w_ref, 0, PART)
    i, j = pairs()
    back = (i >> 2) - (j >> 2)
    dist = jnp.where((((i ^ j) & 3) == 0) & (back >= 0), back, FAR)
    attend(reach_ref, gain_ref, x_ref, w_ref, n_ref, qkv_ref, out_ref, dist)


def row_kernel(place, reach_ref, gain_ref, x_ref, *refs):
    *parts, base_ref, low_ref, done_ref, w_ref, n_ref, qkv_ref, a_ref, o_ref = refs
    done_ref[0] = 0
    assemble(place, parts, REST_PIECES, REST_ORDER, slice(0, PART), w_ref, 0, PART)
    i, j = pairs()
    dist = jnp.where(j <= i, (i >> 5) - (j >> 5), FAR)
    attend(reach_ref, gain_ref, x_ref, w_ref, n_ref, qkv_ref, a_ref, dist)
    assemble(place, parts, REST_PIECES, REST_ORDER, slice(PART, PART + 128), o_ref, 0, 128)
    assemble(place, parts, REST_PIECES, REST_ORDER, slice(PART + 128, PART + 256), o_ref, 512, 128)
    for n in range(0, FEATURES, 256):
        base_ref[:, n : n + 256] = x_ref[:, n : n + 256].astype(jnp.float32) + jnp.dot(
            a_ref[...],
            o_ref[:Z, :, n : n + 256].reshape(HALF, 256),
            preferred_element_type=jnp.float32,
        )
    low_ref[...] = o_ref[Z:].reshape(HALF, FEATURES)


def copies_kernel(qkv_ref, out_ref, copies_ref):
    for z in range(Z):
        copies_ref[z, :, :PART] = qkv_ref[...]
        copies_ref[z, :, PART:] = out_ref[...]


def last_kernel(base_ref, col_ref, low_ref, out_ref):
    for n in range(0, FEATURES, 256):
        out_ref[:, n : n + 256] = (
            base_ref[:, n : n + 256]
            + jnp.dot(col_ref[...], low_ref[:, n : n + 256], preferred_element_type=jnp.float32)
        ).astype(jnp.bfloat16)


VMEM = pl.BlockSpec(memory_space=pltpu.VMEM)
SMEM = pl.BlockSpec(memory_space=pltpu.SMEM)
WORK = [
    pltpu.VMEM((2 * Z, 32, WIDTH), jnp.bfloat16),
    pltpu.VMEM((STRIDE, FEATURES), jnp.bfloat16),
    pltpu.VMEM((STRIDE, WIDTH), jnp.bfloat16),
]
PARAMS = pltpu.CompilerParams(vmem_limit_bytes=24 * 1024 * 1024)
COST = pl.CostEstimate(
    flops=2 * 256 * 1024 * 1536 + 16 * 256 * 256 * 128,
    bytes_accessed=6 << 20,
    transcendentals=8 * 256 * 256,
)


def column_attention(place, reach, gain, x, parts):
    return pl.pallas_call(
        column_kernel,
        out_shape=jax.ShapeDtypeStruct((STRIDE, HALF), jnp.bfloat16),
        in_specs=[SMEM, SMEM] + [VMEM] * (2 + len(parts)),
        out_specs=VMEM,
        scratch_shapes=WORK,
        compiler_params=PARAMS,
        cost_estimate=COST,
        name="columns",
    )(place, reach, gain, x, *parts)


def row_attention(place, reach, gain, x, parts):
    return pl.pallas_call(
        row_kernel,
        out_shape=[
            jax.ShapeDtypeStruct((STRIDE, FEATURES), jnp.float32),
            jax.ShapeDtypeStruct((HALF, FEATURES), jnp.bfloat16),
            jax.ShapeDtypeStruct((1,), jnp.int32),
        ],
        in_specs=[SMEM, SMEM] + [VMEM] * (2 + len(parts)),
        out_specs=[VMEM, VMEM, SMEM],
        scratch_shapes=WORK
        + [
            pltpu.VMEM((STRIDE, HALF), jnp.bfloat16),
            pltpu.VMEM((2 * Z, 32, FEATURES), jnp.bfloat16),
        ],
        compiler_params=PARAMS,
        cost_estimate=pl.CostEstimate(flops=1 << 20, bytes_accessed=1 << 20, transcendentals=0),
        name="rows",
    )(place, reach, gain, x, *parts)


def ring(part, axes, order):
    size = len(order)
    got = {
        t: lax.ppermute(part, axes, [(order[i], order[(i - t) % size]) for i in range(size)])
        for t in sorted(range(1, size), key=lambda t: -min(t, size - t))
    }
    return [got[t] for t in range(1, size)]


def body(tokens, norm_gain, w_qkv, w_out, row_blocks, col_rows):
    xl, y, xh, c = (lax.axis_index(a) for a in ("xl", "y", "xh", "c"))
    rows = tokens.reshape(STRIDE, FEATURES)
    gain = norm_gain.reshape(1, FEATURES)
    place = jnp.stack([xh, y, c]).astype(jnp.int32)

    block = pl.pallas_call(
        copies_kernel,
        out_shape=jax.ShapeDtypeStruct((Z, 16, 512), jnp.bfloat16),
        in_specs=[VMEM, VMEM],
        out_specs=VMEM,
        name="copies",
    )(w_qkv, w_out)
    column = lax.all_to_all(block, "z", split_axis=0, concat_axis=0)

    sent, column = lax.optimization_barrier((rows.reshape(64, 4, FEATURES), column))
    turned = lax.all_to_all(sent, SEQ, split_axis=0, concat_axis=0)
    turned = turned.reshape(STRIDE, FEATURES)

    part = column.reshape(Z * 16, 512)
    ahead, across, behind = ring(part, ("xl", "xh"), [0, 2, 1, 3])
    for_rows = [jnp.where(xl == 0, part, behind), jnp.where(xl == 0, across, ahead)]
    for_columns = [jnp.where(xl == 0, ahead, part), jnp.where(xl == 0, behind, across)]
    near = jnp.stack([a[:, :PART] for a in for_columns])
    rest = jnp.stack(
        [jnp.concatenate([a, b[:, PART:]], axis=1) for a, b in zip(for_rows, for_columns, strict=True)]
    )

    def plane(part):
        return [part, *ring(part, "y", range(Y))]

    def swap(part):
        return lax.ppermute(part, "c", [(0, 1), (1, 0)])

    held, *came = plane(near)
    beside = came[0]
    held, came[1] = lax.optimization_barrier((held, came[1]))
    early = [held, came[1]]
    first = [swap(a) for a in early]
    came = jnp.concatenate([came[t - 1] for t in COLUMN_ORDER[2:]])
    came, first = lax.optimization_barrier((came, first))
    col_mid = column_attention(
        place, col_rows, gain, turned, [*early, came, *first, swap(came)]
    )
    col_out = lax.all_to_all(col_mid.reshape(64, 4, HALF), SEQ, split_axis=0, concat_axis=0)

    rest, _ = lax.optimization_barrier((rest, beside))
    rest, *later = plane(rest)
    rest = [rest, *(lax.optimization_barrier((a, col_mid))[0] for a in later)]
    rest = [*rest, *(swap(a) for a in rest)]
    base, low, last = row_attention(place, row_blocks, gain, rows, rest)
    col_out = jnp.where(last[0] == 0, col_out, 0).reshape(STRIDE, HALF)

    mixed = pl.pallas_call(
        last_kernel,
        out_shape=jax.ShapeDtypeStruct((STRIDE, FEATURES), jnp.bfloat16),
        in_specs=[VMEM, VMEM, VMEM],
        out_specs=VMEM,
        compiler_params=PARAMS,
        name="mixed",
    )(base, col_out, low)
    return mixed.reshape(tokens.shape)


def solution(mesh):
    fine = Mesh(mesh.devices.reshape(XL, Y, XH, Z, C), ("xl", "y", "xh", "z", "c"))
    fsdp = ("xl", "y")
    return jax.shard_map(
        body,
        mesh=fine,
        in_specs=(P(fsdp, SEQ, None, None), P(), P(SEQ, fsdp), P(SEQ, fsdp), P(), P()),
        out_specs=P(fsdp, SEQ, None, None),
        check_vma=False,
    )
```

```python
import math

import jax
import jax.numpy as jnp
from jax import lax
from jax.experimental import pallas as pl
from jax.experimental.pallas import tpu as pltpu
from jax.sharding import Mesh
from jax.sharding import PartitionSpec as P

XL, Y, XH, Z, C = 2, 4, 2, 16, 2
X = XH * XL
FEATURES, STRIDE, HEADS, HEAD_DIM = 1024, 256, 8, 64
HALF = HEADS * HEAD_DIM
WIDTH = 3 * HALF
PART = 384
SEQ = ("xh", "z", "c")
FAR = 1 << 20
COLUMN_PIECES = (1, 3)
REST_PIECES = (1, 1, 1, 1)
COLUMN_ORDER = (0, 2, 1, 3)
REST_ORDER = (0, 1, 2, 3)


def assemble(place, refs, sizes, order, lanes, w_ref, first, width):
    xh, y, core = place[0], place[1], place[2]
    pieces = [(i, j) for i, size in enumerate(sizes) for j in range(size)]
    for t in range(Y):
        cols = pl.ds(pl.multiple_of(first + width * ((y + t) & 3), 128), width)
        piece, at = pieces[order.index(t)]
        for u in range(XH):
            for ref, c in ((refs[piece], core), (refs[len(sizes) + piece], 1 - core)):
                rows = pl.ds(pl.multiple_of(16 * c, 16), 16)
                block = ref[at * XH + u, :, lanes].reshape(Z, 16, width)
                w_ref[pl.ds(Z * ((xh + u) & 1), Z), rows, cols] = block


def attend(reach_ref, gain_ref, x_ref, w_ref, n_ref, qkv_ref, out_ref, dist):
    def norm(i, _):
        rows = pl.ds(pl.multiple_of(i * 64, 64), 64)
        x = x_ref[rows, :].astype(jnp.float32)
        scale = lax.rsqrt(jnp.mean(x * x, axis=-1, keepdims=True) + 1e-05)
        n_ref[rows, :] = (x * scale * gain_ref[...]).astype(jnp.bfloat16)
        return 0

    lax.fori_loop(0, STRIDE // 64, norm, 0)

    for n in range(0, WIDTH, 512):
        qkv_ref[:, n : n + 512] = jnp.dot(
            n_ref[...],
            w_ref[:, :, n : n + 512].reshape(FEATURES, 512),
            preferred_element_type=jnp.float32,
        ).astype(jnp.bfloat16)

    lane = lax.broadcasted_iota(jnp.int32, (STRIDE // 2, 128), 1)
    low = (lane < 64).astype(jnp.float32)
    masks = [low.astype(jnp.bfloat16), (1.0 - low).astype(jnp.bfloat16)]
    scale = 0.125 * math.log2(math.e)
    mid = STRIDE // 2
    for h in range(0, HEADS, 2):
        for first, seen in ((0, mid), (mid, STRIDE)):
            q, k, v = (qkv_ref[:, n * HALF + h * 64 : n * HALF + h * 64 + 128] for n in range(3))
            q = q[first : first + mid]
            s = lax.dot_general(
                jnp.concatenate([q * masks[0], q * masks[1]]),
                k[:seen],
                (((1,), (1,)), ((), ())),
                preferred_element_type=jnp.float32,
            )
            near = dist[first : first + mid, :seen]
            ps, sums = [], []
            for e in range(2):
                se = jnp.where(near < reach_ref[h + e], s[e * mid : e * mid + mid] * scale, -1e30)
                p = jnp.exp2(se - jnp.max(se, axis=-1, keepdims=True))
                sums.append(jnp.sum(p, axis=-1, keepdims=True))
                ps.append(p.astype(jnp.bfloat16))
            o = jnp.dot(jnp.concatenate(ps), v[:seen], preferred_element_type=jnp.float32)
            both = jnp.where(lane < 64, o[:mid] / sums[0], o[mid:] / sums[1])
            out_ref[first : first + mid, h * 64 : h * 64 + 128] = both.astype(jnp.bfloat16)


def pairs():
    i = lax.broadcasted_iota(jnp.int32, (STRIDE, STRIDE), 0)
    return i, lax.broadcasted_iota(jnp.int32, (STRIDE, STRIDE), 1)


def column_kernel(place, reach_ref, gain_ref, x_ref, *refs):
    *parts, out_ref, w_ref, n_ref, qkv_ref = refs
    assemble(place, parts, COLUMN_PIECES, COLUMN_ORDER, slice(0, PART), w_ref, 0, PART)
    i, j = pairs()
    back = (i >> 2) - (j >> 2)
    dist = jnp.where((((i ^ j) & 3) == 0) & (back >= 0), back, FAR)
    attend(reach_ref, gain_ref, x_ref, w_ref, n_ref, qkv_ref, out_ref, dist)


def row_kernel(place, reach_ref, gain_ref, x_ref, *refs):
    *parts, base_ref, low_ref, done_ref, w_ref, n_ref, qkv_ref, a_ref, o_ref = refs
    done_ref[0] = 0
    assemble(place, parts, REST_PIECES, REST_ORDER, slice(0, PART), w_ref, 0, PART)
    i, j = pairs()
    dist = jnp.where(j <= i, (i >> 5) - (j >> 5), FAR)
    attend(reach_ref, gain_ref, x_ref, w_ref, n_ref, qkv_ref, a_ref, dist)
    assemble(place, parts, REST_PIECES, REST_ORDER, slice(PART, PART + 128), o_ref, 0, 128)
    assemble(place, parts, REST_PIECES, REST_ORDER, slice(PART + 128, PART + 256), o_ref, 512, 128)
    for n in range(0, FEATURES, 256):
        base_ref[:, n : n + 256] = x_ref[:, n : n + 256].astype(jnp.float32) + jnp.dot(
            a_ref[...],
            o_ref[:Z, :, n : n + 256].reshape(HALF, 256),
            preferred_element_type=jnp.float32,
        )
    low_ref[...] = o_ref[Z:].reshape(HALF, FEATURES)


def copies_kernel(qkv_ref, out_ref, copies_ref):
    for z in range(Z):
        copies_ref[z, :, :PART] = qkv_ref[...]
        copies_ref[z, :, PART:] = out_ref[...]


def last_kernel(base_ref, col_ref, low_ref, out_ref):
    for n in range(0, FEATURES, 512):
        out_ref[:, n : n + 512] = (
            base_ref[:, n : n + 512]
            + jnp.dot(col_ref[...], low_ref[:, n : n + 512], preferred_element_type=jnp.float32)
        ).astype(jnp.bfloat16)


VMEM = pl.BlockSpec(memory_space=pltpu.VMEM)
SMEM = pl.BlockSpec(memory_space=pltpu.SMEM)
WORK = [
    pltpu.VMEM((2 * Z, 32, WIDTH), jnp.bfloat16),
    pltpu.VMEM((STRIDE, FEATURES), jnp.bfloat16),
    pltpu.VMEM((STRIDE, WIDTH), jnp.bfloat16),
]
PARAMS = pltpu.CompilerParams(vmem_limit_bytes=24 * 1024 * 1024)
COST = pl.CostEstimate(
    flops=2 * 256 * 1024 * 1536 + 16 * 256 * 256 * 128,
    bytes_accessed=6 << 20,
    transcendentals=8 * 256 * 256,
)


def column_attention(place, reach, gain, x, parts):
    return pl.pallas_call(
        column_kernel,
        out_shape=jax.ShapeDtypeStruct((STRIDE, HALF), jnp.bfloat16),
        in_specs=[SMEM, SMEM] + [VMEM] * (2 + len(parts)),
        out_specs=VMEM,
        scratch_shapes=WORK,
        compiler_params=PARAMS,
        cost_estimate=COST,
        name="columns",
    )(place, reach, gain, x, *parts)


def row_attention(place, reach, gain, x, parts):
    return pl.pallas_call(
        row_kernel,
        out_shape=[
            jax.ShapeDtypeStruct((STRIDE, FEATURES), jnp.float32),
            jax.ShapeDtypeStruct((HALF, FEATURES), jnp.bfloat16),
            jax.ShapeDtypeStruct((1,), jnp.int32),
        ],
        in_specs=[SMEM, SMEM] + [VMEM] * (2 + len(parts)),
        out_specs=[VMEM, VMEM, SMEM],
        scratch_shapes=WORK
        + [
            pltpu.VMEM((STRIDE, HALF), jnp.bfloat16),
            pltpu.VMEM((2 * Z, 32, FEATURES), jnp.bfloat16),
        ],
        compiler_params=PARAMS,
        cost_estimate=pl.CostEstimate(flops=1 << 20, bytes_accessed=1 << 20, transcendentals=0),
        name="rows",
    )(place, reach, gain, x, *parts)


def ring(part, axes, order):
    size = len(order)
    got = {
        t: lax.ppermute(part, axes, [(order[i], order[(i - t) % size]) for i in range(size)])
        for t in sorted(range(1, size), key=lambda t: -min(t, size - t))
    }
    return [got[t] for t in range(1, size)]


def body(tokens, norm_gain, w_qkv, w_out, row_blocks, col_rows):
    xl, y, xh, c = (lax.axis_index(a) for a in ("xl", "y", "xh", "c"))
    rows = tokens.reshape(STRIDE, FEATURES)
    gain = norm_gain.reshape(1, FEATURES)
    place = jnp.stack([xh, y, c]).astype(jnp.int32)

    block = pl.pallas_call(
        copies_kernel,
        out_shape=jax.ShapeDtypeStruct((Z, 16, 512), jnp.bfloat16),
        in_specs=[VMEM, VMEM],
        out_specs=VMEM,
        name="copies",
    )(w_qkv, w_out)
    column = lax.all_to_all(block, "z", split_axis=0, concat_axis=0)

    sent, column = lax.optimization_barrier((rows.reshape(64, 4, FEATURES), column))
    turned = lax.all_to_all(sent, SEQ, split_axis=0, concat_axis=0)
    turned = turned.reshape(STRIDE, FEATURES)

    part = column.reshape(Z * 16, 512)
    ahead, across, behind = ring(part, ("xl", "xh"), [0, 2, 1, 3])
    for_rows = [jnp.where(xl == 0, part, behind), jnp.where(xl == 0, across, ahead)]
    for_columns = [jnp.where(xl == 0, ahead, part), jnp.where(xl == 0, behind, across)]
    near = jnp.stack([a[:, :PART] for a in for_columns])
    rest = jnp.stack(
        [jnp.concatenate([a, b[:, PART:]], axis=1) for a, b in zip(for_rows, for_columns, strict=True)]
    )

    def plane(part):
        return [part, *ring(part, "y", range(Y))]

    def swap(part):
        return lax.ppermute(part, "c", [(0, 1), (1, 0)])

    held, *came = plane(near)
    beside = came[0]
    held, came[1] = lax.optimization_barrier((held, came[1]))
    first = swap(held)
    came = jnp.concatenate([came[t - 1] for t in COLUMN_ORDER[1:]])
    came, first = lax.optimization_barrier((came, first))
    col_mid = column_attention(
        place, col_rows, gain, turned, [held, came, first, swap(came)]
    )
    col_out = lax.all_to_all(col_mid.reshape(64, 4, HALF), SEQ, split_axis=0, concat_axis=0)

    rest, _ = lax.optimization_barrier((rest, beside))
    rest, *later = plane(rest)
    rest = [rest, *(lax.optimization_barrier((a, col_mid))[0] for a in later)]
    rest = [*rest, *(swap(a) for a in rest)]
    base, low, last = row_attention(place, row_blocks, gain, rows, rest)
    col_out = jnp.where(last[0] == 0, col_out, 0).reshape(STRIDE, HALF)

    mixed = pl.pallas_call(
        last_kernel,
        out_shape=jax.ShapeDtypeStruct((STRIDE, FEATURES), jnp.bfloat16),
        in_specs=[VMEM, VMEM, VMEM],
        out_specs=VMEM,
        compiler_params=PARAMS,
        name="mixed",
    )(base, col_out, low)
    return mixed.reshape(tokens.shape)


def solution(mesh):
    fine = Mesh(mesh.devices.reshape(XL, Y, XH, Z, C), ("xl", "y", "xh", "z", "c"))
    fsdp = ("xl", "y")
    return jax.shard_map(
        body,
        mesh=fine,
        in_specs=(P(fsdp, SEQ, None, None), P(), P(SEQ, fsdp), P(SEQ, fsdp), P(), P()),
        out_specs=P(fsdp, SEQ, None, None),
        check_vma=False,
    )
```
